256 devices in a mesh: gx: 8 (over z), gy: 4 (over x), gz: 8 (over y, core).
Axes of the slice: x: 4, y: 4, z: 8, core: 2. Of those that a mesh axis runs over, the one named last changes fastest.
Arguments:
- right_side: float32 [256, 64, 1024], P('gx', 'gy', 'gz'), may hold values from -4 to 4
- phase_mask: int32 [256, 64, 1024], P('gx', 'gy', 'gz'), may hold values 0 or 1
Outputs:
- pressure: float32 [256, 64, 1024], P('gx', 'gy', 'gz')
- residual: float32 [256, 64, 1024], P('gx', 'gy', 'gz')
The draws below stay inside these ranges and needn't reach their ends.
All inputs are finite; a program needn't handle non-finite values. No bound on the sum of `phase_mask` on one device may be relied on, other than what follows from the above.
Results may differ from the reference program's by a relative error of at most 0.0003.
Values sent between devices are 32-bit elements; how exact they have to be, the bound alone decides.
No kernel may reach another device: no remote copies, remote signals or barrier semaphores. Data moves between devices by JAX's collectives and lax.ppermute only.
A program may use at most 192 MiB of HBM per device.

```python
import jax
import jax.numpy as jnp

LEVELS = 4
SMOOTH_DEG = 2
COARSE_ITERS = 8
CYCLES = 2
NX = 256
NY = 64
NZ = 1024


def draw_right_side(key, part):
    key = jax.random.fold_in(key, 17)
    noise = jax.random.normal(key, (NX, NY, NZ), jnp.float32)
    return jnp.clip(noise, -4.0, 4.0)


def set_ends(values, own_key, low, top_value):
    index_at = [jax.random.randint(jax.random.fold_in(own_key, axis), (), 0, length) for axis, length in enumerate(values.shape)]
    widest = values.shape.index(max(values.shape))
    next_to = index_at[:widest] + [(index_at[widest] + 1) % values.shape[widest]] + index_at[widest + 1:]
    return values.at[tuple(index_at)].set(low).at[tuple(next_to)].set(top_value)


def setup_inputs(seed: int = 0) -> dict:
    arg_keys = jax.random.split(jax.random.key(seed), 3)
    right_side = draw_right_side(jax.random.fold_in(arg_keys[2], 71), 0)
    phase_mask = set_ends((jax.random.randint(arg_keys[1], (NX, NY, NZ), 0, 2) < 1).astype(jnp.int32), jax.random.fold_in(arg_keys[1], 1), 0, 1)
    return dict(right_side=right_side, phase_mask=phase_mask)


SMOOTH_LOW = 0.25
SMOOTH_HIGH = 2.0
COARSE_LOW = 0.02
LIQUID = 10.0
GAS = 1.0


def upper_faces(density):
    beyond = jnp.full_like(density[:1], GAS)
    face_x = 2.0 / (density + jnp.concatenate([density[1:], beyond], 0))
    beyond = jnp.full_like(density[:, :1], GAS)
    face_y = 2.0 / (density + jnp.concatenate([density[:, 1:], beyond], 1))
    beyond = jnp.full_like(density[:, :, :1], GAS)
    face_z = 2.0 / (density + jnp.concatenate([density[:, :, 1:], beyond], 2))
    return face_x, face_y, face_z


def coarsen_faces(face_set):
    face_x, face_y, face_z = face_set
    size_a, size_b, size_c = face_x.shape
    coarse_x = face_x[1::2].reshape(size_a // 2, size_b // 2, 2, size_c // 2, 2).sum((2, 4)) * 0.125
    coarse_y = face_y[:, 1::2].reshape(size_a // 2, 2, size_b // 2, size_c // 2, 2).sum((1, 4)) * 0.125
    coarse_z = face_z[:, :, 1::2].reshape(size_a // 2, 2, size_b // 2, 2, size_c // 2).sum((1, 3)) * 0.125
    return coarse_x, coarse_y, coarse_z


def restrict(values):
    size_a, size_b, size_c = values.shape
    return values.reshape(size_a // 2, 2, size_b // 2, 2, size_c // 2, 2).sum((1, 3, 5)) * 0.125


def prolong(values):
    return jnp.repeat(jnp.repeat(jnp.repeat(values, 2, 0), 2, 1), 2, 2)


def assemble(face_x, face_y, face_z, lower_x, lower_y, lower_z):
    diagonal = face_x + lower_x + face_y + lower_y + face_z + lower_z
    return (face_x, face_y, face_z, lower_x, lower_y, lower_z, diagonal)


def whole_level(face_set):
    face_x, face_y, face_z = face_set
    lower_x = jnp.concatenate([jnp.zeros_like(face_x[:1]), face_x[:-1]], 0)
    lower_y = jnp.concatenate([jnp.zeros_like(face_y[:, :1]), face_y[:, :-1]], 1)
    lower_z = jnp.concatenate([jnp.zeros_like(face_z[:, :, :1]), face_z[:, :, :-1]], 2)
    return assemble(face_x, face_y, face_z, lower_x, lower_y, lower_z)


def local_pad(values):
    return jnp.pad(values, 1)


def operate(values, stencil, padder):
    face_x, face_y, face_z, lower_x, lower_y, lower_z, diagonal = stencil
    padded = padder(values)
    result_sum = diagonal * values - face_x * padded[2:, 1:-1, 1:-1] - lower_x * padded[:-2, 1:-1, 1:-1]
    result_sum = result_sum - face_y * padded[1:-1, 2:, 1:-1] - lower_y * padded[1:-1, :-2, 1:-1]
    return result_sum - face_z * padded[1:-1, 1:-1, 2:] - lower_z * padded[1:-1, 1:-1, :-2]


def smooth(residual, stencil, padder, degree, low_end, want_residual):
    mid_value = 0.5 * (SMOOTH_HIGH + low_end)
    half_width = 0.5 * (SMOOTH_HIGH - low_end)
    ratio_value = mid_value / half_width
    rho_old = 1.0 / ratio_value
    diagonal = stencil[6]
    update = residual / (mid_value * diagonal)
    accumulated = update
    for turn_index in range(1, degree):
        residual = residual - operate(update, stencil, padder)
        rho_new = 1.0 / (2.0 * ratio_value - rho_old)
        update = (rho_new * rho_old) * update + (2.0 * rho_new / half_width) * (residual / diagonal)
        accumulated = accumulated + update
        rho_old = rho_new
    if want_residual:
        residual = residual - operate(update, stencil, padder)
    return accumulated, residual


def vcycle(levels, level_index, residual, want_residual, padder, bottom):
    if level_index == len(levels):
        return bottom(residual), residual
    stencil = levels[level_index]
    pre_smooth, residual_mid = smooth(residual, stencil, padder, SMOOTH_DEG, SMOOTH_LOW, True)
    coarse, unused = vcycle(levels, level_index + 1, restrict(residual_mid), False, padder, bottom)
    lifted = prolong(coarse)
    residual_mid = residual_mid - operate(lifted, stencil, padder)
    second, residual_out = smooth(residual_mid, stencil, padder, SMOOTH_DEG, SMOOTH_LOW, want_residual)
    return pre_smooth + lifted + second, residual_out


def reference(right_side, phase_mask):
    density = GAS + (LIQUID - GAS) * phase_mask.astype(jnp.float32)
    face_sets = [upper_faces(density)]
    for level_index in range(LEVELS - 1):
        face_sets.append(coarsen_faces(face_sets[-1]))
    all_levels = [whole_level(face_set) for face_set in face_sets]
    coarse_level = all_levels[-1]

    def bottom(residual):
        return smooth(residual, coarse_level, local_pad, COARSE_ITERS, COARSE_LOW, False)[0]

    pressure = jnp.zeros_like(right_side)
    residual = right_side
    for turn_index in range(CYCLES):
        correction, residual = vcycle(all_levels[:-1], 0, residual, True, local_pad, bottom)
        pressure = pressure + correction
    return pressure, residual
```

```python
import functools

import jax
import jax.numpy as jnp
from jax import lax
from jax.experimental import pallas as pl
from jax.experimental.pallas import tpu as pltpu
from jax.sharding import PartitionSpec as P

COARSE_ITERS = 8
SMOOTH_LOW = 0.25
SMOOTH_HIGH = 2.0
COARSE_LOW = 0.02
LIQUID = 10.0
GAS = 1.0

INTERPRET = False
VMEM_LIMIT = 40 * 1024 * 1024

BX, BY, BZ = 32, 16, 128
WX = 8
X0, Y0, Z0 = BX + 2 * WX, 32, 256
X1, Y1G, Z1 = 48, 8, 128
X2 = 24
F32 = jnp.float32


def chebyshev(low, degree):
    theta = 0.5 * (SMOOTH_HIGH + low)
    delta = 0.5 * (SMOOTH_HIGH - low)
    sigma = theta / delta
    rho_old = 1.0 / sigma
    steps = []
    for _ in range(1, degree):
        rho_new = 1.0 / (2.0 * sigma - rho_old)
        steps.append((rho_new * rho_old, 2.0 * rho_new / delta))
        rho_old = rho_new
    return 1.0 / theta, steps


FIRST, ((KEEP, GAIN),) = chebyshev(SMOOTH_LOW, 2)
COARSE_FIRST, COARSE_STEPS = chebyshev(COARSE_LOW, COARSE_ITERS)


def roll(values, shift, axis):
    return pltpu.roll(values, shift % values.shape[axis], axis)


def iota(shape, dim):
    return lax.broadcasted_iota(jnp.int32, shape, dim)


def dot(left, right):
    return jnp.dot(left, right, precision=lax.Precision.HIGHEST, preferred_element_type=F32)


def lane_pairs(fine, weight, odd_only=False):
    z = iota((fine, 128), 0)
    half = z >> 1
    if fine == 128:
        half = jnp.where(z >= 96, half + 64, half)
    hit = half == iota((fine, 128), 1)
    if odd_only:
        hit = hit & ((z & 1) == 1)
    return jnp.where(hit, weight, 0.0).astype(F32)


def lane_copies(fine):
    z = iota((128, fine), 1)
    half = z >> 1
    if fine == 128:
        half = jnp.where(z >= 96, half + 64, half)
    return jnp.where(half == iota((128, fine), 0), 1.0, 0.0).astype(F32)


def row_pairs(rows, odd_x=False, odd_y=False):
    shape = (2 * rows, 8 * rows)
    shift = rows.bit_length() - 1
    c, f = iota(shape, 0), iota(shape, 1)
    cx, cy = c >> (shift - 1), c & (rows // 2 - 1)
    x, y = f >> shift, f & (rows - 1)
    hit = ((x >> 1) == cx) & ((y >> 1) == cy)
    if odd_x:
        hit = hit & ((x & 1) == 1)
    if odd_y:
        hit = hit & ((y & 1) == 1)
    return jnp.where(hit, 1.0, 0.0).astype(F32)


def row_copies(rows):
    shape = (8 * rows, 2 * rows)
    shift = rows.bit_length() - 1
    f, c = iota(shape, 0), iota(shape, 1)
    hit = ((f >> (shift + 1)) == (c >> (shift - 1))) & (((f & (rows - 1)) >> 1) == (c & (rows // 2 - 1)))
    return jnp.where(hit, 1.0, 0.0).astype(F32)


def coarsen(block, rows_matrix, lanes_matrix):
    planes, rows, lanes = block.shape
    out = dot(dot(rows_matrix, block.reshape(planes * rows, lanes)), lanes_matrix)
    return out.reshape(4, rows // 2, 128)


def refine(block, rows_matrix, lanes_matrix):
    planes, rows, lanes = block.shape
    out = dot(rows_matrix, dot(block.reshape(planes * rows, lanes), lanes_matrix))
    return out.reshape(8, 2 * rows, lanes_matrix.shape[1])


def apply_at(v, at, planes, faces):
    fx, fy, fz, diag = faces
    here = pl.ds(at, planes)
    c = v[here]
    y, z = fy[here], fz[here]
    out = diag[here] * c - fx[here] * v[pl.ds(at + 1, planes)] - fx[pl.ds(at - 1, planes)] * v[pl.ds(at - 1, planes)]
    out = out - y * roll(c, -1, 1) - roll(y * c, 1, 1)
    return out - z * roll(c, -1, 2) - roll(z * c, 1, 2)


def step_x(values, by):
    if by > 0:
        return jnp.concatenate([values[-1:], values[:-1]], 0)
    return jnp.concatenate([values[1:], values[:1]], 0)


def apply_to(v, faces):
    fx, fy, fz, diag = faces
    out = diag * v - fx * step_x(v, -1) - step_x(fx * v, 1)
    out = out - fy * roll(v, -1, 1) - roll(fy * v, 1, 1)
    return out - fz * roll(v, -1, 2) - roll(fz * v, 1, 2)


def inverse(diag):
    return 1.0 / jnp.where(diag > 0.0, diag, 1.0)


def level_of(fx, fx_before, fy, fz, gx, gy, gz, sizes):
    nx, ny, nz = sizes
    diag = fx + jnp.where(gx == 0, 0.0, fx_before)
    diag = diag + fy + jnp.where(gy == 0, 0.0, roll(fy, 1, 1))
    diag = diag + fz + jnp.where(gz == 0, 0.0, roll(fz, 1, 2))
    fx = jnp.where((gx == nx - 1) | (gx == -1), 0.0, fx)
    fy = jnp.where((gy == ny - 1) | (gy == -1), 0.0, fy)
    fz = jnp.where((gz == nz - 1) | (gz == -1), 0.0, fz)
    return fx, fy, fz, diag, inverse(diag)


def loop(start, stop, block, body):
    count = (stop - start) // block
    assert count * block == stop - start

    def step(i, carry):
        body(start + i * block)
        return carry

    lax.fori_loop(0, count, step, 0)


def send_z(r, mask, to_upper, to_lower):
    density = GAS + (LIQUID - GAS) * mask[...].astype(F32)
    turned = roll(density, 64, 2)
    lane = iota(density.shape, 2)
    to_upper[...] = jnp.where(lane >= 64, r[...], turned)
    to_lower[...] = jnp.where(lane < 64, r[...], turned)


def send_y(r, mask, below, above, to_upper, to_lower):
    density = GAS + (LIQUID - GAS) * mask[...].astype(F32)
    low, high = below[...], above[...]
    lane = iota(density.shape, 2)
    r_side = jnp.where(lane < 64, high, low)
    d_side = roll(jnp.where(lane >= 64, high, low), 64, 2)
    for out, rows, line in ((to_upper, slice(8, 16), 7), (to_lower, slice(0, 8), 8)):
        out[0:BX, :, 0:128] = r[:, rows, :]
        out[0:BX, :, 128:256] = r_side[:, rows]
        out[BX : 2 * BX, :, 0:128] = density[:, rows]
        out[BX : 2 * BX, :, 128:256] = d_side[:, rows]
        for x in range(BX):
            at = 2 * BX + x // 8
            out[at, x % 8 : x % 8 + 1, 0:128] = density[x, line : line + 1]
            out[at, x % 8 : x % 8 + 1, 128:256] = d_side[x, line : line + 1]


def send_x(lower, upper, below, above, to_upper, to_lower):
    for out, r_at, d_at, pack in ((to_upper, BX - 8, BX - 9, 3), (to_lower, 0, 0, 0)):
        for tile, source in enumerate((lower, upper, above, below)):
            rows = slice(8 * tile, 8 * tile + 8)
            out[0:8, rows] = source[r_at : r_at + 8]
            out[8:17, rows] = source[BX + d_at : BX + d_at + 9]
        out[17, 0:8] = below[2 * BX + pack]
        out[17, 8:16] = above[2 * BX + pack]
        out[17, 16:32] = jnp.zeros((16, Z0), F32)


def presmooth_0(where, r, faces, inv, d0, d1, start, stop, have_first):
    if not have_first:
        def first(at):
            here = pl.ds(at, 2)
            d0[here] = (FIRST * r[here]) * inv[here]

        loop(start, stop, 2, first)

    def second(at):
        here = pl.ds(at, 2)
        left = r[here] - apply_at(d0, at, 2, faces)
        r[here] = left
        d1[here] = KEEP * d0[here] + GAIN * (left * inv[here])

    loop(start + 1, stop - 1, 2, second)

    def third(at):
        here = pl.ds(at, 2)
        r[here] = r[here] - apply_at(d1, at, 2, faces)

    loop(start + 2, stop - 2, 2, third)


def restrict_0(r, out):
    rows, lanes = row_pairs(16), lane_pairs(256, 0.125)
    for g in range(4):
        block = r[WX + 8 * g : WX + 8 * g + 8, 0:16, :]
        out[4 * g : 4 * g + 4] = coarsen(block, rows, lanes)


def add_own(total, terms, first):
    value = None if first else total[...]
    for term in terms:
        own = term[WX : WX + BX, 0:BY, 0:BZ]
        value = own if value is None else value + own
    total[...] = value


def begin(sizes, where, lower, upper, below, above, x_below, x_above,
          fx, fy, fz, diag, inv, r, total, packed, rho, low, up, raw_x, raw_y, raw_z, d0, d1):
    nx, ny, nz = sizes
    gx0, gy0, gz0 = where[0] * BX, where[1] * BY, where[2] * BZ
    r[0:8] = x_below[0:8]
    r[40:48] = x_above[0:8]
    rho[0:9] = x_below[8:17]
    rho[41:50] = x_above[8:17]
    for tile, source in enumerate((lower, upper, above, below)):
        rows = slice(8 * tile, 8 * tile + 8)
        r[8:40, rows] = source[0:BX]
        rho[9:41, rows] = source[BX : 2 * BX]
    low[0:8] = x_below[17, 0:8]
    up[0:8] = x_below[17, 8:16]
    low[40:48] = x_above[17, 0:8]
    up[40:48] = x_above[17, 8:16]
    low[8:40] = below[2 * BX : 2 * BX + 4].reshape(BX, Z0)
    up[8:40] = above[2 * BX : 2 * BX + 4].reshape(BX, Z0)

    def plane(p):
        shape = (Y0, Z0)
        row, lane = iota(shape, 0), iota(shape, 1)
        gy = gy0 + jnp.where(row < 24, row, row - 32)
        gz = gz0 + jnp.where(lane < 192, lane, lane - 256)
        gx = gx0 + p - WX
        c = rho[p + 1]
        f_x = 2.0 / (c + jnp.where(gx == nx - 1, GAS, rho[p + 2]))
        l_x = jnp.where(gx == 0, 0.0, 2.0 / (c + rho[p]))
        over = jnp.where(row == 23, up[pl.ds(p, 1)], roll(c, -1, 0))
        under = jnp.where(row == 24, low[pl.ds(p, 1)], roll(c, 1, 0))
        f_y = 2.0 / (c + jnp.where(gy == ny - 1, GAS, over))
        l_y = jnp.where(gy == 0, 0.0, 2.0 / (c + under))
        f_z = 2.0 / (c + jnp.where(gz == nz - 1, GAS, roll(c, -1, 1)))
        l_z = jnp.where(gz == 0, 0.0, roll(f_z, 1, 1))
        d = f_x + l_x + f_y + l_y + f_z + l_z
        i = 1.0 / d
        diag[p] = d
        inv[p] = i
        d0[p] = (FIRST * r[p]) * i
        raw_x[p] = f_x[0:16]
        raw_y[p] = f_y[0:16]
        raw_z[p] = f_z[0:16]
        fx[p] = jnp.where((gx == nx - 1) | (gx == -1), 0.0, f_x)
        fy[p] = jnp.where((gy == ny - 1) | (gy == -1), 0.0, f_y)
        fz[p] = jnp.where((gz == nz - 1) | (gz == -1), 0.0, f_z)

    loop(0, X0, 1, plane)
    faces = (fx, fy, fz, diag)
    presmooth_0(where, r, faces, inv, d0, d1, 0, X0, True)
    add_own(total, (d0, d1), True)
    restrict_0(r, packed.at[0:16])
    lanes, odd_lanes = lane_pairs(256, 0.125), lane_pairs(256, 0.125, True)
    for n, (raw, rows, columns) in enumerate((
        (raw_x, row_pairs(16, odd_x=True), lanes),
        (raw_y, row_pairs(16, odd_y=True), lanes),
        (raw_z, row_pairs(16), odd_lanes),
    )):
        for g in range(4):
            block = raw[WX + 8 * g : WX + 8 * g + 8]
            packed[16 * (n + 1) + 4 * g : 16 * (n + 1) + 4 * g + 4] = coarsen(block, rows, columns)


def assemble_1(part, own, below, above, out):
    out[0:16] = below[part]
    out[16:32] = own[part]
    out[32:48] = above[part]


def relax_1(r, faces, inv, d0, d1, start, stop):
    def second(at):
        here = pl.ds(at, 2)
        left = r[here] - apply_at(d0, at, 2, faces)
        r[here] = left
        d1[here] = KEEP * d0[here] + GAIN * (left * inv[here])

    loop(start, stop, 2, second)


def down(sizes, first, where, own, below, above, *refs):
    n1 = tuple(n // 2 for n in sizes)
    n2 = tuple(n // 4 for n in sizes)
    if first:
        (fx, fy, fz, diag, inv, gx2, gy2, gz2, diag2, inv2, r, e, r2_out, e2_out, packed, d0, d1) = refs
    else:
        (fx, fy, fz, diag, inv, gx2, gy2, gz2, diag2, inv2, r, e, r2_out, e2_out, packed, d0, d1) = refs
    ny1 = fx.shape[1]
    ny2 = ny1 // 2
    assemble_1(slice(0, 16), own, below, above, r)
    rows, lanes = row_pairs(ny1), lane_pairs(128, 0.125)
    if first:
        raws = (fx, fy, fz)
        for n, raw in enumerate(raws):
            assemble_1(slice(16 * (n + 1), 16 * (n + 2)), own, below, above, raw)
        odd_lanes = lane_pairs(128, 0.125, True)
        coarse = []
        for raw, rows_matrix, columns in (
            (fx, row_pairs(ny1, odd_x=True), lanes),
            (fy, row_pairs(ny1, odd_y=True), lanes),
            (fz, rows, odd_lanes),
        ):
            coarse.append(jnp.concatenate(
                [coarsen(raw[8 * g : 8 * g + 8], rows_matrix, columns) for g in range(6)], 0))
        shape = (2, ny1, 128)
        gy = lax.rem(where[1] * 8 + iota(shape, 1), n1[1])
        lane = iota(shape, 2)
        gz = where[2] * 64 + jnp.where(lane < 96, lane, lane - 128)

        def planes(n):
            at = X1 - 2 - n
            here = pl.ds(at, 2)
            gx = where[0] * 16 + at - 16 + iota(shape, 0)
            before = jnp.concatenate([fx[pl.ds(jnp.maximum(at - 1, 0), 1)], fx[pl.ds(at, 1)]], 0)
            level = level_of(fx[here], before, fy[here], fz[here], gx, gy, gz, n1)
            fx[here], fy[here], fz[here], diag[here], inv[here] = level
            d0[here] = (FIRST * r[here]) * level[4]

        loop(0, X1, 2, planes)
        shape = (X2, ny2, 128)
        lane = iota(shape, 2)
        at_2 = (
            where[0] * 8 - 8 + iota(shape, 0),
            lax.rem(where[1] * 4 + iota(shape, 1), n2[1]),
            where[2] * 32 + jnp.where(lane < 64, lane, lane - 128),
        )
        raw_2 = tuple(coarse)
        level_2 = level_of(raw_2[0], step_x(raw_2[0], 1), raw_2[1], raw_2[2], *at_2, n2)
        gx2[...], gy2[...], gz2[...], diag2[...], inv2[...] = level_2
        for n, (rows_matrix, columns) in enumerate((
            (row_pairs(ny2, odd_x=True), lanes),
            (row_pairs(ny2, odd_y=True), lanes),
            (row_pairs(ny2), odd_lanes),
        )):
            packed[4 * (n + 1) : 4 * (n + 2)] = coarsen(raw_2[n][8:16], rows_matrix, columns)
    else:
        def begin_1(at):
            here = pl.ds(at, 2)
            d0[here] = (FIRST * r[here]) * inv[here]

        loop(0, X1, 2, begin_1)

    faces = (fx, fy, fz, diag)
    relax_1(r, faces, inv, d0, d1, 1, X1 - 1)

    def third(at):
        here = pl.ds(at, 2)
        r[here] = r[here] - apply_at(d1, at, 2, faces)
        e[here] = d0[here] + d1[here]

    loop(2, X1 - 2, 2, third)
    e[0:2] = d0[0:2]
    e[X1 - 2 : X1] = d0[X1 - 2 : X1]
    r2 = jnp.concatenate([coarsen(r[8 * g : 8 * g + 8], rows, lanes) for g in range(6)], 0)
    faces_2 = (gx2[...], gy2[...], gz2[...], diag2[...])
    d = (FIRST * r2) * inv2[...]
    r2 = r2 - apply_to(d, faces_2)
    d_next = KEEP * d + GAIN * (r2 * inv2[...])
    r2 = r2 - apply_to(d_next, faces_2)
    r2_out[...] = r2
    e2_out[...] = d + d_next
    packed[0:4] = coarsen(r2[8:16], row_pairs(ny2), lanes)


def spread(own, below, above, out):
    lane = iota(own.shape, 2)
    values = jnp.where(lane < 16, own[...], 0.0)
    values = jnp.where((lane >= 16) & (lane < 32), roll(above[...], 16, 2), values)
    values = jnp.where(lane >= 112, roll(below[...], 112, 2), values)
    for d in range(out.shape[0]):
        out[d] = values


def up(sizes, last, where, gathered, *refs):
    n3 = tuple(n // 8 for n in sizes)
    first = not last
    refs = list(refs)
    take = lambda n: [refs.pop(0) for _ in range(n)]
    if last:
        level_3 = take(5)
    gx2, gy2, gz2, diag2, inv2, r2_in, e2_in = take(7)
    fx1, fy1, fz1, diag1, inv1, r1_in, e1_in = take(7)
    fx, fy, fz, diag, inv, r_in, total_in = take(7)
    if first:
        level_3 = take(5)
        r, total, packed = take(3)
    else:
        pressure, residual = take(2)
        (r,) = take(1)
    e3, p1, r1, a1, b1, c1, p0, d0, d1 = take(9)

    count = gathered.shape[0]
    ny3 = gathered.shape[2]
    shape = (4 * count, ny3, 128)
    r3 = gathered[:, 0:4].reshape(shape)
    if first:
        raw = [gathered[:, 4 * n : 4 * n + 4].reshape(shape) for n in (1, 2, 3)]
        lane = iota(shape, 2)
        at = (
            iota(shape, 0),
            lax.rem(where[1] * 2 + iota(shape, 1), n3[1]),
            where[2] * 16 + jnp.where(lane < 64, lane, lane - 128),
        )
        values = level_of(raw[0], step_x(raw[0], 1), raw[1], raw[2], *at, n3)
        for ref, value in zip(level_3, values):
            ref[...] = value
    faces = tuple(ref[...] for ref in level_3[:4])
    inv3 = level_3[4][...]
    d = (COARSE_FIRST * r3) * inv3
    total3 = d
    for keep, gain in COARSE_STEPS:
        r3 = r3 - apply_to(d, faces)
        d = keep * d + gain * (r3 * inv3)
        total3 = total3 + d
    e3[...] = total3

    copies_rows, copies_lanes = row_copies(2 * ny3), lane_copies(128)
    blocks = []
    for g in range(3):
        start = lax.rem(where[0] * 4 + 4 * (g - 1) + 4 * count, 4 * count)
        blocks.append(refine(e3[pl.ds(start, 4)], copies_rows, copies_lanes))
    p = jnp.concatenate(blocks, 0)
    faces = (gx2[...], gy2[...], gz2[...], diag2[...])
    r2 = r2_in[...] - apply_to(p, faces)
    d = (FIRST * r2) * inv2[...]
    r2 = r2 - apply_to(d, faces)
    d_next = KEEP * d + GAIN * (r2 * inv2[...])
    e2 = e2_in[...] + p + d + d_next

    copies_rows = row_copies(4 * ny3)
    for g in range(4):
        p1[8 + 8 * g : 16 + 8 * g] = refine(e2[4 + 4 * g : 8 + 4 * g], copies_rows, copies_lanes)
    faces = (fx1, fy1, fz1, diag1)

    def lift_1(at):
        here = pl.ds(at, 2)
        left = r1_in[here] - apply_at(p1, at, 2, faces)
        r1[here] = left
        a1[here] = (FIRST * left) * inv1[here]

    loop(11, 37, 2, lift_1)
    relax_1(r1, faces, inv1, a1, b1, 12, 36)

    def sum_1(at):
        here = pl.ds(at, 4)
        value = e1_in[here] + p1[here] + a1[here] + b1[here]
        c1[here, 0:8] = value[:, 0:8]
        tile = (4, 8, 128)
        c1[here, 8:16] = jnp.where(iota(tile, 1) < 4, value[:, 8:16], value[:, -8:])

    loop(12, 36, 4, sum_1)

    copies_rows, copies_lanes = row_copies(32), lane_copies(256)
    for g in range(6):
        p0[8 * g : 8 * g + 8] = refine(c1[12 + 4 * g : 16 + 4 * g], copies_rows, copies_lanes)
    faces = (fx, fy, fz, diag)
    begin_at, end_at = (6, 42) if last else (2, 46)

    def lift_0(at):
        here = pl.ds(at, 2)
        left = r_in[here] - apply_at(p0, at, 2, faces)
        r[here] = left
        d0[here] = (FIRST * left) * inv[here]

    loop(begin_at, end_at, 2, lift_0)
    presmooth_0(where, r, faces, inv, d0, d1, begin_at, end_at, True)
    if last:
        pressure[...] = total_in[...]
        add_own(pressure, (p0, d0, d1), False)
        residual[...] = r[WX : WX + BX, 0:BY, 0:BZ]
        return
    total[...] = total_in[...]
    add_own(total, (p0, d0, d1), False)
    presmooth_0(where, r, faces, inv, d0, d1, 4, 44, False)
    add_own(total, (d0, d1), False)
    restrict_0(r, packed)


def call(kernel, name, args, outs, scratch=()):
    vmem = pl.BlockSpec(memory_space=pltpu.VMEM)
    smem = pl.BlockSpec(memory_space=pltpu.SMEM)
    return pl.pallas_call(
        kernel,
        out_shape=[jax.ShapeDtypeStruct(s, F32) for s in outs],
        in_specs=[smem if a.ndim == 1 else vmem for a in args],
        out_specs=[vmem] * len(outs),
        scratch_shapes=[pltpu.VMEM(s, F32) for s in scratch],
        compiler_params=pltpu.CompilerParams(vmem_limit_bytes=VMEM_LIMIT),
        name=name,
        interpret=INTERPRET,
    )(*args)


def from_below(array, axis):
    n = lax.axis_size(axis)
    return lax.ppermute(array, axis, [(i, (i + 1) % n) for i in range(n)])


def from_above(array, axis, by=1):
    n = lax.axis_size(axis)
    return lax.ppermute(array, axis, [((i + by) % n, i) for i in range(n)])


def body(right_side, phase_mask):
    nx, ny, nz = (lax.axis_size(a) for a in ("gx", "gy", "gz"))
    sizes = (nx * BX, ny * BY, nz * BZ)
    where = jnp.stack([lax.axis_index(a) for a in ("gx", "gy", "gz")]).astype(jnp.int32)
    own = (BX, BY, BZ)
    to_upper, to_lower = call(send_z, "send_z", (right_side, phase_mask), [own] * 2)
    below, above = from_below(to_upper, "gz"), from_above(to_lower, "gz")
    part = (2 * BX + 4, 8, Z0)
    upper, lower = call(send_y, "send_y", (right_side, phase_mask, below, above), [part] * 2)
    below, above = from_below(upper, "gy"), from_above(lower, "gy")
    to_upper, to_lower = call(send_x, "send_x", (lower, upper, below, above), [(18, Y0, Z0)] * 2)
    x_below, x_above = from_below(to_upper, "gx"), from_above(to_lower, "gx")

    full = (X0, Y0, Z0)
    *faces_0, r0, total, packed = call(
        functools.partial(begin, sizes), "begin",
        (where, lower, upper, below, above, x_below, x_above),
        [full] * 6 + [own, (64, 8, 128)],
        [(X0 + 2, Y0, Z0), (X0, Z0), (X0, Z0)] + [(X0, BY, Z0)] * 3 + [full] * 2,
    )
    full_1 = (X1, 8 * ny, 128)
    full_2 = (X2, 4 * ny, 128)
    levels = []
    level_3 = []
    for cycle in range(2):
        first = cycle == 0
        parts = [packed] + [from_above(packed, "gy", s) for s in range(1, ny)]
        rows = jnp.concatenate(parts, 1)
        below, above = from_below(rows, "gx"), from_above(rows, "gx")
        state = [full_1] * 2 + [full_2] * 2
        planes = 16 if first else 4
        made = call(
            functools.partial(down, sizes, first), "down",
            (where, rows, below, above, *levels),
            ([full_1] * 5 + [full_2] * 5 if first else []) + state + [(planes, 2 * ny, 128)],
            [full_1] * 2,
        )
        if first:
            levels, made = made[:10], made[10:]
        r1, e1, r2, e2, packed = made
        below, above = from_below(packed, "gz"), from_above(packed, "gz")
        (copies,) = call(spread, "spread", (packed, below, above), [(nx,) + packed.shape])
        gathered = lax.all_to_all(copies, "gx", 0, 0)
        args = (where, gathered, *level_3, *levels[5:], r2, e2, *levels[:5], r1, e1, *faces_0, r0, total)
        full_3 = (4 * nx, 2 * ny, 128)
        scratch = [full_3] + [full_1] * 4 + [(X1, 16, 128)] + [full] * 3
        if first:
            *level_3, r0, total, packed = call(
                functools.partial(up, sizes, False), "up", args,
                [full_3] * 5 + [full, own, (16, 8, 128)], scratch)
        else:
            return tuple(call(functools.partial(up, sizes, True), "up_last", args, [own] * 2, [full] + scratch))


def solution(mesh):
    spec = P("gx", "gy", "gz")
    return jax.shard_map(body, mesh=mesh, in_specs=(spec, spec), out_specs=(spec, spec), check_vma=False)
```

```python
import functools

import jax
import jax.numpy as jnp
from jax import lax
from jax.experimental import pallas as pl
from jax.experimental.pallas import tpu as pltpu
from jax.sharding import PartitionSpec as P

COARSE_ITERS = 8
SMOOTH_LOW = 0.25
SMOOTH_HIGH = 2.0
COARSE_LOW = 0.02
LIQUID = 10.0
GAS = 1.0

INTERPRET = False
VMEM_LIMIT = 40 * 1024 * 1024

BX, BY, BZ = 32, 16, 128
WX = 8
X0, Y0, Z0 = BX + 2 * WX, 32, 256
X1, Y1G, Z1 = 48, 8, 128
X2 = 24
F32 = jnp.float32
BF16 = jnp.bfloat16
DOWN, UP = 3, 3
UC, B0, U0, B1 = 4, 4, 2, 16


def chebyshev(low, degree):
    theta = 0.5 * (SMOOTH_HIGH + low)
    delta = 0.5 * (SMOOTH_HIGH - low)
    sigma = theta / delta
    rho_old = 1.0 / sigma
    steps = []
    for _ in range(1, degree):
        rho_new = 1.0 / (2.0 * sigma - rho_old)
        steps.append((rho_new * rho_old, 2.0 * rho_new / delta))
        rho_old = rho_new
    return 1.0 / theta, steps


FIRST, ((KEEP, GAIN),) = chebyshev(SMOOTH_LOW, 2)
COARSE_FIRST, COARSE_STEPS = chebyshev(COARSE_LOW, COARSE_ITERS)


def roll(values, shift, axis):
    return pltpu.roll(values, shift % values.shape[axis], axis)


def iota(shape, dim):
    return lax.broadcasted_iota(jnp.int32, shape, dim)


def split(values, terms):
    parts = []
    for n in range(terms):
        part = values.astype(BF16)
        parts.append(part)
        if n + 1 < terms:
            values = values - part.astype(F32)
    return parts


def times(values, matrix, terms):
    return sum(jnp.dot(p, matrix, preferred_element_type=F32) for p in split(values, terms))


def times_left(matrix, values, terms):
    return sum(jnp.dot(matrix, p, preferred_element_type=F32) for p in split(values, terms))


def lane_pairs(fine, weight, odd_only=False):
    z = iota((fine, 128), 0)
    half = z >> 1
    if fine == 128:
        half = jnp.where(z >= 96, half + 64, half)
    hit = half == iota((fine, 128), 1)
    if odd_only:
        hit = hit & ((z & 1) == 1)
    return jnp.where(hit, weight, 0.0).astype(BF16)


def lane_copies(fine):
    z = iota((128, fine), 1)
    half = z >> 1
    if fine == 128:
        half = jnp.where(z >= 96, half + 64, half)
    return jnp.where(half == iota((128, fine), 0), 1.0, 0.0).astype(BF16)


def row_pairs(rows, odd_x=False, odd_y=False):
    shape = (2 * rows, 8 * rows)
    shift = rows.bit_length() - 1
    c, f = iota(shape, 0), iota(shape, 1)
    cx, cy = c >> (shift - 1), c & (rows // 2 - 1)
    x, y = f >> shift, f & (rows - 1)
    hit = ((x >> 1) == cx) & ((y >> 1) == cy)
    if odd_x:
        hit = hit & ((x & 1) == 1)
    if odd_y:
        hit = hit & ((y & 1) == 1)
    return jnp.where(hit, 1.0, 0.0).astype(BF16)


def row_copies(rows):
    shape = (8 * rows, 2 * rows)
    shift = rows.bit_length() - 1
    f, c = iota(shape, 0), iota(shape, 1)
    hit = ((f >> (shift + 1)) == (c >> (shift - 1))) & (((f & (rows - 1)) >> 1) == (c & (rows // 2 - 1)))
    return jnp.where(hit, 1.0, 0.0).astype(BF16)


def coarsen(block, rows_matrix, lanes_matrix):
    planes, rows, lanes = block.shape
    out = times(times_left(rows_matrix, block.reshape(planes * rows, lanes), DOWN), lanes_matrix, DOWN)
    return out.reshape(4, rows // 2, 128)


def refine(block, rows_matrix, lanes_matrix):
    planes, rows, lanes = block.shape
    out = times_left(rows_matrix, times(block.reshape(planes * rows, lanes), lanes_matrix, UP), UP)
    return out.reshape(8, 2 * rows, lanes_matrix.shape[1])


def apply_at(v, at, planes, faces):
    fx, fy, fz, diag = faces
    here = pl.ds(at, planes)
    c = v[here]
    y, z = fy[here], fz[here]
    out = diag[here] * c - fx[here] * v[pl.ds(at + 1, planes)] - fx[pl.ds(at - 1, planes)] * v[pl.ds(at - 1, planes)]
    out = out - y * roll(c, -1, 1) - roll(y * c, 1, 1)
    return out - z * roll(c, -1, 2) - roll(z * c, 1, 2)


def step_x(values, by):
    if by > 0:
        return jnp.concatenate([values[-1:], values[:-1]], 0)
    return jnp.concatenate([values[1:], values[:1]], 0)


def apply_to(v, faces):
    fx, fy, fz, diag = faces
    out = diag * v - fx * step_x(v, -1) - step_x(fx * v, 1)
    out = out - fy * roll(v, -1, 1) - roll(fy * v, 1, 1)
    return out - fz * roll(v, -1, 2) - roll(fz * v, 1, 2)


def inverse(diag):
    return 1.0 / jnp.where(diag > 0.0, diag, 1.0)


def level_of(fx, fx_before, fy, fz, gx, gy, gz, sizes):
    nx, ny, nz = sizes
    diag = fx + jnp.where(gx == 0, 0.0, fx_before)
    diag = diag + fy + jnp.where(gy == 0, 0.0, roll(fy, 1, 1))
    diag = diag + fz + jnp.where(gz == 0, 0.0, roll(fz, 1, 2))
    fx = jnp.where((gx == nx - 1) | (gx == -1), 0.0, fx)
    fy = jnp.where((gy == ny - 1) | (gy == -1), 0.0, fy)
    fz = jnp.where((gz == nz - 1) | (gz == -1), 0.0, fz)
    return fx, fy, fz, diag, inverse(diag)


def loop(start, stop, block, body, unroll=1):
    count = (stop - start) // block

    def step(i, carry):
        body(start + i * block, block)
        return carry

    if count:
        lax.fori_loop(0, count, step, 0, unroll=unroll)
    rest = stop - start - count * block
    if rest:
        body(stop - rest, rest)


def send_y(r, mask, to_upper, to_lower):
    density = GAS + (LIQUID - GAS) * mask[...].astype(F32)
    for out, rows, line in ((to_upper, slice(8, 16), 7), (to_lower, slice(0, 8), 8)):
        out[0:BX] = r[:, rows, :]
        out[BX : 2 * BX] = density[:, rows]
        for x in range(BX):
            out[2 * BX + x // 8, x % 8 : x % 8 + 1] = density[x, line : line + 1]


def send_x(lower, upper, below, above, to_upper, to_lower):
    for out, r_at, d_at, pack in ((to_upper, BX - 8, BX - 9, 3), (to_lower, 0, 0, 0)):
        for tile, source in enumerate((lower, upper, above, below)):
            rows = slice(8 * tile, 8 * tile + 8)
            out[0:8, rows] = source[r_at : r_at + 8]
            out[8:17, rows] = source[BX + d_at : BX + d_at + 9]
        out[17, 0:8] = below[2 * BX + pack]
        out[17, 8:16] = above[2 * BX + pack]
        out[17, 16:32] = jnp.zeros((16, 128), F32)


def send_z(lower, upper, below, above, x_below, x_above, to_upper, to_lower):
    for out, high in ((to_upper, True), (to_lower, False)):
        def beside(one, two):
            lane = iota(one.shape, one.ndim - 1)
            return jnp.where((lane >= 64) == high, one, roll(two, 64, one.ndim - 1))

        out[0:8] = beside(x_below[0:8], x_below[9:17])
        out[40:48] = beside(x_above[0:8], x_above[8:16])
        out[48] = beside(x_below[8], x_above[16])
        for tile, source in enumerate((lower, upper, above, below)):
            out[8:40, 8 * tile : 8 * tile + 8] = beside(source[0:BX], source[BX : 2 * BX])
        out[49, 0:8] = beside(x_below[17, 0:8], x_below[17, 8:16])
        for n in range(4):
            at = 8 * (n + 1)
            out[49 + at // 32, at % 32 : at % 32 + 8] = beside(below[2 * BX + n], above[2 * BX + n])
        out[50, 8:16] = beside(x_above[17, 0:8], x_above[17, 8:16])
        out[50, 16:32] = jnp.zeros((16, 128), F32)


def presmooth_0(where, r, faces, inv, d0, d1, start, stop, have_first):
    if not have_first:
        def first(at, n):
            here = pl.ds(at, n)
            d0[here] = (FIRST * r[here]) * inv[here]

        loop(start, stop, B0, first, U0)

    def second(at, n):
        here = pl.ds(at, n)
        left = r[here] - apply_at(d0, at, n, faces)
        r[here] = left
        d1[here] = KEEP * d0[here] + GAIN * (left * inv[here])

    loop(start + 1, stop - 1, B0, second, U0)

    def third(at, n):
        here = pl.ds(at, n)
        r[here] = r[here] - apply_at(d1, at, n, faces)

    loop(start + 2, stop - 2, B0, third, U0)


def restrict_0(r, out):
    rows, lanes = row_pairs(16), lane_pairs(256, 0.125)
    for g in range(4):
        block = r[WX + 8 * g : WX + 8 * g + 8, 0:16, :]
        out[4 * g : 4 * g + 4] = coarsen(block, rows, lanes)


def add_own(total, terms, first):
    value = None if first else total[...]
    for term in terms:
        own = term[WX : WX + BX, 0:BY, 0:BZ]
        value = own if value is None else value + own
    total[...] = value


def face(total):
    return jnp.where(total < 5.0, 1.0, jnp.where(total < 15.0, 2.0 / 11.0, 0.1))


def begin(sizes, where, lower, upper, below, above, x_below, x_above, z_below, z_above,
          fx, fy, fz, diag, inv, r, total, packed, rho, low, up, raw_x, raw_y, raw_z, d0, d1):
    nx, ny, nz = sizes
    gx0, gy0, gz0 = where[0] * BX, where[1] * BY, where[2] * BZ
    own, side = slice(0, 128), slice(128, 256)
    r[0:8, :, own] = x_below[0:8]
    r[40:48, :, own] = x_above[0:8]
    rho[0:9, :, own] = x_below[8:17]
    rho[41:50, :, own] = x_above[8:17]
    for tile, source in enumerate((lower, upper, above, below)):
        rows = slice(8 * tile, 8 * tile + 8)
        r[8:40, rows, own] = source[0:BX]
        rho[9:41, rows, own] = source[BX : 2 * BX]
    low[0:8, own] = x_below[17, 0:8]
    up[0:8, own] = x_below[17, 8:16]
    low[40:48, own] = x_above[17, 0:8]
    up[40:48, own] = x_above[17, 8:16]
    for n in range(4):
        low[8 + 8 * n : 16 + 8 * n, own] = below[2 * BX + n]
        up[8 + 8 * n : 16 + 8 * n, own] = above[2 * BX + n]

    def sides(at):
        one, two = z_above[at], z_below[at]
        axis = one.ndim - 1
        lane = iota(one.shape, axis)
        return jnp.where(lane < 64, one, two), roll(jnp.where(lane >= 64, one, two), 64, axis)

    def side_planes(p, n):
        r[pl.ds(p, n), :, side], rho[pl.ds(p + 1, n), :, side] = sides(pl.ds(p, n))

    loop(0, X0, 4, side_planes)
    rho[0, :, side], rho[49, :, side] = sides(48)
    low[0:32, side], up[0:32, side] = sides(49)
    low_rest, up_rest = sides(50)
    low[32:48, side], up[32:48, side] = low_rest[0:16], up_rest[0:16]

    def plane(p, n):
        shape = (Y0, Z0)
        row, lane = iota(shape, 0), iota(shape, 1)
        gy = gy0 + jnp.where(row < 24, row, row - 32)
        gz = gz0 + jnp.where(lane < 192, lane, lane - 256)
        gx = gx0 + p - WX
        c = rho[p + 1]
        f_x = face(c + jnp.where(gx == nx - 1, GAS, rho[p + 2]))
        l_x = jnp.where(gx == 0, 0.0, face(c + rho[p]))
        over = jnp.where(row == 23, up[pl.ds(p, 1)], roll(c, -1, 0))
        under = jnp.where(row == 24, low[pl.ds(p, 1)], roll(c, 1, 0))
        f_y = face(c + jnp.where(gy == ny - 1, GAS, over))
        l_y = jnp.where(gy == 0, 0.0, face(c + under))
        f_z = face(c + jnp.where(gz == nz - 1, GAS, roll(c, -1, 1)))
        l_z = jnp.where(gz == 0, 0.0, roll(f_z, 1, 1))
        d = f_x + l_x + f_y + l_y + f_z + l_z
        i = 1.0 / d
        diag[p] = d
        inv[p] = i
        d0[p] = (FIRST * r[p]) * i
        raw_x[p] = f_x[0:16]
        raw_y[p] = f_y[0:16]
        raw_z[p] = f_z[0:16]
        fx[p] = jnp.where((gx == nx - 1) | (gx == -1), 0.0, f_x)
        fy[p] = jnp.where((gy == ny - 1) | (gy == -1), 0.0, f_y)
        fz[p] = jnp.where((gz == nz - 1) | (gz == -1), 0.0, f_z)

    loop(0, X0, 1, plane, UC)
    faces = (fx, fy, fz, diag)
    presmooth_0(where, r, faces, inv, d0, d1, 0, X0, True)
    add_own(total, (d0, d1), True)
    restrict_0(r, packed.at[0:16])
    lanes, odd_lanes = lane_pairs(256, 0.125), lane_pairs(256, 0.125, True)
    for n, (raw, rows, columns) in enumerate((
        (raw_x, row_pairs(16, odd_x=True), lanes),
        (raw_y, row_pairs(16, odd_y=True), lanes),
        (raw_z, row_pairs(16), odd_lanes),
    )):
        for g in range(4):
            block = raw[WX + 8 * g : WX + 8 * g + 8]
            packed[16 * (n + 1) + 4 * g : 16 * (n + 1) + 4 * g + 4] = coarsen(block, rows, columns)


def assemble_1(part, own, below, above, out):
    out[0:16] = below[part]
    out[16:32] = own[part]
    out[32:48] = above[part]


def relax_1(r, faces, inv, d0, d1, start, stop):
    def second(at, n):
        here = pl.ds(at, n)
        left = r[here] - apply_at(d0, at, n, faces)
        r[here] = left
        d1[here] = KEEP * d0[here] + GAIN * (left * inv[here])

    loop(start, stop, B1, second)


def down(sizes, first, where, own, below, above, *refs):
    n1 = tuple(n // 2 for n in sizes)
    n2 = tuple(n // 4 for n in sizes)
    if first:
        (fx, fy, fz, diag, inv, gx2, gy2, gz2, diag2, inv2, r, e, r2_out, e2_out, packed, d0, d1) = refs
    else:
        (fx, fy, fz, diag, inv, gx2, gy2, gz2, diag2, inv2, r, e, r2_out, e2_out, packed, d0, d1) = refs
    ny1 = fx.shape[1]
    ny2 = ny1 // 2
    assemble_1(slice(0, 16), own, below, above, r)
    rows, lanes = row_pairs(ny1), lane_pairs(128, 0.125)
    if first:
        raws = (fx, fy, fz)
        for n, raw in enumerate(raws):
            assemble_1(slice(16 * (n + 1), 16 * (n + 2)), own, below, above, raw)
        odd_lanes = lane_pairs(128, 0.125, True)
        coarse = []
        for raw, rows_matrix, columns in (
            (fx, row_pairs(ny1, odd_x=True), lanes),
            (fy, row_pairs(ny1, odd_y=True), lanes),
            (fz, rows, odd_lanes),
        ):
            coarse.append(jnp.concatenate(
                [coarsen(raw[8 * g : 8 * g + 8], rows_matrix, columns) for g in range(6)], 0))
        shape = (B1, ny1, 128)
        gy = lax.rem(where[1] * 8 + iota(shape, 1), n1[1])
        lane = iota(shape, 2)
        gz = where[2] * 64 + jnp.where(lane < 96, lane, lane - 128)

        def planes(n, count):
            at = X1 - B1 - n
            here = pl.ds(at, B1)
            gx = where[0] * 16 + at - 16 + iota(shape, 0)
            c = fx[here]
            before = jnp.concatenate([fx[pl.ds(jnp.maximum(at - 1, 0), 1)], c[:-1]], 0)
            level = level_of(c, before, fy[here], fz[here], gx, gy, gz, n1)
            fx[here], fy[here], fz[here], diag[here], inv[here] = level
            d0[here] = (FIRST * r[here]) * level[4]

        loop(0, X1, B1, planes)
        shape = (X2, ny2, 128)
        lane = iota(shape, 2)
        at_2 = (
            where[0] * 8 - 8 + iota(shape, 0),
            lax.rem(where[1] * 4 + iota(shape, 1), n2[1]),
            where[2] * 32 + jnp.where(lane < 64, lane, lane - 128),
        )
        raw_2 = tuple(coarse)
        level_2 = level_of(raw_2[0], step_x(raw_2[0], 1), raw_2[1], raw_2[2], *at_2, n2)
        gx2[...], gy2[...], gz2[...], diag2[...], inv2[...] = level_2
        for n, (rows_matrix, columns) in enumerate((
            (row_pairs(ny2, odd_x=True), lanes),
            (row_pairs(ny2, odd_y=True), lanes),
            (row_pairs(ny2), odd_lanes),
        )):
            coarse[n] = coarsen(raw_2[n][8:16], rows_matrix, columns)
    else:
        def begin_1(at, n):
            here = pl.ds(at, n)
            d0[here] = (FIRST * r[here]) * inv[here]

        loop(0, X1, B1, begin_1)

    faces = (fx, fy, fz, diag)
    relax_1(r, faces, inv, d0, d1, 1, X1 - 1)

    def third(at, n):
        here = pl.ds(at, n)
        r[here] = r[here] - apply_at(d1, at, n, faces)
        e[here] = d0[here] + d1[here]

    loop(2, X1 - 2, B1, third)
    e[0:2] = d0[0:2]
    e[X1 - 2 : X1] = d0[X1 - 2 : X1]
    r2 = jnp.concatenate([coarsen(r[8 * g : 8 * g + 8], rows, lanes) for g in range(6)], 0)
    faces_2 = (gx2[...], gy2[...], gz2[...], diag2[...])
    d = (FIRST * r2) * inv2[...]
    r2 = r2 - apply_to(d, faces_2)
    d_next = KEEP * d + GAIN * (r2 * inv2[...])
    r2 = r2 - apply_to(d_next, faces_2)
    r2_out[...] = r2
    e2_out[...] = d + d_next
    sent = coarsen(r2[8:16], row_pairs(ny2), lanes)
    if first:
        lane = iota(sent.shape, 2)
        for n in range(3):
            at = 16 * (n + 1)
            sent = jnp.where(lane < at, sent, roll(coarse[n], at, 2))
    packed[...] = sent


def spread(own, below, above, out):
    shape = own.shape
    lane = iota(shape, 2)
    arrays = 2 * (out.shape[1] // shape[0]) if out.shape[1] > shape[0] else 1
    values = []
    for n in range(arrays):
        start = 64 * (n % 2)
        here = lane - start
        value = jnp.where(here < 16, roll(own[...], start - 16 * n, 2), 0.0)
        value = jnp.where((here >= 16) & (here < 32), roll(above[...], start + 16 - 16 * n, 2), value)
        value = jnp.where(here >= 48, roll(below[...], start + 48 - 16 * n, 2), value)
        if n % 2:
            values[-1] = jnp.where(here < 0, values[-1], value)
        else:
            values.append(value)
    for d in range(out.shape[0]):
        for n, value in enumerate(values):
            out[d, shape[0] * n : shape[0] * (n + 1)] = value


def unspread(gathered, n):
    count, _, rows, lanes = gathered.shape
    value = gathered[:, 4 * (n // 2) : 4 * (n // 2) + 4].reshape(4 * count, rows, lanes)
    lane = iota(value.shape, 2)
    near, far = (roll(value, 64, 2), value) if n % 2 else (value, roll(value, 64, 2))
    return jnp.where(lane < 32, near, jnp.where(lane >= 112, far, 0.0))


def up(sizes, last, where, gathered, *refs):
    n3 = tuple(n // 8 for n in sizes)
    first = not last
    refs = list(refs)
    take = lambda n: [refs.pop(0) for _ in range(n)]
    if last:
        level_3 = take(5)
    gx2, gy2, gz2, diag2, inv2, r2_in, e2_in = take(7)
    fx1, fy1, fz1, diag1, inv1, r1_in, e1_in = take(7)
    fx, fy, fz, diag, inv, r_in, total_in = take(7)
    if first:
        level_3 = take(5)
        r, total, packed = take(3)
    else:
        pressure, residual = take(2)
        (r,) = take(1)
    e3, p1, r1, a1, b1, c1, p0, d0, d1 = take(9)

    count = gathered.shape[0]
    ny3 = gathered.shape[2]
    shape = (4 * count, ny3, 128)
    r3 = unspread(gathered, 0)
    if first:
        raw = [unspread(gathered, n) for n in (1, 2, 3)]
        lane = iota(shape, 2)
        at = (
            iota(shape, 0),
            lax.rem(where[1] * 2 + iota(shape, 1), n3[1]),
            where[2] * 16 + jnp.where(lane < 64, lane, lane - 128),
        )
        values = level_of(raw[0], step_x(raw[0], 1), raw[1], raw[2], *at, n3)
        for ref, value in zip(level_3, values):
            ref[...] = value
    faces = tuple(ref[...] for ref in level_3[:4])
    inv3 = level_3[4][...]
    d = (COARSE_FIRST * r3) * inv3
    total3 = d
    for keep, gain in COARSE_STEPS:
        r3 = r3 - apply_to(d, faces)
        d = keep * d + gain * (r3 * inv3)
        total3 = total3 + d
    e3[...] = total3

    copies_rows, copies_lanes = row_copies(2 * ny3), lane_copies(128)
    blocks = []
    for g in range(3):
        start = lax.rem(where[0] * 4 + 4 * (g - 1) + 4 * count, 4 * count)
        blocks.append(refine(e3[pl.ds(start, 4)], copies_rows, copies_lanes))
    p = jnp.concatenate(blocks, 0)
    faces = (gx2[...], gy2[...], gz2[...], diag2[...])
    r2 = r2_in[...] - apply_to(p, faces)
    d = (FIRST * r2) * inv2[...]
    r2 = r2 - apply_to(d, faces)
    d_next = KEEP * d + GAIN * (r2 * inv2[...])
    e2 = e2_in[...] + p + d + d_next

    copies_rows = row_copies(4 * ny3)
    for g in range(4):
        p1[8 + 8 * g : 16 + 8 * g] = refine(e2[4 + 4 * g : 8 + 4 * g], copies_rows, copies_lanes)
    faces = (fx1, fy1, fz1, diag1)

    def lift_1(at, n):
        here = pl.ds(at, n)
        left = r1_in[here] - apply_at(p1, at, n, faces)
        r1[here] = left
        a1[here] = (FIRST * left) * inv1[here]

    loop(11, 37, B1, lift_1)
    relax_1(r1, faces, inv1, a1, b1, 12, 36)

    def sum_1(at, n):
        here = pl.ds(at, n)
        value = e1_in[here] + p1[here] + a1[here] + b1[here]
        c1[here, 0:8] = value[:, 0:8]
        tile = (n, 8, 128)
        c1[here, 8:16] = jnp.where(iota(tile, 1) < 4, value[:, 8:16], value[:, -8:])

    loop(12, 36, B1, sum_1)

    copies_rows, copies_lanes = row_copies(32), lane_copies(256)
    for g in range(6):
        p0[8 * g : 8 * g + 8] = refine(c1[12 + 4 * g : 16 + 4 * g], copies_rows, copies_lanes)
    faces = (fx, fy, fz, diag)
    begin_at, end_at = (6, 42) if last else (2, 46)

    def lift_0(at, n):
        here = pl.ds(at, n)
        left = r_in[here] - apply_at(p0, at, n, faces)
        r[here] = left
        d0[here] = (FIRST * left) * inv[here]

    loop(begin_at, end_at, B0, lift_0, U0)
    presmooth_0(where, r, faces, inv, d0, d1, begin_at, end_at, True)
    if last:
        pressure[...] = total_in[...]
        add_own(pressure, (p0, d0, d1), False)
        residual[...] = r[WX : WX + BX, 0:BY, 0:BZ]
        return
    total[...] = total_in[...]
    add_own(total, (p0, d0, d1), False)
    presmooth_0(where, r, faces, inv, d0, d1, 4, 44, False)
    add_own(total, (d0, d1), False)
    restrict_0(r, packed)


def call(kernel, name, args, outs, scratch=()):
    vmem = pl.BlockSpec(memory_space=pltpu.VMEM)
    smem = pl.BlockSpec(memory_space=pltpu.SMEM)
    return pl.pallas_call(
        kernel,
        out_shape=[jax.ShapeDtypeStruct(s, F32) for s in outs],
        in_specs=[smem if a.ndim == 1 else vmem for a in args],
        out_specs=[vmem] * len(outs),
        scratch_shapes=[pltpu.VMEM(s, F32) for s in scratch],
        compiler_params=pltpu.CompilerParams(vmem_limit_bytes=VMEM_LIMIT),
        name=name,
        interpret=INTERPRET,
    )(*args)


def from_below(array, axis):
    n = lax.axis_size(axis)
    return lax.ppermute(array, axis, [(i, (i + 1) % n) for i in range(n)])


def from_above(array, axis, by=1):
    n = lax.axis_size(axis)
    return lax.ppermute(array, axis, [((i + by) % n, i) for i in range(n)])


def body(right_side, phase_mask):
    nx, ny, nz = (lax.axis_size(a) for a in ("gx", "gy", "gz"))
    sizes = (nx * BX, ny * BY, nz * BZ)
    where = jnp.stack([lax.axis_index(a) for a in ("gx", "gy", "gz")]).astype(jnp.int32)
    own = (BX, BY, BZ)
    upper, lower = call(send_y, "send_y", (right_side, phase_mask), [(2 * BX + 4, 8, 128)] * 2)
    below, above = from_below(upper, "gy"), from_above(lower, "gy")
    to_upper, to_lower = call(send_x, "send_x", (lower, upper, below, above), [(18, Y0, 128)] * 2)
    x_below, x_above = from_below(to_upper, "gx"), from_above(to_lower, "gx")
    pieces = (lower, upper, below, above, x_below, x_above)
    to_upper, to_lower = call(send_z, "send_z", pieces, [(51, Y0, 128)] * 2)
    z_below, z_above = from_below(to_upper, "gz"), from_above(to_lower, "gz")

    full = (X0, Y0, Z0)
    *faces_0, r0, total, packed = call(
        functools.partial(begin, sizes), "begin",
        (where, *pieces, z_below, z_above),
        [full] * 6 + [own, (64, 8, 128)],
        [(X0 + 2, Y0, Z0), (X0, Z0), (X0, Z0)] + [(X0, BY, Z0)] * 3 + [full] * 2,
    )
    full_1 = (X1, 8 * ny, 128)
    full_2 = (X2, 4 * ny, 128)
    levels = []
    level_3 = []
    for cycle in range(2):
        first = cycle == 0
        parts = [packed] + [from_above(packed, "gy", s) for s in range(1, ny)]
        rows = jnp.concatenate(parts, 1)
        below, above = from_below(rows, "gx"), from_above(rows, "gx")
        state = [full_1] * 2 + [full_2] * 2
        made = call(
            functools.partial(down, sizes, first), "down",
            (where, rows, below, above, *levels),
            ([full_1] * 5 + [full_2] * 5 if first else []) + state + [(4, 2 * ny, 128)],
            [full_1] * 2,
        )
        if first:
            levels, made = made[:10], made[10:]
        r1, e1, r2, e2, packed = made
        below, above = from_below(packed, "gz"), from_above(packed, "gz")
        (copies,) = call(spread, "spread", (packed, below, above), [(nx, 8 if first else 4, 2 * ny, 128)])
        gathered = lax.all_to_all(copies, "gx", 0, 0)
        args = (where, gathered, *level_3, *levels[5:], r2, e2, *levels[:5], r1, e1, *faces_0, r0, total)
        full_3 = (4 * nx, 2 * ny, 128)
        scratch = [full_3] + [full_1] * 4 + [(X1, 16, 128)] + [full] * 3
        if first:
            *level_3, r0, total, packed = call(
                functools.partial(up, sizes, False), "up", args,
                [full_3] * 5 + [full, own, (16, 8, 128)], scratch)
        else:
            return tuple(call(functools.partial(up, sizes, True), "up_last", args, [own] * 2, [full] + scratch))


def solution(mesh):
    spec = P("gx", "gy", "gz")
    return jax.shard_map(body, mesh=mesh, in_specs=(spec, spec), out_specs=(spec, spec), check_vma=False)
```

```python
import functools

import jax
import jax.numpy as jnp
from jax import lax
from jax.experimental import pallas as pl
from jax.experimental.pallas import tpu as pltpu
from jax.sharding import PartitionSpec as P

COARSE_ITERS = 8
SMOOTH_LOW = 0.25
SMOOTH_HIGH = 2.0
COARSE_LOW = 0.02
LIQUID = 10.0
GAS = 1.0

INTERPRET = False
VMEM_LIMIT = 28 * 1024 * 1024

BX, BY, BZ = 32, 16, 128
WX = 8
X0, Y0, Z0 = BX + 2 * WX, 32, 256
X1, Y1G, Z1 = 48, 8, 128
X2 = 24
F32 = jnp.float32
BF16 = jnp.bfloat16
DOWN, UP = 3, 3
UC, B0, U0, B1 = 4, 4, 2, 16


def chebyshev(low, degree):
    theta = 0.5 * (SMOOTH_HIGH + low)
    delta = 0.5 * (SMOOTH_HIGH - low)
    sigma = theta / delta
    rho_old = 1.0 / sigma
    steps = []
    for _ in range(1, degree):
        rho_new = 1.0 / (2.0 * sigma - rho_old)
        steps.append((rho_new * rho_old, 2.0 * rho_new / delta))
        rho_old = rho_new
    return 1.0 / theta, steps


FIRST, ((KEEP, GAIN),) = chebyshev(SMOOTH_LOW, 2)
COARSE_FIRST, COARSE_STEPS = chebyshev(COARSE_LOW, COARSE_ITERS)


def roll(values, shift, axis):
    return pltpu.roll(values, shift % values.shape[axis], axis)


def iota(shape, dim):
    return lax.broadcasted_iota(jnp.int32, shape, dim)


def split(values, terms):
    parts = []
    for n in range(terms):
        part = values.astype(BF16)
        parts.append(part)
        if n + 1 < terms:
            values = values - part.astype(F32)
    return parts


def times(values, matrix, terms):
    return sum(jnp.dot(p, matrix, preferred_element_type=F32) for p in split(values, terms))


def times_left(matrix, values, terms):
    return sum(jnp.dot(matrix, p, preferred_element_type=F32) for p in split(values, terms))


def lane_pairs(fine, weight, odd_only=False):
    z = iota((fine, 128), 0)
    half = z >> 1
    if fine == 128:
        half = jnp.where(z >= 96, half + 64, half)
    hit = half == iota((fine, 128), 1)
    if odd_only:
        hit = hit & ((z & 1) == 1)
    return jnp.where(hit, weight, 0.0).astype(BF16)


def lane_copies(fine):
    z = iota((128, fine), 1)
    half = z >> 1
    if fine == 128:
        half = jnp.where(z >= 96, half + 64, half)
    return jnp.where(half == iota((128, fine), 0), 1.0, 0.0).astype(BF16)


def row_pairs(rows, odd_x=False, odd_y=False):
    shape = (2 * rows, 8 * rows)
    shift = rows.bit_length() - 1
    c, f = iota(shape, 0), iota(shape, 1)
    cx, cy = c >> (shift - 1), c & (rows // 2 - 1)
    x, y = f >> shift, f & (rows - 1)
    hit = ((x >> 1) == cx) & ((y >> 1) == cy)
    if odd_x:
        hit = hit & ((x & 1) == 1)
    if odd_y:
        hit = hit & ((y & 1) == 1)
    return jnp.where(hit, 1.0, 0.0).astype(BF16)


def row_copies(rows):
    shape = (8 * rows, 2 * rows)
    shift = rows.bit_length() - 1
    f, c = iota(shape, 0), iota(shape, 1)
    hit = ((f >> (shift + 1)) == (c >> (shift - 1))) & (((f & (rows - 1)) >> 1) == (c & (rows // 2 - 1)))
    return jnp.where(hit, 1.0, 0.0).astype(BF16)


def coarsen(block, rows_matrix, lanes_matrix):
    planes, rows, lanes = block.shape
    out = times(times_left(rows_matrix, block.reshape(planes * rows, lanes), DOWN), lanes_matrix, DOWN)
    return out.reshape(4, rows // 2, 128)


def refine(block, rows_matrix, lanes_matrix):
    planes, rows, lanes = block.shape
    out = times_left(rows_matrix, times(block.reshape(planes * rows, lanes), lanes_matrix, UP), UP)
    return out.reshape(8, 2 * rows, lanes_matrix.shape[1])


def apply_at(v, at, planes, faces):
    fx, fy, fz, diag = faces
    here = pl.ds(at, planes)
    c = v[here]
    y, z = fy[here], fz[here]
    out = diag[here] * c - fx[here] * v[pl.ds(at + 1, planes)] - fx[pl.ds(at - 1, planes)] * v[pl.ds(at - 1, planes)]
    out = out - y * roll(c, -1, 1) - roll(y * c, 1, 1)
    return out - z * roll(c, -1, 2) - roll(z * c, 1, 2)


def step_x(values, by):
    if by > 0:
        return jnp.concatenate([values[-1:], values[:-1]], 0)
    return jnp.concatenate([values[1:], values[:1]], 0)


def apply_to(v, faces):
    fx, fy, fz, diag = faces
    out = diag * v - fx * step_x(v, -1) - step_x(fx * v, 1)
    out = out - fy * roll(v, -1, 1) - roll(fy * v, 1, 1)
    return out - fz * roll(v, -1, 2) - roll(fz * v, 1, 2)


def inverse(diag):
    return 1.0 / jnp.where(diag > 0.0, diag, 1.0)


def level_of(fx, fx_before, fy, fz, gx, gy, gz, sizes):
    nx, ny, nz = sizes
    diag = fx + jnp.where(gx == 0, 0.0, fx_before)
    diag = diag + fy + jnp.where(gy == 0, 0.0, roll(fy, 1, 1))
    diag = diag + fz + jnp.where(gz == 0, 0.0, roll(fz, 1, 2))
    fx = jnp.where((gx == nx - 1) | (gx == -1), 0.0, fx)
    fy = jnp.where((gy == ny - 1) | (gy == -1), 0.0, fy)
    fz = jnp.where((gz == nz - 1) | (gz == -1), 0.0, fz)
    return fx, fy, fz, diag, inverse(diag)


def loop(start, stop, block, body, unroll=1):
    count = (stop - start) // block

    def step(i, carry):
        body(start + i * block, block)
        return carry

    if count:
        lax.fori_loop(0, count, step, 0, unroll=unroll)
    rest = stop - start - count * block
    if rest:
        body(stop - rest, rest)


def send_y(r, mask, to_upper, to_lower):
    density = GAS + (LIQUID - GAS) * mask[...].astype(F32)
    for out, rows, line in ((to_upper, slice(8, 16), 7), (to_lower, slice(0, 8), 8)):
        out[0:BX] = r[:, rows, :]
        out[BX : 2 * BX] = density[:, rows]
        for x in range(BX):
            out[2 * BX + x // 8, x % 8 : x % 8 + 1] = density[x, line : line + 1]


def send_x(lower, upper, below, above, to_upper, to_lower):
    for out, r_at, d_at, pack in ((to_upper, BX - 8, BX - 9, 3), (to_lower, 0, 0, 0)):
        for tile, source in enumerate((lower, upper, above, below)):
            rows = slice(8 * tile, 8 * tile + 8)
            out[0:8, rows] = source[r_at : r_at + 8]
            out[8:17, rows] = source[BX + d_at : BX + d_at + 9]
        out[17, 0:8] = below[2 * BX + pack]
        out[17, 8:16] = above[2 * BX + pack]
        out[17, 16:32] = jnp.zeros((16, 128), F32)


def send_z(lower, upper, below, above, x_below, x_above, to_upper, to_lower):
    for out, high in ((to_upper, True), (to_lower, False)):
        def beside(one, two):
            lane = iota(one.shape, one.ndim - 1)
            return jnp.where((lane >= 64) == high, one, roll(two, 64, one.ndim - 1))

        out[0:8] = beside(x_below[0:8], x_below[9:17])
        out[40:48] = beside(x_above[0:8], x_above[8:16])
        out[48] = beside(x_below[8], x_above[16])
        for tile, source in enumerate((lower, upper, above, below)):
            out[8:40, 8 * tile : 8 * tile + 8] = beside(source[0:BX], source[BX : 2 * BX])
        out[49, 0:8] = beside(x_below[17, 0:8], x_below[17, 8:16])
        for n in range(4):
            at = 8 * (n + 1)
            out[49 + at // 32, at % 32 : at % 32 + 8] = beside(below[2 * BX + n], above[2 * BX + n])
        out[50, 8:16] = beside(x_above[17, 0:8], x_above[17, 8:16])
        out[50, 16:32] = jnp.zeros((16, 128), F32)


def presmooth_0(r, faces, inv, d0, d1, start, stop, have_first):
    if not have_first:
        def first(at, n):
            here = pl.ds(at, n)
            d0[here] = (FIRST * r[here]) * inv[here]

        loop(start, stop, B0, first, U0)

    def second(at, n):
        here = pl.ds(at, n)
        left = r[here] - apply_at(d0, at, n, faces)
        r[here] = left
        d1[here] = KEEP * d0[here] + GAIN * (left * inv[here])

    loop(start + 1, stop - 1, B0, second, U0)

    def third(at, n):
        here = pl.ds(at, n)
        r[here] = r[here] - apply_at(d1, at, n, faces)

    loop(start + 2, stop - 2, B0, third, U0)


def restrict_0(r, out):
    rows, lanes = row_pairs(16), lane_pairs(256, 0.125)
    for g in range(4):
        block = r[WX + 8 * g : WX + 8 * g + 8, 0:16, :]
        out[4 * g : 4 * g + 4] = coarsen(block, rows, lanes)


def add_own(total, terms, first):
    value = None if first else total[...]
    for term in terms:
        own = term[WX : WX + BX, 0:BY, 0:BZ]
        value = own if value is None else value + own
    total[...] = value


def face(total):
    return jnp.where(total < 5.0, 1.0, jnp.where(total < 15.0, 2.0 / 11.0, 0.1))


def sides(below, above, at):
    one, two = above[at], below[at]
    axis = one.ndim - 1
    lane = iota(one.shape, axis)
    return jnp.where(lane < 64, one, two), roll(jnp.where(lane >= 64, one, two), 64, axis)


def faces_0(sizes, where, lower, upper, below, above, x_below, x_above, z_below, z_above,
            fx, fy, fz, diag, inv, packed, rho, low, up, raw_x, raw_y, raw_z):
    nx, ny, nz = sizes
    gx0, gy0, gz0 = where[0] * BX, where[1] * BY, where[2] * BZ
    own, side = slice(0, 128), slice(128, 256)
    rho[0:9, :, own] = x_below[8:17]
    rho[41:50, :, own] = x_above[8:17]
    for tile, source in enumerate((lower, upper, above, below)):
        rho[9:41, 8 * tile : 8 * tile + 8, own] = source[BX : 2 * BX]
    low[0:8, own] = x_below[17, 0:8]
    up[0:8, own] = x_below[17, 8:16]
    low[40:48, own] = x_above[17, 0:8]
    up[40:48, own] = x_above[17, 8:16]
    for n in range(4):
        low[8 + 8 * n : 16 + 8 * n, own] = below[2 * BX + n]
        up[8 + 8 * n : 16 + 8 * n, own] = above[2 * BX + n]

    def side_planes(p, n):
        rho[pl.ds(p + 1, n), :, side] = sides(z_below, z_above, pl.ds(p, n))[1]

    loop(0, X0, 4, side_planes)
    rho[0, :, side], rho[49, :, side] = sides(z_below, z_above, 48)
    low[0:32, side], up[0:32, side] = sides(z_below, z_above, 49)
    low_rest, up_rest = sides(z_below, z_above, 50)
    low[32:48, side], up[32:48, side] = low_rest[0:16], up_rest[0:16]

    def plane(p, n):
        shape = (Y0, Z0)
        row, lane = iota(shape, 0), iota(shape, 1)
        gy = gy0 + jnp.where(row < 24, row, row - 32)
        gz = gz0 + jnp.where(lane < 192, lane, lane - 256)
        gx = gx0 + p - WX
        c = rho[p + 1]
        f_x = face(c + jnp.where(gx == nx - 1, GAS, rho[p + 2]))
        l_x = jnp.where(gx == 0, 0.0, face(c + rho[p]))
        over = jnp.where(row == 23, up[pl.ds(p, 1)], roll(c, -1, 0))
        under = jnp.where(row == 24, low[pl.ds(p, 1)], roll(c, 1, 0))
        f_y = face(c + jnp.where(gy == ny - 1, GAS, over))
        l_y = jnp.where(gy == 0, 0.0, face(c + under))
        f_z = face(c + jnp.where(gz == nz - 1, GAS, roll(c, -1, 1)))
        l_z = jnp.where(gz == 0, 0.0, roll(f_z, 1, 1))
        d = f_x + l_x + f_y + l_y + f_z + l_z
        i = 1.0 / d
        diag[p] = d
        inv[p] = i
        raw_x[p] = f_x[0:16]
        raw_y[p] = f_y[0:16]
        raw_z[p] = f_z[0:16]
        fx[p] = jnp.where((gx == nx - 1) | (gx == -1), 0.0, f_x)
        fy[p] = jnp.where((gy == ny - 1) | (gy == -1), 0.0, f_y)
        fz[p] = jnp.where((gz == nz - 1) | (gz == -1), 0.0, f_z)

    loop(0, X0, 1, plane, UC)
    lanes, odd_lanes = lane_pairs(256, 0.125), lane_pairs(256, 0.125, True)
    for n, (raw, rows, columns) in enumerate((
        (raw_x, row_pairs(16, odd_x=True), lanes),
        (raw_y, row_pairs(16, odd_y=True), lanes),
        (raw_z, row_pairs(16), odd_lanes),
    )):
        for g in range(4):
            block = raw[WX + 8 * g : WX + 8 * g + 8]
            packed[16 * n + 4 * g : 16 * n + 4 * g + 4] = coarsen(block, rows, columns)


def begin(lower, upper, below, above, x_below, x_above, z_below, z_above, fx, fy, fz, diag, inv,
          r, total, packed, d0, d1):
    own, side = slice(0, 128), slice(128, 256)
    r[0:8, :, own] = x_below[0:8]
    r[40:48, :, own] = x_above[0:8]
    for tile, source in enumerate((lower, upper, above, below)):
        r[8:40, 8 * tile : 8 * tile + 8, own] = source[0:BX]

    def first(p, n):
        here = pl.ds(p, n)
        r[here, :, side] = sides(z_below, z_above, here)[0]
        d0[here] = (FIRST * r[here]) * inv[here]

    loop(0, X0, B0, first, U0)
    presmooth_0(r, (fx, fy, fz, diag), inv, d0, d1, 0, X0, True)
    add_own(total, (d0, d1), True)
    restrict_0(r, packed)


def assemble_1(part, own, below, above, out):
    out[0:16] = below[part]
    out[16:32] = own[part]
    out[32:48] = above[part]


def relax_1(r, faces, inv, d0, d1, start, stop):
    def second(at, n):
        here = pl.ds(at, n)
        left = r[here] - apply_at(d0, at, n, faces)
        r[here] = left
        d1[here] = KEEP * d0[here] + GAIN * (left * inv[here])

    loop(start, stop, B1, second)


def faces_1(sizes, where, own, below, above,
            fx, fy, fz, diag, inv, gx2, gy2, gz2, diag2, inv2, packed):
    n1 = tuple(n // 2 for n in sizes)
    n2 = tuple(n // 4 for n in sizes)
    ny1 = fx.shape[1]
    ny2 = ny1 // 2
    rows, lanes, odd_lanes = row_pairs(ny1), lane_pairs(128, 0.125), lane_pairs(128, 0.125, True)
    coarse = []
    for n, (raw, rows_matrix, columns) in enumerate((
        (fx, row_pairs(ny1, odd_x=True), lanes),
        (fy, row_pairs(ny1, odd_y=True), lanes),
        (fz, rows, odd_lanes),
    )):
        assemble_1(slice(16 * n, 16 * (n + 1)), own, below, above, raw)
        coarse.append(jnp.concatenate(
            [coarsen(raw[8 * g : 8 * g + 8], rows_matrix, columns) for g in range(6)], 0))
    shape = (B1, ny1, 128)
    gy = lax.rem(where[1] * 8 + iota(shape, 1), n1[1])
    lane = iota(shape, 2)
    gz = where[2] * 64 + jnp.where(lane < 96, lane, lane - 128)

    def planes(n, count):
        at = X1 - B1 - n
        here = pl.ds(at, B1)
        gx = where[0] * 16 + at - 16 + iota(shape, 0)
        c = fx[here]
        before = jnp.concatenate([fx[pl.ds(jnp.maximum(at - 1, 0), 1)], c[:-1]], 0)
        level = level_of(c, before, fy[here], fz[here], gx, gy, gz, n1)
        fx[here], fy[here], fz[here], diag[here], inv[here] = level

    loop(0, X1, B1, planes)
    shape = (X2, ny2, 128)
    lane = iota(shape, 2)
    at_2 = (
        where[0] * 8 - 8 + iota(shape, 0),
        lax.rem(where[1] * 4 + iota(shape, 1), n2[1]),
        where[2] * 32 + jnp.where(lane < 64, lane, lane - 128),
    )
    level_2 = level_of(coarse[0], step_x(coarse[0], 1), coarse[1], coarse[2], *at_2, n2)
    gx2[...], gy2[...], gz2[...], diag2[...], inv2[...] = level_2
    sent = None
    for n, (rows_matrix, columns) in enumerate((
        (row_pairs(ny2, odd_x=True), lanes),
        (row_pairs(ny2, odd_y=True), lanes),
        (row_pairs(ny2), odd_lanes),
    )):
        at = 16 * (n + 1)
        value = roll(coarsen(coarse[n][8:16], rows_matrix, columns), at, 2)
        sent = value if sent is None else jnp.where(iota(value.shape, 2) < at, sent, value)
    packed[...] = sent


def down(own, below, above, fx, fy, fz, diag, inv, gx2, gy2, gz2, diag2, inv2, *refs):
    *given, r, e, r2_out, e2_out, packed, d0, d1 = refs
    ny1 = fx.shape[1]
    ny2 = ny1 // 2
    assemble_1(slice(0, 16), own, below, above, r)
    rows, lanes = row_pairs(ny1), lane_pairs(128, 0.125)

    def begin_1(at, n):
        here = pl.ds(at, n)
        d0[here] = (FIRST * r[here]) * inv[here]

    loop(0, X1, B1, begin_1)
    faces = (fx, fy, fz, diag)
    relax_1(r, faces, inv, d0, d1, 1, X1 - 1)

    def third(at, n):
        here = pl.ds(at, n)
        r[here] = r[here] - apply_at(d1, at, n, faces)
        e[here] = d0[here] + d1[here]

    loop(2, X1 - 2, B1, third)
    e[0:2] = d0[0:2]
    e[X1 - 2 : X1] = d0[X1 - 2 : X1]
    r2 = jnp.concatenate([coarsen(r[8 * g : 8 * g + 8], rows, lanes) for g in range(6)], 0)
    faces_2 = (gx2[...], gy2[...], gz2[...], diag2[...])
    d = (FIRST * r2) * inv2[...]
    r2 = r2 - apply_to(d, faces_2)
    d_next = KEEP * d + GAIN * (r2 * inv2[...])
    r2 = r2 - apply_to(d_next, faces_2)
    r2_out[...] = r2
    e2_out[...] = d + d_next
    sent = coarsen(r2[8:16], row_pairs(ny2), lanes)
    if given:
        sent = jnp.where(iota(sent.shape, 2) < 16, sent, given[0][...])
    packed[...] = sent


def spread(own, below, above, out):
    shape = own.shape
    lane = iota(shape, 2)
    arrays = 2 * (out.shape[1] // shape[0]) if out.shape[1] > shape[0] else 1
    values = []
    for n in range(arrays):
        start = 64 * (n % 2)
        here = lane - start
        value = jnp.where(here < 16, roll(own[...], start - 16 * n, 2), 0.0)
        value = jnp.where((here >= 16) & (here < 32), roll(above[...], start + 16 - 16 * n, 2), value)
        value = jnp.where(here >= 48, roll(below[...], start + 48 - 16 * n, 2), value)
        if n % 2:
            values[-1] = jnp.where(here < 0, values[-1], value)
        else:
            values.append(value)
    for d in range(out.shape[0]):
        for n, value in enumerate(values):
            out[d, shape[0] * n : shape[0] * (n + 1)] = value


def unspread(gathered, n):
    count, _, rows, lanes = gathered.shape
    value = gathered[:, 4 * (n // 2) : 4 * (n // 2) + 4].reshape(4 * count, rows, lanes)
    lane = iota(value.shape, 2)
    near, far = (roll(value, 64, 2), value) if n % 2 else (value, roll(value, 64, 2))
    return jnp.where(lane < 32, near, jnp.where(lane >= 112, far, 0.0))


def up(sizes, last, where, gathered, *refs):
    n3 = tuple(n // 8 for n in sizes)
    first = not last
    refs = list(refs)
    take = lambda n: [refs.pop(0) for _ in range(n)]
    if last:
        level_3 = take(5)
    gx2, gy2, gz2, diag2, inv2, r2_in, e2_in = take(7)
    fx1, fy1, fz1, diag1, inv1, r1_in, e1_in = take(7)
    fx, fy, fz, diag, inv, r_in, total_in = take(7)
    if first:
        level_3 = take(5)
        r, total, packed = take(3)
    else:
        pressure, residual = take(2)
        (r,) = take(1)
    e3, p1, r1, a1, b1, c1, p0, d0, d1 = take(9)

    count = gathered.shape[0]
    ny3 = gathered.shape[2]
    shape = (4 * count, ny3, 128)
    r3 = unspread(gathered, 0)
    if first:
        raw = [unspread(gathered, n) for n in (1, 2, 3)]
        lane = iota(shape, 2)
        at = (
            iota(shape, 0),
            lax.rem(where[1] * 2 + iota(shape, 1), n3[1]),
            where[2] * 16 + jnp.where(lane < 64, lane, lane - 128),
        )
        values = level_of(raw[0], step_x(raw[0], 1), raw[1], raw[2], *at, n3)
        for ref, value in zip(level_3, values):
            ref[...] = value
    faces = tuple(ref[...] for ref in level_3[:4])
    inv3 = level_3[4][...]
    d = (COARSE_FIRST * r3) * inv3
    total3 = d
    for keep, gain in COARSE_STEPS:
        r3 = r3 - apply_to(d, faces)
        d = keep * d + gain * (r3 * inv3)
        total3 = total3 + d
    e3[...] = total3

    copies_rows, copies_lanes = row_copies(2 * ny3), lane_copies(128)
    blocks = []
    for g in range(3):
        start = lax.rem(where[0] * 4 + 4 * (g - 1) + 4 * count, 4 * count)
        blocks.append(refine(e3[pl.ds(start, 4)], copies_rows, copies_lanes))
    p = jnp.concatenate(blocks, 0)
    faces = (gx2[...], gy2[...], gz2[...], diag2[...])
    r2 = r2_in[...] - apply_to(p, faces)
    d = (FIRST * r2) * inv2[...]
    r2 = r2 - apply_to(d, faces)
    d_next = KEEP * d + GAIN * (r2 * inv2[...])
    e2 = e2_in[...] + p + d + d_next

    copies_rows = row_copies(4 * ny3)
    for g in range(4):
        p1[8 + 8 * g : 16 + 8 * g] = refine(e2[4 + 4 * g : 8 + 4 * g], copies_rows, copies_lanes)
    faces = (fx1, fy1, fz1, diag1)

    def lift_1(at, n):
        here = pl.ds(at, n)
        left = r1_in[here] - apply_at(p1, at, n, faces)
        r1[here] = left
        a1[here] = (FIRST * left) * inv1[here]

    loop(11, 37, B1, lift_1)
    relax_1(r1, faces, inv1, a1, b1, 12, 36)

    def sum_1(at, n):
        here = pl.ds(at, n)
        value = e1_in[here] + p1[here] + a1[here] + b1[here]
        c1[here, 0:8] = value[:, 0:8]
        tile = (n, 8, 128)
        c1[here, 8:16] = jnp.where(iota(tile, 1) < 4, value[:, 8:16], value[:, -8:])

    loop(12, 36, B1, sum_1)

    copies_rows, copies_lanes = row_copies(32), lane_copies(256)
    for g in range(6):
        p0[8 * g : 8 * g + 8] = refine(c1[12 + 4 * g : 16 + 4 * g], copies_rows, copies_lanes)
    faces = (fx, fy, fz, diag)
    begin_at, end_at = (6, 42) if last else (2, 46)

    def lift_0(at, n):
        here = pl.ds(at, n)
        left = r_in[here] - apply_at(p0, at, n, faces)
        r[here] = left
        d0[here] = (FIRST * left) * inv[here]

    loop(begin_at, end_at, B0, lift_0, U0)
    presmooth_0(r, faces, inv, d0, d1, begin_at, end_at, True)
    if last:
        pressure[...] = total_in[...]
        add_own(pressure, (p0, d0, d1), False)
        residual[...] = r[WX : WX + BX, 0:BY, 0:BZ]
        return
    total[...] = total_in[...]
    add_own(total, (p0, d0, d1), False)
    presmooth_0(r, faces, inv, d0, d1, 4, 44, False)
    add_own(total, (d0, d1), False)
    restrict_0(r, packed)


def call(kernel, name, args, outs, scratch=(), us=0):
    vmem = pl.BlockSpec(memory_space=pltpu.VMEM)
    smem = pl.BlockSpec(memory_space=pltpu.SMEM)
    return pl.pallas_call(
        kernel,
        out_shape=[jax.ShapeDtypeStruct(s, F32) for s in outs],
        in_specs=[smem if a.ndim == 1 else vmem for a in args],
        out_specs=[vmem] * len(outs),
        scratch_shapes=[pltpu.VMEM(s, F32) for s in scratch],
        compiler_params=pltpu.CompilerParams(vmem_limit_bytes=VMEM_LIMIT),
        name=name,
        cost_estimate=pl.CostEstimate(flops=0, bytes_accessed=us * 3_500_000, transcendentals=0) if us else None,
        interpret=INTERPRET,
    )(*args)


def from_below(array, axis):
    n = lax.axis_size(axis)
    return lax.ppermute(array, axis, [(i, (i + 1) % n) for i in range(n)])


def from_above(array, axis, by=1):
    n = lax.axis_size(axis)
    return lax.ppermute(array, axis, [((i + by) % n, i) for i in range(n)])


def body(right_side, phase_mask):
    nx, ny, nz = (lax.axis_size(a) for a in ("gx", "gy", "gz"))
    sizes = (nx * BX, ny * BY, nz * BZ)
    where = jnp.stack([lax.axis_index(a) for a in ("gx", "gy", "gz")]).astype(jnp.int32)
    own = (BX, BY, BZ)
    upper, lower = call(send_y, "send_y", (right_side, phase_mask), [(2 * BX + 4, 8, 128)] * 2)
    below, above = from_below(upper, "gy"), from_above(lower, "gy")
    to_upper, to_lower = call(send_x, "send_x", (lower, upper, below, above), [(18, Y0, 128)] * 2)
    x_below, x_above = from_below(to_upper, "gx"), from_above(to_lower, "gx")
    pieces = (lower, upper, below, above, x_below, x_above)
    to_upper, to_lower = call(send_z, "send_z", pieces, [(51, Y0, 128)] * 2)
    z_below, z_above = from_below(to_upper, "gz"), from_above(to_lower, "gz")

    full = (X0, Y0, Z0)
    full_1 = (X1, 8 * ny, 128)
    full_2 = (X2, 4 * ny, 128)
    full_3 = (4 * nx, 2 * ny, 128)

    def around(packed):
        parts = [packed] + [from_above(packed, "gy", s) for s in range(1, ny)]
        rows = jnp.concatenate(parts, 1)
        return rows, from_below(rows, "gx"), from_above(rows, "gx")

    *level_0, packed = call(
        functools.partial(faces_0, sizes), "faces_0", (where, *pieces, z_below, z_above),
        [full] * 5 + [(48, 8, 128)],
        [(X0 + 2, Y0, Z0), (X0, Z0), (X0, Z0)] + [(X0, BY, Z0)] * 3, us=5,
    )
    around_faces = around(packed)
    r0, total, packed = call(
        begin, "begin", (*pieces, z_below, z_above, *level_0), [full, own, (16, 8, 128)], [full] * 2, us=6)
    *levels, faces_3 = call(
        functools.partial(faces_1, sizes), "faces_1", (where, *around_faces),
        [full_1] * 5 + [full_2] * 5 + [(4, 2 * ny, 128)], us=3)
    level_3 = []
    for cycle in range(2):
        first = cycle == 0
        r1, e1, r2, e2, packed = call(
            down, "down", (*around(packed), *levels, *([faces_3] if first else [])),
            [full_1] * 2 + [full_2] * 2 + [(4, 2 * ny, 128)], [full_1] * 2, us=4)
        below, above = from_below(packed, "gz"), from_above(packed, "gz")
        (copies,) = call(spread, "spread", (packed, below, above), [(nx, 8 if first else 4, 2 * ny, 128)])
        gathered = lax.all_to_all(copies, "gx", 0, 0)
        args = (where, gathered, *level_3, *levels[5:], r2, e2, *levels[:5], r1, e1, *level_0, r0, total)
        scratch = [full_3] + [full_1] * 4 + [(X1, 16, 128)] + [full] * 3
        if first:
            *level_3, r0, total, packed = call(
                functools.partial(up, sizes, False), "up", args,
                [full_3] * 5 + [full, own, (16, 8, 128)], scratch, us=15)
        else:
            return tuple(call(functools.partial(up, sizes, True), "up_last", args, [own] * 2, [full] + scratch, us=10))


def solution(mesh):
    spec = P("gx", "gy", "gz")
    return jax.shard_map(body, mesh=mesh, in_specs=(spec, spec), out_specs=(spec, spec), check_vma=False)
```

```python
import functools

import jax
import jax.numpy as jnp
from jax import lax
from jax.experimental import pallas as pl
from jax.experimental.pallas import tpu as pltpu
from jax.sharding import PartitionSpec as P

COARSE_ITERS = 8
SMOOTH_LOW = 0.25
SMOOTH_HIGH = 2.0
COARSE_LOW = 0.02
LIQUID = 10.0
GAS = 1.0

INTERPRET = False
VMEM_LIMIT = 28 * 1024 * 1024

BX, BY, BZ = 32, 16, 128
WX = 8
X0, Y0, Z0 = BX + 2 * WX, 32, 256
X1, Y1G, Z1 = 48, 8, 128
X2 = 24
X3 = 26
F32 = jnp.float32
BF16 = jnp.bfloat16
DOWN, UP = 3, 3
UC, B0, U0, B1 = 4, 4, 2, 16


def chebyshev(low, degree):
    theta = 0.5 * (SMOOTH_HIGH + low)
    delta = 0.5 * (SMOOTH_HIGH - low)
    sigma = theta / delta
    rho_old = 1.0 / sigma
    steps = []
    for _ in range(1, degree):
        rho_new = 1.0 / (2.0 * sigma - rho_old)
        steps.append((rho_new * rho_old, 2.0 * rho_new / delta))
        rho_old = rho_new
    return 1.0 / theta, steps


FIRST, ((KEEP, GAIN),) = chebyshev(SMOOTH_LOW, 2)
COARSE_FIRST, COARSE_STEPS = chebyshev(COARSE_LOW, COARSE_ITERS)


def roll(values, shift, axis):
    return pltpu.roll(values, shift % values.shape[axis], axis)


def iota(shape, dim):
    return lax.broadcasted_iota(jnp.int32, shape, dim)


def split(values, terms):
    parts = []
    for n in range(terms):
        part = values.astype(BF16)
        parts.append(part)
        if n + 1 < terms:
            values = values - part.astype(F32)
    return parts


def times(values, matrix, terms):
    return sum(jnp.dot(p, matrix, preferred_element_type=F32) for p in split(values, terms))


def times_left(matrix, values, terms):
    return sum(jnp.dot(matrix, p, preferred_element_type=F32) for p in split(values, terms))


def lane_pairs(fine, weight, odd_only=False):
    z = iota((fine, 128), 0)
    half = z >> 1
    if fine == 128:
        half = jnp.where(z >= 96, half + 64, half)
    hit = half == iota((fine, 128), 1)
    if odd_only:
        hit = hit & ((z & 1) == 1)
    return jnp.where(hit, weight, 0.0).astype(BF16)


def lane_copies(fine):
    z = iota((128, fine), 1)
    half = z >> 1
    if fine == 128:
        half = jnp.where(z >= 96, half + 64, half)
    return jnp.where(half == iota((128, fine), 0), 1.0, 0.0).astype(BF16)


def row_pairs(rows, odd_x=False, odd_y=False):
    shape = (2 * rows, 8 * rows)
    shift = rows.bit_length() - 1
    c, f = iota(shape, 0), iota(shape, 1)
    cx, cy = c >> (shift - 1), c & (rows // 2 - 1)
    x, y = f >> shift, f & (rows - 1)
    hit = ((x >> 1) == cx) & ((y >> 1) == cy)
    if odd_x:
        hit = hit & ((x & 1) == 1)
    if odd_y:
        hit = hit & ((y & 1) == 1)
    return jnp.where(hit, 1.0, 0.0).astype(BF16)


def row_copies(rows):
    shape = (8 * rows, 2 * rows)
    shift = rows.bit_length() - 1
    f, c = iota(shape, 0), iota(shape, 1)
    hit = ((f >> (shift + 1)) == (c >> (shift - 1))) & (((f & (rows - 1)) >> 1) == (c & (rows // 2 - 1)))
    return jnp.where(hit, 1.0, 0.0).astype(BF16)


def coarsen(block, rows_matrix, lanes_matrix):
    planes, rows, lanes = block.shape
    out = times(times_left(rows_matrix, block.reshape(planes * rows, lanes), DOWN), lanes_matrix, DOWN)
    return out.reshape(4, rows // 2, 128)


def coarsen_all(planes, rows_matrix, lanes_matrix):
    return jnp.concatenate(
        [coarsen(planes[at : at + 8], rows_matrix, lanes_matrix) for at in range(0, planes.shape[0], 8)], 0)


def refine(block, rows_matrix, lanes_matrix):
    planes, rows, lanes = block.shape
    out = times_left(rows_matrix, times(block.reshape(planes * rows, lanes), lanes_matrix, UP), UP)
    return out.reshape(8, 2 * rows, lanes_matrix.shape[1])


def apply_at(v, at, planes, faces):
    fx, fy, fz, diag = faces
    here = pl.ds(at, planes)
    c = v[here]
    y, z = fy[here], fz[here]
    out = diag[here] * c - fx[here] * v[pl.ds(at + 1, planes)] - fx[pl.ds(at - 1, planes)] * v[pl.ds(at - 1, planes)]
    out = out - y * roll(c, -1, 1) - roll(y * c, 1, 1)
    return out - z * roll(c, -1, 2) - roll(z * c, 1, 2)


def step_x(values, by):
    if by > 0:
        return jnp.concatenate([values[-1:], values[:-1]], 0)
    return jnp.concatenate([values[1:], values[:1]], 0)


def apply_to(v, faces):
    fx, fy, fz, diag = faces
    out = diag * v - fx * step_x(v, -1) - step_x(fx * v, 1)
    out = out - fy * roll(v, -1, 1) - roll(fy * v, 1, 1)
    return out - fz * roll(v, -1, 2) - roll(fz * v, 1, 2)


def inverse(diag):
    return 1.0 / jnp.where(diag > 0.0, diag, 1.0)


def level_of(fx, fx_before, fy, fz, gx, gy, gz, sizes):
    nx, ny, nz = sizes
    diag = fx + jnp.where((gx == 0) | (gx == nx), 0.0, fx_before)
    diag = diag + fy + jnp.where(gy == 0, 0.0, roll(fy, 1, 1))
    diag = diag + fz + jnp.where(gz == 0, 0.0, roll(fz, 1, 2))
    fx = jnp.where((gx == nx - 1) | (gx == -1), 0.0, fx)
    fy = jnp.where((gy == ny - 1) | (gy == -1), 0.0, fy)
    fz = jnp.where((gz == nz - 1) | (gz == -1), 0.0, fz)
    return fx, fy, fz, diag, inverse(diag)


def loop(start, stop, block, body, unroll=1):
    count = (stop - start) // block

    def step(i, carry):
        body(start + i * block, block)
        return carry

    if count:
        lax.fori_loop(0, count, step, 0, unroll=unroll)
    rest = stop - start - count * block
    if rest:
        body(stop - rest, rest)


def send_y_density(mask, to_upper, to_lower):
    density = GAS + (LIQUID - GAS) * mask[...].astype(F32)
    for out, rows, line in ((to_upper, slice(8, 16), 7), (to_lower, slice(0, 8), 8)):
        out[0:BX] = density[:, rows]
        for x in range(BX):
            out[BX + x // 8, x % 8 : x % 8 + 1] = density[x, line : line + 1]


def send_y(r, to_upper, to_lower):
    to_upper[...] = r[:, 8:16]
    to_lower[...] = r[:, 0:8]


def send_x_density(lower, upper, below, above, to_upper, to_lower):
    for out, at, pack in ((to_upper, BX - 9, 3), (to_lower, 0, 0)):
        for tile, source in enumerate((lower, upper, above, below)):
            out[0:9, 8 * tile : 8 * tile + 8] = source[at : at + 9]
        out[9, 0:8] = below[BX + pack]
        out[9, 8:16] = above[BX + pack]
        out[9, 16:32] = jnp.zeros((16, 128), F32)


def send_x(lower, upper, below, above, to_upper, to_lower):
    for out, at in ((to_upper, BX - 8), (to_lower, 0)):
        for tile, source in enumerate((lower, upper, above, below)):
            out[:, 8 * tile : 8 * tile + 8] = source[at : at + 8]


def beside(one, two, high):
    axis = one.ndim - 1
    return jnp.where((iota(one.shape, axis) >= 64) == high, one, roll(two, 64, axis))


def sides(below, above, at):
    one, two = above[at], below[at]
    axis = one.ndim - 1
    lane = iota(one.shape, axis)
    return jnp.where(lane < 64, one, two), roll(jnp.where(lane >= 64, one, two), 64, axis)


def send_z_density(lower, upper, below, above, x_below, x_above, own, low, up, to_upper, to_lower):
    own[0:9] = x_below[0:9]
    own[41:50] = x_above[0:9]
    for tile, source in enumerate((lower, upper, above, below)):
        own[9:41, 8 * tile : 8 * tile + 8] = source[0:BX]
    low[0:8] = x_below[9, 0:8]
    up[0:8] = x_below[9, 8:16]
    low[40:48] = x_above[9, 0:8]
    up[40:48] = x_above[9, 8:16]
    for n in range(4):
        low[8 + 8 * n : 16 + 8 * n] = below[BX + n]
        up[8 + 8 * n : 16 + 8 * n] = above[BX + n]
    for out, high in ((to_upper, True), (to_lower, False)):
        out[0:25] = beside(own[0:25], own[25:50], high)
        out[25] = beside(low[0:32], up[0:32], high)
        out[26, 0:16] = beside(low[32:48], up[32:48], high)
        out[26, 16:32] = jnp.zeros((16, 128), F32)


def send_z(lower, upper, below, above, x_below, x_above, own, to_upper, to_lower):
    own[0:8] = x_below[...]
    own[40:48] = x_above[...]
    for tile, source in enumerate((lower, upper, above, below)):
        own[8:40, 8 * tile : 8 * tile + 8] = source[...]
    for out, high in ((to_upper, True), (to_lower, False)):
        out[...] = beside(own[0:24], own[24:48], high)


def smooth_0(r, faces, inv, d0, d1, start, stop, between, again=False):
    def second(at, n):
        here = pl.ds(at, n)
        left = r[here] - apply_at(d0, at, n, faces)
        r[here] = left
        d1[here] = KEEP * d0[here] + GAIN * (left * inv[here])

    loop(start + 1, stop - 1, B0, second, U0)
    between()

    def third(at, n):
        here = pl.ds(at, n)
        left = r[here] - apply_at(d1, at, n, faces)
        r[here] = left
        if again:
            d0[here] = (FIRST * left) * inv[here]

    loop(start + 2, stop - 2, B0, third, U0)


def restrict_0(r, out):
    rows, lanes = row_pairs(16), lane_pairs(256, 0.125)
    for g in range(4):
        block = r[WX + 8 * g : WX + 8 * g + 8, 0:16, :]
        out[4 * g : 4 * g + 4] = coarsen(block, rows, lanes)


def add_own(total, terms, first):
    value = None if first else total[...]
    for term in terms:
        own = term[WX : WX + BX, 0:BY, 0:BZ]
        value = own if value is None else value + own
    total[...] = value


def face(total):
    return jnp.where(total < 5.0, 1.0, jnp.where(total < 15.0, 2.0 / 11.0, 0.1))


def own_faces_0(sizes, where, rho_own, low_own, up_own, z_below, z_above, packed, rho, low, up, raw_x, raw_y, raw_z):
    nx, ny, nz = sizes
    own, side = slice(0, 128), slice(128, 256)
    rho[:, :, own] = rho_own[...]
    low[:, own] = low_own[...]
    up[:, own] = up_own[...]
    low[0:32, side], up[0:32, side] = sides(z_below, z_above, 25)
    low_rest, up_rest = sides(z_below, z_above, 26)
    low[32:48, side], up[32:48, side] = low_rest[0:16], up_rest[0:16]

    def side_planes(p, n):
        rho[pl.ds(p, n), :, side], rho[pl.ds(p + 25, n), :, side] = sides(z_below, z_above, pl.ds(p, n))

    loop(0, 25, 5, side_planes)
    shape = (BY, Z0)
    gy = where[1] * BY + iota(shape, 0)
    lane = iota(shape, 1)
    gz = where[2] * BZ + jnp.where(lane < 192, lane, lane - 256)

    def plane(p, n):
        wide = rho[p + 9, 0:24]
        c = wide[0:BY]
        after = jnp.where(where[0] * BX + p == nx - 1, GAS, rho[p + 10, 0:BY])
        raw_x[p] = face(c + after)
        raw_y[p] = face(c + jnp.where(gy == ny - 1, GAS, roll(wide, -1, 0)[0:BY]))
        raw_z[p] = face(c + jnp.where(gz == nz - 1, GAS, roll(c, -1, 1)))

    loop(0, BX, 1, plane, UC)
    lanes, odd_lanes = lane_pairs(256, 0.125), lane_pairs(256, 0.125, True)
    for n, (raw, rows, columns) in enumerate((
        (raw_x, row_pairs(16, odd_x=True), lanes),
        (raw_y, row_pairs(16, odd_y=True), lanes),
        (raw_z, row_pairs(16), odd_lanes),
    )):
        for g in range(4):
            packed[16 * n + 4 * g : 16 * n + 4 * g + 4] = coarsen(raw[8 * g : 8 * g + 8], rows, columns)


def faces_0(sizes, where, rho, low, up, fx, fy, fz, diag, inv):
    nx, ny, nz = sizes
    gx0, gy0, gz0 = where[0] * BX, where[1] * BY, where[2] * BZ

    def plane(p, n):
        shape = (Y0, Z0)
        row, lane = iota(shape, 0), iota(shape, 1)
        gy = gy0 + jnp.where(row < 24, row, row - 32)
        gz = gz0 + jnp.where(lane < 192, lane, lane - 256)
        gx = gx0 + p - WX
        c = rho[p + 1]
        f_x = face(c + jnp.where(gx == nx - 1, GAS, rho[p + 2]))
        l_x = jnp.where(gx == 0, 0.0, face(c + rho[p]))
        over = jnp.where(row == 23, up[pl.ds(p, 1)], roll(c, -1, 0))
        under = jnp.where(row == 24, low[pl.ds(p, 1)], roll(c, 1, 0))
        f_y = face(c + jnp.where(gy == ny - 1, GAS, over))
        l_y = jnp.where(gy == 0, 0.0, face(c + under))
        f_z = face(c + jnp.where(gz == nz - 1, GAS, roll(c, -1, 1)))
        l_z = jnp.where(gz == 0, 0.0, roll(f_z, 1, 1))
        d = f_x + l_x + f_y + l_y + f_z + l_z
        i = 1.0 / d
        diag[p] = d
        inv[p] = i
        fx[p] = jnp.where((gx == nx - 1) | (gx == -1), 0.0, f_x)
        fy[p] = jnp.where((gy == ny - 1) | (gy == -1), 0.0, f_y)
        fz[p] = jnp.where((gz == nz - 1) | (gz == -1), 0.0, f_z)

    loop(0, X0, 1, plane, UC)


def begin(own, z_below, z_above, fx, fy, fz, diag, inv, r, total, packed, d0, d1):
    def whole(p, n):
        one, two = sides(z_below, z_above, pl.ds(p, n))
        for here, side in ((pl.ds(p, n), one), (pl.ds(p + 24, n), two)):
            value = jnp.concatenate([own[here], side], 2)
            r[here] = value
            d0[here] = (FIRST * value) * inv[here]

    loop(0, 24, 4, whole)
    smooth_0(r, (fx, fy, fz, diag), inv, d0, d1, 0, X0, lambda: add_own(total, (d0, d1), True))
    restrict_0(r, packed)


def assemble_1(part, own, below, above, out):
    out[0:16] = below[part]
    out[16:32] = own[part]
    out[32:48] = above[part]


def relax_1(r, faces, inv, d0, d1, start, stop):
    def second(at, n):
        here = pl.ds(at, n)
        left = r[here] - apply_at(d0, at, n, faces)
        r[here] = left
        d1[here] = KEEP * d0[here] + GAIN * (left * inv[here])

    loop(start, stop, B1, second)


def faces_1(sizes, where, own, below, above,
            fx, fy, fz, diag, inv, gx2, gy2, gz2, diag2, inv2, packed):
    n1 = tuple(n // 2 for n in sizes)
    n2 = tuple(n // 4 for n in sizes)
    ny1 = fx.shape[1]
    ny2 = ny1 // 2
    rows, lanes, odd_lanes = row_pairs(ny1), lane_pairs(128, 0.125), lane_pairs(128, 0.125, True)
    coarse = []
    for n, (raw, rows_matrix, columns) in enumerate((
        (fx, row_pairs(ny1, odd_x=True), lanes),
        (fy, row_pairs(ny1, odd_y=True), lanes),
        (fz, rows, odd_lanes),
    )):
        assemble_1(slice(16 * n, 16 * (n + 1)), own, below, above, raw)
        coarse.append(jnp.concatenate(
            [coarsen(raw[8 * g : 8 * g + 8], rows_matrix, columns) for g in range(6)], 0))
    shape = (B1, ny1, 128)
    gy = lax.rem(where[1] * 8 + iota(shape, 1), n1[1])
    lane = iota(shape, 2)
    gz = where[2] * 64 + jnp.where(lane < 96, lane, lane - 128)

    def planes(n, count):
        at = X1 - B1 - n
        here = pl.ds(at, B1)
        gx = where[0] * 16 + at - 16 + iota(shape, 0)
        c = fx[here]
        before = jnp.concatenate([fx[pl.ds(jnp.maximum(at - 1, 0), 1)], c[:-1]], 0)
        level = level_of(c, before, fy[here], fz[here], gx, gy, gz, n1)
        fx[here], fy[here], fz[here], diag[here], inv[here] = level

    loop(0, X1, B1, planes)
    shape = (X2, ny2, 128)
    lane = iota(shape, 2)
    at_2 = (
        where[0] * 8 - 8 + iota(shape, 0),
        lax.rem(where[1] * 4 + iota(shape, 1), n2[1]),
        where[2] * 32 + jnp.where(lane < 64, lane, lane - 128),
    )
    level_2 = level_of(coarse[0], step_x(coarse[0], 1), coarse[1], coarse[2], *at_2, n2)
    gx2[...], gy2[...], gz2[...], diag2[...], inv2[...] = level_2
    sent = None
    for n, (rows_matrix, columns) in enumerate((
        (row_pairs(ny2, odd_x=True), lanes),
        (row_pairs(ny2, odd_y=True), lanes),
        (row_pairs(ny2), odd_lanes),
    )):
        at = 16 * (n + 1)
        value = roll(coarsen_all(coarse[n], rows_matrix, columns)[0:10], at, 2)
        sent = value if sent is None else jnp.where(iota(value.shape, 2) < at, sent, value)
    packed[...] = sent


def down(own, below, above, fx, fy, fz, diag, inv, gx2, gy2, gz2, diag2, inv2, *refs):
    *given, r, e, r2_out, e2_out, packed, d0, d1 = refs
    ny1 = fx.shape[1]
    ny2 = ny1 // 2
    assemble_1(slice(0, 16), own, below, above, r)
    rows, lanes = row_pairs(ny1), lane_pairs(128, 0.125)

    def begin_1(at, n):
        here = pl.ds(at, n)
        d0[here] = (FIRST * r[here]) * inv[here]

    loop(0, X1, B1, begin_1)
    faces = (fx, fy, fz, diag)
    relax_1(r, faces, inv, d0, d1, 1, X1 - 1)

    def third(at, n):
        here = pl.ds(at, n)
        r[here] = r[here] - apply_at(d1, at, n, faces)
        e[here] = d0[here] + d1[here]

    loop(2, X1 - 2, B1, third)
    e[0:2] = d0[0:2]
    e[X1 - 2 : X1] = d0[X1 - 2 : X1]
    r2 = jnp.concatenate([coarsen(r[8 * g : 8 * g + 8], rows, lanes) for g in range(6)], 0)
    faces_2 = (gx2[...], gy2[...], gz2[...], diag2[...])
    d = (FIRST * r2) * inv2[...]
    r2 = r2 - apply_to(d, faces_2)
    d_next = KEEP * d + GAIN * (r2 * inv2[...])
    r2 = r2 - apply_to(d_next, faces_2)
    r2_out[...] = r2
    e2_out[...] = d + d_next
    sent = coarsen_all(r2, row_pairs(ny2), lanes)
    if given:
        packed[...] = jnp.where(iota(packed.shape, 2) < 16, sent[0:10], given[0][...])
    else:
        packed[...] = sent[2:10]


def spread(own, below, above, out):
    shape = own.shape
    lane = iota(shape, 2)
    values = []
    for n in range(4 if out.shape[0] > shape[0] else 1):
        start = 64 * (n % 2)
        here = lane - start
        value = jnp.where(here < 16, roll(own[...], start - 16 * n, 2), 0.0)
        value = jnp.where((here >= 16) & (here < 32), roll(above[...], start + 16 - 16 * n, 2), value)
        value = jnp.where(here >= 48, roll(below[...], start + 48 - 16 * n, 2), value)
        if n % 2:
            values[-1] = jnp.where(here < 0, values[-1], value)
        else:
            values.append(value)
    for n, value in enumerate(values):
        out[shape[0] * n : shape[0] * (n + 1)] = value


def unspread(own, below, above, n):
    if own.shape[0] == 20:
        at = 10 * (n // 2)
        parts = [below[at : at + 10]] + [part[at + 2 : at + 10] for part in (own, above)]
    else:
        parts = [jnp.zeros((2,) + own.shape[1:], F32), below[...], own[...], above[...]]
    value = jnp.concatenate(parts, 0)
    lane = iota(value.shape, 2)
    near, far = (roll(value, 64, 2), value) if n % 2 else (value, roll(value, 64, 2))
    return jnp.where(lane < 32, near, jnp.where(lane >= 112, far, 0.0))


def up(sizes, last, where, own3, below3, above3, *refs):
    n3 = tuple(n // 8 for n in sizes)
    first = not last
    refs = list(refs)
    take = lambda n: [refs.pop(0) for _ in range(n)]
    if last:
        level_3 = take(5)
    gx2, gy2, gz2, diag2, inv2, r2_in, e2_in = take(7)
    fx1, fy1, fz1, diag1, inv1, r1_in, e1_in = take(7)
    fx, fy, fz, diag, inv, r_in, total_in = take(7)
    if first:
        level_3 = take(5)
        r, total, packed = take(3)
    else:
        pressure, residual = take(2)
        (r,) = take(1)
    p1, r1, a1, b1, c1, p0, d0, d1 = take(8)

    ny3 = own3.shape[1]
    shape = (X3, ny3, 128)
    r3 = unspread(own3, below3, above3, 0)
    if first:
        raw = [unspread(own3, below3, above3, n) for n in (1, 2, 3)]
        lane = iota(shape, 2)
        at = (
            where[0] * 4 - 12 + iota(shape, 0),
            lax.rem(where[1] * 2 + iota(shape, 1), n3[1]),
            where[2] * 16 + jnp.where(lane < 64, lane, lane - 128),
        )
        values = level_of(raw[0], step_x(raw[0], 1), raw[1], raw[2], *at, n3)
        for ref, value in zip(level_3, values):
            ref[...] = value
    faces = tuple(ref[...] for ref in level_3[:4])
    inv3 = level_3[4][...]
    d = (COARSE_FIRST * r3) * inv3
    total3 = d
    for keep, gain in COARSE_STEPS:
        r3 = r3 - apply_to(d, faces)
        d = keep * d + gain * (r3 * inv3)
        total3 = total3 + d

    copies_rows, copies_lanes = row_copies(2 * ny3), lane_copies(128)
    blocks = [refine(total3[8 + 4 * g : 12 + 4 * g], copies_rows, copies_lanes) for g in range(3)]
    p = jnp.concatenate(blocks, 0)
    faces = (gx2[...], gy2[...], gz2[...], diag2[...])
    r2 = r2_in[...] - apply_to(p, faces)
    d = (FIRST * r2) * inv2[...]
    r2 = r2 - apply_to(d, faces)
    d_next = KEEP * d + GAIN * (r2 * inv2[...])
    e2 = e2_in[...] + p + d + d_next

    copies_rows = row_copies(4 * ny3)
    for g in range(4):
        p1[8 + 8 * g : 16 + 8 * g] = refine(e2[4 + 4 * g : 8 + 4 * g], copies_rows, copies_lanes)
    faces = (fx1, fy1, fz1, diag1)

    def lift_1(at, n):
        here = pl.ds(at, n)
        left = r1_in[here] - apply_at(p1, at, n, faces)
        r1[here] = left
        a1[here] = (FIRST * left) * inv1[here]

    loop(11, 37, B1, lift_1)
    relax_1(r1, faces, inv1, a1, b1, 12, 36)

    def sum_1(at, n):
        here = pl.ds(at, n)
        value = e1_in[here] + p1[here] + a1[here] + b1[here]
        c1[here, 0:8] = value[:, 0:8]
        tile = (n, 8, 128)
        c1[here, 8:16] = jnp.where(iota(tile, 1) < 4, value[:, 8:16], value[:, -8:])

    loop(12, 36, B1, sum_1)

    copies_rows, copies_lanes = row_copies(32), lane_copies(256)
    for g in range(6):
        p0[8 * g : 8 * g + 8] = refine(c1[12 + 4 * g : 16 + 4 * g], copies_rows, copies_lanes)
    faces = (fx, fy, fz, diag)
    begin_at, end_at = (6, 42) if last else (2, 46)

    def lift_0(at, n):
        here = pl.ds(at, n)
        left = r_in[here] - apply_at(p0, at, n, faces)
        r[here] = left
        d0[here] = (FIRST * left) * inv[here]

    loop(begin_at, end_at, B0, lift_0, U0)
    into = pressure if last else total
    into[...] = total_in[...]
    smooth_0(r, faces, inv, d0, d1, begin_at, end_at, lambda: add_own(into, (p0, d0, d1), False), again=first)
    if last:
        residual[...] = r[WX : WX + BX, 0:BY, 0:BZ]
    else:
        smooth_0(r, faces, inv, d0, d1, 4, 44, lambda: add_own(total, (d0, d1), False))
        restrict_0(r, packed)


def call(kernel, name, args, outs, scratch=(), us=0, after=()):
    body, count = kernel, len(args)
    if after:
        def kernel(*refs):
            body(*refs[:count], *refs[count + len(after) :])

    vmem = pl.BlockSpec(memory_space=pltpu.VMEM)
    smem = pl.BlockSpec(memory_space=pltpu.SMEM)
    return pl.pallas_call(
        kernel,
        out_shape=[jax.ShapeDtypeStruct(s, F32) for s in outs],
        in_specs=[smem if a.ndim == 1 else vmem for a in args] + [pl.BlockSpec(memory_space=pl.ANY)] * len(after),
        out_specs=[vmem] * len(outs),
        scratch_shapes=[pltpu.VMEM(s, F32) for s in scratch],
        compiler_params=pltpu.CompilerParams(vmem_limit_bytes=VMEM_LIMIT),
        name=name,
        cost_estimate=pl.CostEstimate(flops=0, bytes_accessed=us * 3_500_000, transcendentals=0) if us else None,
        interpret=INTERPRET,
    )(*args, *after)


def from_below(array, axis, by=1):
    n = lax.axis_size(axis)
    return lax.ppermute(array, axis, [(i, (i + by) % n) for i in range(n)])


def from_above(array, axis, by=1):
    n = lax.axis_size(axis)
    return lax.ppermute(array, axis, [((i + by) % n, i) for i in range(n)])


def body(right_side, phase_mask):
    nx, ny, nz = (lax.axis_size(a) for a in ("gx", "gy", "gz"))
    sizes = (nx * BX, ny * BY, nz * BZ)
    where = jnp.stack([lax.axis_index(a) for a in ("gx", "gy", "gz")]).astype(jnp.int32)
    own = (BX, BY, BZ)
    half, half_d = (BX, 8, 128), (BX + 4, 8, 128)
    upper_d, lower_d = call(send_y_density, "send_y_density", (phase_mask,), [half_d] * 2)
    below_d, above_d = from_below(upper_d, "gy"), from_above(lower_d, "gy")
    upper, lower = call(send_y, "send_y", (right_side,), [half] * 2)
    below, above = from_below(upper, "gy"), from_above(lower, "gy")

    pieces_d = (lower_d, upper_d, below_d, above_d)
    to_upper, to_lower = call(send_x_density, "send_x_density", pieces_d, [(10, Y0, 128)] * 2)
    pieces_d += (from_below(to_upper, "gx"), from_above(to_lower, "gx"))
    pieces = (lower, upper, below, above)
    to_upper, to_lower = call(send_x, "send_x", pieces, [(8, Y0, 128)] * 2)
    pieces += (from_below(to_upper, "gx"), from_above(to_lower, "gx"))

    rho, low, up_rows, to_upper, to_lower = call(
        send_z_density, "send_z_density", pieces_d, [(50, Y0, 128)] + [(X0, 128)] * 2 + [(27, Y0, 128)] * 2)
    density = (rho, low, up_rows, from_below(to_upper, "gz"), from_above(to_lower, "gz"))
    full = (X0, Y0, Z0)
    full_1 = (X1, 8 * ny, 128)
    full_2 = (X2, 4 * ny, 128)
    full_3 = (X3, 2 * ny, 128)

    def around(packed):
        parts = [packed] + [from_above(packed, "gy", s) for s in range(1, ny)]
        rows = jnp.concatenate(parts, 1)
        return rows, from_below(rows, "gx"), from_above(rows, "gx")

    packed, *density = call(
        functools.partial(own_faces_0, sizes), "own_faces_0", (where, *density),
        [(48, 8, 128), (X0 + 2, Y0, Z0), (X0, Z0), (X0, Z0)], [(BX, BY, Z0)] * 3, us=2)
    r_own, to_upper, to_lower = call(send_z, "send_z", pieces, [(X0, Y0, 128)] + [(24, Y0, 128)] * 2,
        after=(packed,))
    residual = (r_own, from_below(to_upper, "gz"), from_above(to_lower, "gz"))
    around_faces = around(packed)
    level_0 = call(functools.partial(faces_0, sizes), "faces_0", (where, *density), [full] * 5, us=4)
    r0, total, packed = call(
        begin, "begin", (*residual, *level_0), [full, own, (16, 8, 128)], [full] * 2, us=6)
    *levels, faces_3 = call(
        functools.partial(faces_1, sizes), "faces_1", (where, *around_faces),
        [full_1] * 5 + [full_2] * 5 + [(10, 2 * ny, 128)], us=3)
    level_3 = []
    for cycle in range(2):
        first = cycle == 0
        r1, e1, r2, e2, packed = call(
            down, "down", (*around(packed), *levels, *([faces_3] if first else [])),
            [full_1] * 2 + [full_2] * 2 + [(10 if first else 8, 2 * ny, 128)], [full_1] * 2, us=4)
        below, above = from_below(packed, "gz"), from_above(packed, "gz")
        (wide,) = call(spread, "spread", (packed, below, above), [(20 if first else 8, 2 * ny, 128)])
        gathered = (wide, from_below(wide, "gx", 2), from_above(wide, "gx", 2))
        args = (where, *gathered, *level_3, *levels[5:], r2, e2, *levels[:5], r1, e1, *level_0, r0, total)
        scratch = [full_1] * 4 + [(X1, 16, 128)] + [full] * 3
        if first:
            *level_3, r0, total, packed = call(
                functools.partial(up, sizes, False), "up", args,
                [full_3] * 5 + [full, own, (16, 8, 128)], scratch, us=15)
        else:
            return tuple(call(functools.partial(up, sizes, True), "up_last", args, [own] * 2, [full] + scratch, us=10))


def solution(mesh):
    spec = P("gx", "gy", "gz")
    return jax.shard_map(body, mesh=mesh, in_specs=(spec, spec), out_specs=(spec, spec), check_vma=False)
```

```python
import functools

import jax
import jax.numpy as jnp
from jax import lax
from jax.experimental import pallas as pl
from jax.experimental.pallas import tpu as pltpu
from jax.sharding import PartitionSpec as P

COARSE_ITERS = 8
SMOOTH_LOW = 0.25
SMOOTH_HIGH = 2.0
COARSE_LOW = 0.02
LIQUID = 10.0
GAS = 1.0

INTERPRET = False
VMEM_LIMIT = 28 * 1024 * 1024

BX, BY, BZ = 32, 16, 128
WX = 8
X0, Y0, Z0 = BX + 2 * WX, 32, 256
X1, Y1G, Z1 = 48, 8, 128
X2 = 24
X3 = 26
F32 = jnp.float32
BF16 = jnp.bfloat16
DOWN, UP = 3, 3
UC, B0, U0, B1 = 4, 2, 4, 16


def chebyshev(low, degree):
    theta = 0.5 * (SMOOTH_HIGH + low)
    delta = 0.5 * (SMOOTH_HIGH - low)
    sigma = theta / delta
    rho_old = 1.0 / sigma
    steps = []
    for _ in range(1, degree):
        rho_new = 1.0 / (2.0 * sigma - rho_old)
        steps.append((rho_new * rho_old, 2.0 * rho_new / delta))
        rho_old = rho_new
    return 1.0 / theta, steps


FIRST, ((KEEP, GAIN),) = chebyshev(SMOOTH_LOW, 2)
COARSE_FIRST, COARSE_STEPS = chebyshev(COARSE_LOW, COARSE_ITERS)


def roll(values, shift, axis):
    return pltpu.roll(values, shift % values.shape[axis], axis)


def iota(shape, dim):
    return lax.broadcasted_iota(jnp.int32, shape, dim)


def split(values, terms):
    parts = []
    for n in range(terms):
        part = values.astype(BF16)
        parts.append(part)
        if n + 1 < terms:
            values = values - part.astype(F32)
    return parts


def times(values, matrix, terms):
    return sum(jnp.dot(p, matrix, preferred_element_type=F32) for p in split(values, terms))


def times_left(matrix, values, terms):
    return sum(jnp.dot(matrix, p, preferred_element_type=F32) for p in split(values, terms))


def lane_pairs(fine, weight, odd_only=False):
    z = iota((fine, 128), 0)
    half = z >> 1
    if fine == 128:
        half = jnp.where(z >= 96, half + 64, half)
    hit = half == iota((fine, 128), 1)
    if odd_only:
        hit = hit & ((z & 1) == 1)
    return jnp.where(hit, weight, 0.0).astype(BF16)


def lane_copies(fine):
    z = iota((128, fine), 1)
    half = z >> 1
    if fine == 128:
        half = jnp.where(z >= 96, half + 64, half)
    return jnp.where(half == iota((128, fine), 0), 1.0, 0.0).astype(BF16)


def row_pairs(rows, odd_x=False, odd_y=False):
    shape = (2 * rows, 8 * rows)
    shift = rows.bit_length() - 1
    c, f = iota(shape, 0), iota(shape, 1)
    cx, cy = c >> (shift - 1), c & (rows // 2 - 1)
    x, y = f >> shift, f & (rows - 1)
    hit = ((x >> 1) == cx) & ((y >> 1) == cy)
    if odd_x:
        hit = hit & ((x & 1) == 1)
    if odd_y:
        hit = hit & ((y & 1) == 1)
    return jnp.where(hit, 1.0, 0.0).astype(BF16)


def row_copies(rows):
    shape = (8 * rows, 2 * rows)
    shift = rows.bit_length() - 1
    f, c = iota(shape, 0), iota(shape, 1)
    hit = ((f >> (shift + 1)) == (c >> (shift - 1))) & (((f & (rows - 1)) >> 1) == (c & (rows // 2 - 1)))
    return jnp.where(hit, 1.0, 0.0).astype(BF16)


def coarsen(block, rows_matrix, lanes_matrix):
    planes, rows, lanes = block.shape
    out = times(times_left(rows_matrix, block.reshape(planes * rows, lanes), DOWN), lanes_matrix, DOWN)
    return out.reshape(4, rows // 2, 128)


def coarsen_all(planes, rows_matrix, lanes_matrix):
    return jnp.concatenate(
        [coarsen(planes[at : at + 8], rows_matrix, lanes_matrix) for at in range(0, planes.shape[0], 8)], 0)


def refine(block, rows_matrix, lanes_matrix):
    planes, rows, lanes = block.shape
    out = times_left(rows_matrix, times(block.reshape(planes * rows, lanes), lanes_matrix, UP), UP)
    return out.reshape(8, 2 * rows, lanes_matrix.shape[1])


def apply_at(v, at, planes, faces):
    fx, fy, fz, diag = faces
    here = pl.ds(at, planes)
    wide = v[pl.ds(at - 1, planes + 2)]
    x = fx[pl.ds(at - 1, planes + 1)]
    c = wide[1:-1]
    y, z = fy[here], fz[here]
    out = diag[here] * c - x[1:] * wide[2:] - x[:-1] * wide[:-2]
    out = out - y * roll(c, -1, 1) - roll(y * c, 1, 1)
    return out - z * roll(c, -1, 2) - roll(z * c, 1, 2)


def step_x(values, by):
    if by > 0:
        return jnp.concatenate([values[-1:], values[:-1]], 0)
    return jnp.concatenate([values[1:], values[:1]], 0)


def apply_to(v, faces):
    fx, fy, fz, diag = faces
    out = diag * v - fx * step_x(v, -1) - step_x(fx * v, 1)
    out = out - fy * roll(v, -1, 1) - roll(fy * v, 1, 1)
    return out - fz * roll(v, -1, 2) - roll(fz * v, 1, 2)


def inverse(diag):
    return 1.0 / jnp.where(diag > 0.0, diag, 1.0)


def level_of(fx, fx_before, fy, fz, gx, gy, gz, sizes):
    nx, ny, nz = sizes
    diag = fx + jnp.where((gx == 0) | (gx == nx), 0.0, fx_before)
    diag = diag + fy + jnp.where(gy == 0, 0.0, roll(fy, 1, 1))
    diag = diag + fz + jnp.where(gz == 0, 0.0, roll(fz, 1, 2))
    fx = jnp.where((gx == nx - 1) | (gx == -1), 0.0, fx)
    fy = jnp.where((gy == ny - 1) | (gy == -1), 0.0, fy)
    fz = jnp.where((gz == nz - 1) | (gz == -1), 0.0, fz)
    return fx, fy, fz, diag, inverse(diag)


def loop(start, stop, block, body, unroll=1):
    count = (stop - start) // block

    def step(i, carry):
        body(start + i * block, block)
        return carry

    if count:
        lax.fori_loop(0, count, step, 0, unroll=unroll)
    rest = stop - start - count * block
    if rest:
        body(stop - rest, rest)


def beside(one, two, high):
    axis = one.ndim - 1
    return jnp.where((iota(one.shape, axis) >= 64) == high, one, roll(two, 64, axis))


def sides(below, above, at):
    one, two = above[at], below[at]
    axis = one.ndim - 1
    lane = iota(one.shape, axis)
    return jnp.where(lane < 64, one, two), roll(jnp.where(lane >= 64, one, two), 64, axis)


def density_of(mask):
    return GAS + (LIQUID - GAS) * mask[...].astype(F32)


def send_z_own(mask, to_upper, to_lower):
    density = density_of(mask)
    for out, high in ((to_upper, True), (to_lower, False)):
        out[...] = beside(density[0:16], density[16:32], high)


def send_first(mask, below, above, row, plane):
    density = density_of(mask)
    one, two = sides(below, above, slice(0, 16))
    plane[:, 0:128] = density[0]
    plane[:, 128:256] = one[0]
    for x in range(BX):
        row[x : x + 1, 0:128] = density[x, 0:1]
        row[x : x + 1, 128:256] = (one[x, 0:1] if x < 16 else two[x - 16, 0:1])


def send_y(r, mask, to_upper, to_lower):
    density = density_of(mask)
    for out, rows, line in ((to_upper, slice(8, 16), 7), (to_lower, slice(0, 8), 8)):
        out[0:BX] = r[:, rows, :]
        out[BX : 2 * BX] = density[:, rows]
        for x in range(BX):
            out[2 * BX + x // 8, x % 8 : x % 8 + 1] = density[x, line : line + 1]


def send_x(lower, upper, below, above, to_upper, to_lower):
    for out, r_at, d_at, pack in ((to_upper, BX - 8, BX - 9, 3), (to_lower, 0, 0, 0)):
        for tile, source in enumerate((lower, upper, above, below)):
            rows = slice(8 * tile, 8 * tile + 8)
            out[0:8, rows] = source[r_at : r_at + 8]
            out[8:17, rows] = source[BX + d_at : BX + d_at + 9]
        out[17, 0:8] = below[2 * BX + pack]
        out[17, 8:16] = above[2 * BX + pack]
        out[17, 16:32] = jnp.zeros((16, 128), F32)


def send_z(lower, upper, below, above, x_below, x_above, to_upper, to_lower):
    for out, high in ((to_upper, True), (to_lower, False)):
        out[0:8] = beside(x_below[0:8], x_below[9:17], high)
        out[40:48] = beside(x_above[0:8], x_above[8:16], high)
        out[48] = beside(x_below[8], x_above[16], high)
        for tile, source in enumerate((lower, upper, above, below)):
            out[8:40, 8 * tile : 8 * tile + 8] = beside(source[0:BX], source[BX : 2 * BX], high)
        out[49, 0:8] = beside(x_below[17, 0:8], x_below[17, 8:16], high)
        for n in range(4):
            at = 8 * (n + 1)
            out[49 + at // 32, at % 32 : at % 32 + 8] = beside(below[2 * BX + n], above[2 * BX + n], high)
        out[50, 8:16] = beside(x_above[17, 0:8], x_above[17, 8:16], high)
        out[50, 16:32] = jnp.zeros((16, 128), F32)


def smooth_0(r, faces, inv, d0, d1, start, stop, between, again=False):
    def second(at, n):
        here = pl.ds(at, n)
        left = r[here] - apply_at(d0, at, n, faces)
        r[here] = left
        d1[here] = KEEP * d0[here] + GAIN * (left * inv[here])

    loop(start + 1, stop - 1, B0, second, U0)
    between()

    def third(at, n):
        here = pl.ds(at, n)
        left = r[here] - apply_at(d1, at, n, faces)
        r[here] = left
        if again:
            d0[here] = (FIRST * left) * inv[here]

    loop(start + 2, stop - 2, B0, third, U0)


def restrict_0(r, out):
    rows, lanes = row_pairs(16), lane_pairs(256, 0.125)
    for g in range(4):
        block = r[WX + 8 * g : WX + 8 * g + 8, 0:16, :]
        out[4 * g : 4 * g + 4] = coarsen(block, rows, lanes)


def add_own(total, terms, first):
    value = None if first else total[...]
    for term in terms:
        own = term[WX : WX + BX, 0:BY, 0:BZ]
        value = own if value is None else value + own
    total[...] = value


def face(total):
    return jnp.where(total < 5.0, 1.0, jnp.where(total < 15.0, 2.0 / 11.0, 0.1))


def own_faces_0(sizes, where, mask, below, above, row, plane, packed, rho, raw_x, raw_y, raw_z):
    nx, ny, nz = sizes
    own, side = slice(0, 128), slice(128, 256)
    rho[0:BX, :, own] = density_of(mask)
    rho[0:16, :, side], rho[16:32, :, side] = sides(below, above, slice(0, 16))
    rho[BX] = plane[...]
    shape = (BY, Z0)
    y = iota(shape, 0)
    gy = where[1] * BY + y
    lane = iota(shape, 1)
    gz = where[2] * BZ + jnp.where(lane < 192, lane, lane - 256)

    def one_plane(p, n):
        c = rho[p]
        raw_x[p] = face(c + jnp.where(where[0] * BX + p == nx - 1, GAS, rho[p + 1]))
        after = jnp.where(y == BY - 1, row[pl.ds(p, 1)], roll(c, -1, 0))
        raw_y[p] = face(c + jnp.where(gy == ny - 1, GAS, after))
        raw_z[p] = face(c + jnp.where(gz == nz - 1, GAS, roll(c, -1, 1)))

    loop(0, BX, 1, one_plane, UC)
    lanes, odd_lanes = lane_pairs(256, 0.125), lane_pairs(256, 0.125, True)
    for n, (raw, rows, columns) in enumerate((
        (raw_x, row_pairs(16, odd_x=True), lanes),
        (raw_y, row_pairs(16, odd_y=True), lanes),
        (raw_z, row_pairs(16), odd_lanes),
    )):
        for g in range(4):
            packed[16 * n + 4 * g : 16 * n + 4 * g + 4] = coarsen(raw[8 * g : 8 * g + 8], rows, columns)


def faces_0(sizes, where, lower, upper, below, above, x_below, x_above, z_below, z_above,
            fx, fy, fz, diag, inv, rho, low, up):
    nx, ny, nz = sizes
    gx0, gy0, gz0 = where[0] * BX, where[1] * BY, where[2] * BZ
    own, side = slice(0, 128), slice(128, 256)
    rho[0:9, :, own] = x_below[8:17]
    rho[41:50, :, own] = x_above[8:17]
    for tile, source in enumerate((lower, upper, above, below)):
        rho[9:41, 8 * tile : 8 * tile + 8, own] = source[BX : 2 * BX]
    low[0:8, own] = x_below[17, 0:8]
    up[0:8, own] = x_below[17, 8:16]
    low[40:48, own] = x_above[17, 0:8]
    up[40:48, own] = x_above[17, 8:16]
    for n in range(4):
        low[8 + 8 * n : 16 + 8 * n, own] = below[2 * BX + n]
        up[8 + 8 * n : 16 + 8 * n, own] = above[2 * BX + n]

    def side_planes(p, n):
        rho[pl.ds(p + 1, n), :, side] = sides(z_below, z_above, pl.ds(p, n))[1]

    loop(0, X0, 4, side_planes)
    rho[0, :, side], rho[49, :, side] = sides(z_below, z_above, 48)
    low[0:32, side], up[0:32, side] = sides(z_below, z_above, 49)
    low_rest, up_rest = sides(z_below, z_above, 50)
    low[32:48, side], up[32:48, side] = low_rest[0:16], up_rest[0:16]

    def plane(p, n):
        shape = (Y0, Z0)
        row, lane = iota(shape, 0), iota(shape, 1)
        gy = gy0 + jnp.where(row < 24, row, row - 32)
        gz = gz0 + jnp.where(lane < 192, lane, lane - 256)
        gx = gx0 + p - WX
        c = rho[p + 1]
        f_x = face(c + jnp.where(gx == nx - 1, GAS, rho[p + 2]))
        l_x = jnp.where(gx == 0, 0.0, face(c + rho[p]))
        over = jnp.where(row == 23, up[pl.ds(p, 1)], roll(c, -1, 0))
        under = jnp.where(row == 24, low[pl.ds(p, 1)], roll(c, 1, 0))
        f_y = face(c + jnp.where(gy == ny - 1, GAS, over))
        l_y = jnp.where(gy == 0, 0.0, face(c + under))
        f_z = face(c + jnp.where(gz == nz - 1, GAS, roll(c, -1, 1)))
        l_z = jnp.where(gz == 0, 0.0, roll(f_z, 1, 1))
        d = f_x + l_x + f_y + l_y + f_z + l_z
        i = 1.0 / d
        diag[p] = d
        inv[p] = i
        fx[p] = jnp.where((gx == nx - 1) | (gx == -1), 0.0, f_x)
        fy[p] = jnp.where((gy == ny - 1) | (gy == -1), 0.0, f_y)
        fz[p] = jnp.where((gz == nz - 1) | (gz == -1), 0.0, f_z)

    loop(0, X0, 1, plane, UC)


def begin(lower, upper, below, above, x_below, x_above, z_below, z_above, fx, fy, fz, diag, inv,
          r, total, packed, d0, d1):
    own, side = slice(0, 128), slice(128, 256)
    r[0:8, :, own] = x_below[0:8]
    r[40:48, :, own] = x_above[0:8]
    for tile, source in enumerate((lower, upper, above, below)):
        r[8:40, 8 * tile : 8 * tile + 8, own] = source[0:BX]

    def first(p, n):
        here = pl.ds(p, n)
        r[here, :, side] = sides(z_below, z_above, here)[0]
        d0[here] = (FIRST * r[here]) * inv[here]

    loop(0, X0, B0, first, U0)
    smooth_0(r, (fx, fy, fz, diag), inv, d0, d1, 0, X0, lambda: add_own(total, (d0, d1), True))
    restrict_0(r, packed)


def assemble_1(part, own, below, above, out):
    out[0:16] = below[part]
    out[16:32] = own[part]
    out[32:48] = above[part]


def relax_1(r, faces, inv, d0, d1, start, stop):
    def second(at, n):
        here = pl.ds(at, n)
        left = r[here] - apply_at(d0, at, n, faces)
        r[here] = left
        d1[here] = KEEP * d0[here] + GAIN * (left * inv[here])

    loop(start, stop, B1, second)


def faces_1(sizes, where, own, below, above,
            fx, fy, fz, diag, inv, gx2, gy2, gz2, diag2, inv2, packed):
    n1 = tuple(n // 2 for n in sizes)
    n2 = tuple(n // 4 for n in sizes)
    ny1 = fx.shape[1]
    ny2 = ny1 // 2
    rows, lanes, odd_lanes = row_pairs(ny1), lane_pairs(128, 0.125), lane_pairs(128, 0.125, True)
    coarse = []
    for n, (raw, rows_matrix, columns) in enumerate((
        (fx, row_pairs(ny1, odd_x=True), lanes),
        (fy, row_pairs(ny1, odd_y=True), lanes),
        (fz, rows, odd_lanes),
    )):
        assemble_1(slice(16 * n, 16 * (n + 1)), own, below, above, raw)
        coarse.append(jnp.concatenate(
            [coarsen(raw[8 * g : 8 * g + 8], rows_matrix, columns) for g in range(6)], 0))
    shape = (B1, ny1, 128)
    gy = lax.rem(where[1] * 8 + iota(shape, 1), n1[1])
    lane = iota(shape, 2)
    gz = where[2] * 64 + jnp.where(lane < 96, lane, lane - 128)

    def planes(n, count):
        at = X1 - B1 - n
        here = pl.ds(at, B1)
        gx = where[0] * 16 + at - 16 + iota(shape, 0)
        c = fx[here]
        before = jnp.concatenate([fx[pl.ds(jnp.maximum(at - 1, 0), 1)], c[:-1]], 0)
        level = level_of(c, before, fy[here], fz[here], gx, gy, gz, n1)
        fx[here], fy[here], fz[here], diag[here], inv[here] = level

    loop(0, X1, B1, planes)
    shape = (X2, ny2, 128)
    lane = iota(shape, 2)
    at_2 = (
        where[0] * 8 - 8 + iota(shape, 0),
        lax.rem(where[1] * 4 + iota(shape, 1), n2[1]),
        where[2] * 32 + jnp.where(lane < 64, lane, lane - 128),
    )
    level_2 = level_of(coarse[0], step_x(coarse[0], 1), coarse[1], coarse[2], *at_2, n2)
    gx2[...], gy2[...], gz2[...], diag2[...], inv2[...] = level_2
    sent = None
    for n, (rows_matrix, columns) in enumerate((
        (row_pairs(ny2, odd_x=True), lanes),
        (row_pairs(ny2, odd_y=True), lanes),
        (row_pairs(ny2), odd_lanes),
    )):
        at = 16 * (n + 1)
        value = roll(coarsen_all(coarse[n], rows_matrix, columns)[0:10], at, 2)
        sent = value if sent is None else jnp.where(iota(value.shape, 2) < at, sent, value)
    packed[...] = sent


def down(own, below, above, fx, fy, fz, diag, inv, gx2, gy2, gz2, diag2, inv2, *refs):
    *given, r, e, r2_out, e2_out, packed, d0, d1 = refs
    ny1 = fx.shape[1]
    ny2 = ny1 // 2
    assemble_1(slice(0, 16), own, below, above, r)
    rows, lanes = row_pairs(ny1), lane_pairs(128, 0.125)

    def begin_1(at, n):
        here = pl.ds(at, n)
        d0[here] = (FIRST * r[here]) * inv[here]

    loop(0, X1, B1, begin_1)
    faces = (fx, fy, fz, diag)
    relax_1(r, faces, inv, d0, d1, 1, X1 - 1)

    def third(at, n):
        here = pl.ds(at, n)
        r[here] = r[here] - apply_at(d1, at, n, faces)
        e[here] = d0[here] + d1[here]

    loop(2, X1 - 2, B1, third)
    e[0:2] = d0[0:2]
    e[X1 - 2 : X1] = d0[X1 - 2 : X1]
    r2 = jnp.concatenate([coarsen(r[8 * g : 8 * g + 8], rows, lanes) for g in range(6)], 0)
    faces_2 = (gx2[...], gy2[...], gz2[...], diag2[...])
    d = (FIRST * r2) * inv2[...]
    r2 = r2 - apply_to(d, faces_2)
    d_next = KEEP * d + GAIN * (r2 * inv2[...])
    r2 = r2 - apply_to(d_next, faces_2)
    r2_out[...] = r2
    e2_out[...] = d + d_next
    sent = coarsen_all(r2, row_pairs(ny2), lanes)
    if given:
        packed[...] = jnp.where(iota(packed.shape, 2) < 16, sent[0:10], given[0][...])
    else:
        packed[...] = sent[2:10]


def spread(own, below, above, out):
    shape = own.shape
    lane = iota(shape, 2)
    values = []
    for n in range(4 if out.shape[0] > shape[0] else 1):
        start = 64 * (n % 2)
        here = lane - start
        value = jnp.where(here < 16, roll(own[...], start - 16 * n, 2), 0.0)
        value = jnp.where((here >= 16) & (here < 32), roll(above[...], start + 16 - 16 * n, 2), value)
        value = jnp.where(here >= 48, roll(below[...], start + 48 - 16 * n, 2), value)
        if n % 2:
            values[-1] = jnp.where(here < 0, values[-1], value)
        else:
            values.append(value)
    for n, value in enumerate(values):
        out[shape[0] * n : shape[0] * (n + 1)] = value


def unspread(own, below, above, n):
    if own.shape[0] == 20:
        at = 10 * (n // 2)
        parts = [below[at : at + 10]] + [part[at + 2 : at + 10] for part in (own, above)]
    else:
        parts = [jnp.zeros((2,) + own.shape[1:], F32), below[...], own[...], above[...]]
    value = jnp.concatenate(parts, 0)
    lane = iota(value.shape, 2)
    near, far = (roll(value, 64, 2), value) if n % 2 else (value, roll(value, 64, 2))
    return jnp.where(lane < 32, near, jnp.where(lane >= 112, far, 0.0))


def up(sizes, last, where, own3, below3, above3, *refs):
    n3 = tuple(n // 8 for n in sizes)
    first = not last
    refs = list(refs)
    take = lambda n: [refs.pop(0) for _ in range(n)]
    if last:
        level_3 = take(5)
    gx2, gy2, gz2, diag2, inv2, r2_in, e2_in = take(7)
    fx1, fy1, fz1, diag1, inv1, r1_in, e1_in = take(7)
    fx, fy, fz, diag, inv, r_in, total_in = take(7)
    if first:
        level_3 = take(5)
        r, total, packed = take(3)
    else:
        pressure, residual = take(2)
        (r,) = take(1)
    p1, r1, a1, b1, c1, p0, d0, d1 = take(8)

    ny3 = own3.shape[1]
    shape = (X3, ny3, 128)
    r3 = unspread(own3, below3, above3, 0)
    if first:
        raw = [unspread(own3, below3, above3, n) for n in (1, 2, 3)]
        lane = iota(shape, 2)
        at = (
            where[0] * 4 - 12 + iota(shape, 0),
            lax.rem(where[1] * 2 + iota(shape, 1), n3[1]),
            where[2] * 16 + jnp.where(lane < 64, lane, lane - 128),
        )
        values = level_of(raw[0], step_x(raw[0], 1), raw[1], raw[2], *at, n3)
        for ref, value in zip(level_3, values):
            ref[...] = value
    faces = tuple(ref[...] for ref in level_3[:4])
    inv3 = level_3[4][...]
    d = (COARSE_FIRST * r3) * inv3
    total3 = d
    for keep, gain in COARSE_STEPS:
        r3 = r3 - apply_to(d, faces)
        d = keep * d + gain * (r3 * inv3)
        total3 = total3 + d

    copies_rows, copies_lanes = row_copies(2 * ny3), lane_copies(128)
    blocks = [refine(total3[8 + 4 * g : 12 + 4 * g], copies_rows, copies_lanes) for g in range(3)]
    p = jnp.concatenate(blocks, 0)
    faces = (gx2[...], gy2[...], gz2[...], diag2[...])
    r2 = r2_in[...] - apply_to(p, faces)
    d = (FIRST * r2) * inv2[...]
    r2 = r2 - apply_to(d, faces)
    d_next = KEEP * d + GAIN * (r2 * inv2[...])
    e2 = e2_in[...] + p + d + d_next

    copies_rows = row_copies(4 * ny3)
    for g in range(4):
        p1[8 + 8 * g : 16 + 8 * g] = refine(e2[4 + 4 * g : 8 + 4 * g], copies_rows, copies_lanes)
    faces = (fx1, fy1, fz1, diag1)

    def lift_1(at, n):
        here = pl.ds(at, n)
        left = r1_in[here] - apply_at(p1, at, n, faces)
        r1[here] = left
        a1[here] = (FIRST * left) * inv1[here]

    loop(11, 37, B1, lift_1)
    relax_1(r1, faces, inv1, a1, b1, 12, 36)

    def sum_1(at, n):
        here = pl.ds(at, n)
        value = e1_in[here] + p1[here] + a1[here] + b1[here]
        c1[here, 0:8] = value[:, 0:8]
        tile = (n, 8, 128)
        c1[here, 8:16] = jnp.where(iota(tile, 1) < 4, value[:, 8:16], value[:, -8:])

    loop(12, 36, B1, sum_1)

    copies_rows, copies_lanes = row_copies(32), lane_copies(256)
    for g in range(6):
        p0[8 * g : 8 * g + 8] = refine(c1[12 + 4 * g : 16 + 4 * g], copies_rows, copies_lanes)
    faces = (fx, fy, fz, diag)
    begin_at, end_at = (6, 42) if last else (2, 46)

    def lift_0(at, n):
        here = pl.ds(at, n)
        left = r_in[here] - apply_at(p0, at, n, faces)
        r[here] = left
        d0[here] = (FIRST * left) * inv[here]

    loop(begin_at, end_at, B0, lift_0, U0)
    into = pressure if last else total
    into[...] = total_in[...]
    smooth_0(r, faces, inv, d0, d1, begin_at, end_at, lambda: add_own(into, (p0, d0, d1), False), again=first)
    if last:
        residual[...] = r[WX : WX + BX, 0:BY, 0:BZ]
    else:
        smooth_0(r, faces, inv, d0, d1, 4, 44, lambda: add_own(total, (d0, d1), False))
        restrict_0(r, packed)


def call(kernel, name, args, outs, scratch=(), us=0, after=()):
    body, count = kernel, len(args)
    if after:
        def kernel(*refs):
            body(*refs[:count], *refs[count + len(after) :])

    vmem = pl.BlockSpec(memory_space=pltpu.VMEM)
    smem = pl.BlockSpec(memory_space=pltpu.SMEM)
    return pl.pallas_call(
        kernel,
        out_shape=[jax.ShapeDtypeStruct(s, F32) for s in outs],
        in_specs=[smem if a.ndim == 1 else vmem for a in args] + [pl.BlockSpec(memory_space=pl.ANY)] * len(after),
        out_specs=[vmem] * len(outs),
        scratch_shapes=[pltpu.VMEM(s, F32) for s in scratch],
        compiler_params=pltpu.CompilerParams(vmem_limit_bytes=VMEM_LIMIT),
        name=name,
        cost_estimate=pl.CostEstimate(flops=0, bytes_accessed=us * 3_500_000, transcendentals=0) if us else None,
        interpret=INTERPRET,
    )(*args, *after)


def from_below(array, axis, by=1):
    n = lax.axis_size(axis)
    return lax.ppermute(array, axis, [(i, (i + by) % n) for i in range(n)])


def from_above(array, axis, by=1):
    n = lax.axis_size(axis)
    return lax.ppermute(array, axis, [((i + by) % n, i) for i in range(n)])


def body(right_side, phase_mask):
    nx, ny, nz = (lax.axis_size(a) for a in ("gx", "gy", "gz"))
    sizes = (nx * BX, ny * BY, nz * BZ)
    where = jnp.stack([lax.axis_index(a) for a in ("gx", "gy", "gz")]).astype(jnp.int32)
    own = (BX, BY, BZ)
    full = (X0, Y0, Z0)
    full_1 = (X1, 8 * ny, 128)
    full_2 = (X2, 4 * ny, 128)
    full_3 = (X3, 2 * ny, 128)

    def along_y(packed):
        return [packed] + [from_above(packed, "gy", s) for s in range(1, ny)]

    def along_x(parts):
        rows = jnp.concatenate(parts, 1)
        return rows, from_below(rows, "gx"), from_above(rows, "gx")

    to_upper, to_lower = call(send_z_own, "send_z_own", (phase_mask,), [(16, BY, 128)] * 2)
    beside_own = (from_below(to_upper, "gz"), from_above(to_lower, "gz"))
    upper, lower = call(
        send_y, "send_y", (right_side, phase_mask), [(2 * BX + 4, 8, 128)] * 2, after=(to_upper, to_lower))
    below, above = from_below(upper, "gy"), from_above(lower, "gy")
    row, plane = call(send_first, "send_first", (phase_mask, *beside_own), [(BX, Z0), (BY, Z0)])
    row, plane = from_above(row, "gy"), from_above(plane, "gx")
    to_upper, to_lower = call(send_x, "send_x", (lower, upper, below, above), [(18, Y0, 128)] * 2, after=(row, plane))
    x_below, x_above = from_below(to_upper, "gx"), from_above(to_lower, "gx")
    pieces = (lower, upper, below, above, x_below, x_above)
    (packed,) = call(
        functools.partial(own_faces_0, sizes), "own_faces_0", (where, phase_mask, *beside_own, row, plane),
        [(48, 8, 128)], [(BX + 1, BY, Z0)] + [(BX, BY, Z0)] * 3, us=2)
    parts = along_y(packed)
    around_faces = along_x(parts)
    to_upper, to_lower = call(send_z, "send_z", pieces, [(51, Y0, 128)] * 2, after=(packed, parts[1]))
    pieces += (from_below(to_upper, "gz"), from_above(to_lower, "gz"))

    level_0 = call(
        functools.partial(faces_0, sizes), "faces_0", (where, *pieces), [full] * 5,
        [(X0 + 2, Y0, Z0), (X0, Z0), (X0, Z0)], us=4, after=around_faces[:1])
    r0, total, packed = call(
        begin, "begin", (*pieces, *level_0), [full, own, (16, 8, 128)], [full] * 2, us=6)
    *levels, faces_3 = call(
        functools.partial(faces_1, sizes), "faces_1", (where, *around_faces),
        [full_1] * 5 + [full_2] * 5 + [(10, 2 * ny, 128)], us=3)
    level_3 = []
    for cycle in range(2):
        first = cycle == 0
        r1, e1, r2, e2, packed = call(
            down, "down", (*along_x(along_y(packed)), *levels, *([faces_3] if first else [])),
            [full_1] * 2 + [full_2] * 2 + [(10 if first else 8, 2 * ny, 128)], [full_1] * 2, us=4)
        below, above = from_below(packed, "gz"), from_above(packed, "gz")
        (wide,) = call(spread, "spread", (packed, below, above), [(20 if first else 8, 2 * ny, 128)])
        gathered = (wide, from_below(wide, "gx", 2), from_above(wide, "gx", 2))
        args = (where, *gathered, *level_3, *levels[5:], r2, e2, *levels[:5], r1, e1, *level_0, r0, total)
        scratch = [full_1] * 4 + [(X1, 16, 128)] + [full] * 3
        if first:
            *level_3, r0, total, packed = call(
                functools.partial(up, sizes, False), "up", args,
                [full_3] * 5 + [full, own, (16, 8, 128)], scratch, us=15)
        else:
            return tuple(call(functools.partial(up, sizes, True), "up_last", args, [own] * 2, [full] + scratch, us=10))


def solution(mesh):
    spec = P("gx", "gy", "gz")
    return jax.shard_map(body, mesh=mesh, in_specs=(spec, spec), out_specs=(spec, spec), check_vma=False)
```

```python
import functools

import jax
import jax.numpy as jnp
from jax import lax
from jax.experimental import pallas as pl
from jax.experimental.pallas import tpu as pltpu
from jax.sharding import PartitionSpec as P

COARSE_ITERS = 8
SMOOTH_LOW = 0.25
SMOOTH_HIGH = 2.0
COARSE_LOW = 0.02
LIQUID = 10.0
GAS = 1.0

INTERPRET = False
VMEM_LIMIT = 24 * 1024 * 1024

BX, BY, BZ = 32, 16, 128
WX = 8
X0, Y0, Z0 = BX + 2 * WX, 32, 256
X1, Y1G, Z1 = 48, 8, 128
X2 = 24
X3 = 26
F32 = jnp.float32
BF16 = jnp.bfloat16
DOWN, UP = 3, 3
UC, B0, U0, B1 = 4, 2, 4, 16


def chebyshev(low, degree):
    theta = 0.5 * (SMOOTH_HIGH + low)
    delta = 0.5 * (SMOOTH_HIGH - low)
    sigma = theta / delta
    rho_old = 1.0 / sigma
    steps = []
    for _ in range(1, degree):
        rho_new = 1.0 / (2.0 * sigma - rho_old)
        steps.append((rho_new * rho_old, 2.0 * rho_new / delta))
        rho_old = rho_new
    return 1.0 / theta, steps


FIRST, ((KEEP, GAIN),) = chebyshev(SMOOTH_LOW, 2)
COARSE_FIRST, COARSE_STEPS = chebyshev(COARSE_LOW, COARSE_ITERS)


def roll(values, shift, axis):
    return pltpu.roll(values, shift % values.shape[axis], axis)


def iota(shape, dim):
    return lax.broadcasted_iota(jnp.int32, shape, dim)


def split(values, terms):
    parts = []
    for n in range(terms):
        part = values.astype(BF16)
        parts.append(part)
        if n + 1 < terms:
            values = values - part.astype(F32)
    return parts


def times(values, matrix, terms):
    return sum(jnp.dot(p, matrix, preferred_element_type=F32) for p in split(values, terms))


def times_left(matrix, values, terms):
    return sum(jnp.dot(matrix, p, preferred_element_type=F32) for p in split(values, terms))


def lane_pairs(fine, weight, odd_only=False):
    z = iota((fine, 128), 0)
    half = z >> 1
    if fine == 128:
        half = jnp.where(z >= 96, half + 64, half)
    hit = half == iota((fine, 128), 1)
    if odd_only:
        hit = hit & ((z & 1) == 1)
    return jnp.where(hit, weight, 0.0).astype(BF16)


def lane_copies(fine):
    z = iota((128, fine), 1)
    half = z >> 1
    if fine == 128:
        half = jnp.where(z >= 96, half + 64, half)
    return jnp.where(half == iota((128, fine), 0), 1.0, 0.0).astype(BF16)


def row_pairs(rows, odd_x=False, odd_y=False):
    shape = (2 * rows, 8 * rows)
    shift = rows.bit_length() - 1
    c, f = iota(shape, 0), iota(shape, 1)
    cx, cy = c >> (shift - 1), c & (rows // 2 - 1)
    x, y = f >> shift, f & (rows - 1)
    hit = ((x >> 1) == cx) & ((y >> 1) == cy)
    if odd_x:
        hit = hit & ((x & 1) == 1)
    if odd_y:
        hit = hit & ((y & 1) == 1)
    return jnp.where(hit, 1.0, 0.0).astype(BF16)


def row_copies(rows):
    shape = (8 * rows, 2 * rows)
    shift = rows.bit_length() - 1
    f, c = iota(shape, 0), iota(shape, 1)
    hit = ((f >> (shift + 1)) == (c >> (shift - 1))) & (((f & (rows - 1)) >> 1) == (c & (rows // 2 - 1)))
    return jnp.where(hit, 1.0, 0.0).astype(BF16)


def coarsen(block, rows_matrix, lanes_matrix):
    planes, rows, lanes = block.shape
    out = times(times_left(rows_matrix, block.reshape(planes * rows, lanes), DOWN), lanes_matrix, DOWN)
    return out.reshape(4, rows // 2, 128)


def coarsen_all(planes, rows_matrix, lanes_matrix):
    return jnp.concatenate(
        [coarsen(planes[at : at + 8], rows_matrix, lanes_matrix) for at in range(0, planes.shape[0], 8)], 0)


def refine(block, rows_matrix, lanes_matrix):
    planes, rows, lanes = block.shape
    out = times_left(rows_matrix, times(block.reshape(planes * rows, lanes), lanes_matrix, UP), UP)
    return out.reshape(8, 2 * rows, lanes_matrix.shape[1])


def apply_at(v, at, planes, faces):
    fx, fy, fz, diag = faces
    here = pl.ds(at, planes)
    wide = v[pl.ds(at - 1, planes + 2)]
    x = fx[pl.ds(at - 1, planes + 1)]
    c = wide[1:-1]
    y, z = fy[here], fz[here]
    out = diag[here] * c - x[1:] * wide[2:] - x[:-1] * wide[:-2]
    out = out - y * roll(c, -1, 1) - roll(y * c, 1, 1)
    return out - z * roll(c, -1, 2) - roll(z * c, 1, 2)


def step_x(values, by):
    if by > 0:
        return jnp.concatenate([values[-1:], values[:-1]], 0)
    return jnp.concatenate([values[1:], values[:1]], 0)


def apply_to(v, faces):
    fx, fy, fz, diag = faces
    out = diag * v - fx * step_x(v, -1) - step_x(fx * v, 1)
    out = out - fy * roll(v, -1, 1) - roll(fy * v, 1, 1)
    return out - fz * roll(v, -1, 2) - roll(fz * v, 1, 2)


def inverse(diag):
    return 1.0 / jnp.where(diag > 0.0, diag, 1.0)


def level_of(fx, fx_before, fy, fz, gx, gy, gz, sizes):
    nx, ny, nz = sizes
    diag = fx + jnp.where((gx == 0) | (gx == nx), 0.0, fx_before)
    diag = diag + fy + jnp.where(gy == 0, 0.0, roll(fy, 1, 1))
    diag = diag + fz + jnp.where(gz == 0, 0.0, roll(fz, 1, 2))
    fx = jnp.where((gx == nx - 1) | (gx == -1), 0.0, fx)
    fy = jnp.where((gy == ny - 1) | (gy == -1), 0.0, fy)
    fz = jnp.where((gz == nz - 1) | (gz == -1), 0.0, fz)
    return fx, fy, fz, diag, inverse(diag)


def loop(start, stop, block, body, unroll=1):
    count = (stop - start) // block

    def step(i, carry):
        body(start + i * block, block)
        return carry

    if count:
        lax.fori_loop(0, count, step, 0, unroll=unroll)
    rest = stop - start - count * block
    if rest:
        body(stop - rest, rest)


def beside(one, two, high):
    axis = one.ndim - 1
    return jnp.where((iota(one.shape, axis) >= 64) == high, one, roll(two, 64, axis))


def sides(below, above, at):
    one, two = above[at], below[at]
    axis = one.ndim - 1
    lane = iota(one.shape, axis)
    return jnp.where(lane < 64, one, two), roll(jnp.where(lane >= 64, one, two), 64, axis)


def density_of(mask):
    return GAS + (LIQUID - GAS) * mask[...].astype(F32)


def send_z_own(mask, to_upper, to_lower):
    density = density_of(mask)
    for out, high in ((to_upper, True), (to_lower, False)):
        out[...] = beside(density[0:16], density[16:32], high)


def send_y(r, mask, z_below, z_above, to_upper, to_lower, plane):
    density = density_of(mask)
    side = jnp.concatenate(sides(z_below, z_above, slice(0, 16)), 0)
    plane[:, 0:128] = density[0]
    plane[:, 128:256] = side[0]
    for out, rows, line in ((to_upper, slice(8, 16), 7), (to_lower, slice(0, 8), 8)):
        out[0:BX, :, 0:128] = density[:, rows]
        out[0:BX, :, 128:256] = side[:, rows]
        for x in range(BX):
            at = BX + x // 8
            out[at, x % 8 : x % 8 + 1, 0:128] = density[x, line : line + 1]
            out[at, x % 8 : x % 8 + 1, 128:256] = side[x, line : line + 1]
        out[36:52, :, 0:128] = r[0:16, rows]
        out[36:52, :, 128:256] = r[16:32, rows]


def send_x(lower, upper, below, above, to_upper, to_lower):
    for out, at, pack, r_at, lanes in ((to_upper, BX - 9, 3, 44, slice(128, 256)), (to_lower, 0, 0, 36, slice(0, 128))):
        for tile, source in enumerate((lower, upper, above, below)):
            rows = slice(8 * tile, 8 * tile + 8)
            out[0:9, rows] = source[at : at + 9]
            out[10:14, rows, 0:128] = source[r_at : r_at + 4, :, lanes]
            out[10:14, rows, 128:256] = source[r_at + 4 : r_at + 8, :, lanes]
        out[9, 0:8] = below[BX + pack]
        out[9, 8:16] = above[BX + pack]
        out[9, 16:32] = jnp.zeros((16, Z0), F32)


def send_z(lower, upper, below, above, x_below, x_above, own, to_upper, to_lower):
    one, two = slice(0, 128), slice(128, 256)
    own[0:4] = x_below[10:14, :, one]
    own[4:8] = x_below[10:14, :, two]
    own[40:44] = x_above[10:14, :, one]
    own[44:48] = x_above[10:14, :, two]
    for tile, source in enumerate((lower, upper, above, below)):
        rows = slice(8 * tile, 8 * tile + 8)
        own[8:24, rows] = source[36:52, :, one]
        own[24:40, rows] = source[36:52, :, two]
    for out, high in ((to_upper, True), (to_lower, False)):
        out[...] = beside(own[0:24], own[24:48], high)


def smooth_0(r, faces, inv, d0, d1, start, stop, between, again=False):
    def second(at, n):
        here = pl.ds(at, n)
        left = r[here] - apply_at(d0, at, n, faces)
        r[here] = left
        d1[here] = KEEP * d0[here] + GAIN * (left * inv[here])

    loop(start + 1, stop - 1, B0, second, U0)
    between()

    def third(at, n):
        here = pl.ds(at, n)
        left = r[here] - apply_at(d1, at, n, faces)
        r[here] = left
        if again:
            d0[here] = (FIRST * left) * inv[here]

    loop(start + 2, stop - 2, B0, third, U0)


def restrict_0(r, out):
    rows, lanes = row_pairs(16), lane_pairs(256, 0.125)
    for g in range(4):
        block = r[WX + 8 * g : WX + 8 * g + 8, 0:16, :]
        out[4 * g : 4 * g + 4] = coarsen(block, rows, lanes)


def add_own(total, terms, first):
    value = None if first else total[...]
    for term in terms:
        own = term[WX : WX + BX, 0:BY, 0:BZ]
        value = own if value is None else value + own
    total[...] = value


def face(total):
    return jnp.where(total < 5.0, 1.0, jnp.where(total < 15.0, 2.0 / 11.0, 0.1))


def own_faces_0(sizes, where, mask, below, above, rows_above, plane, packed, rho, raw_x, raw_y, raw_z):
    nx, ny, nz = sizes
    own, side = slice(0, 128), slice(128, 256)
    rho[0:BX, :, own] = density_of(mask)
    rho[0:16, :, side], rho[16:32, :, side] = sides(below, above, slice(0, 16))
    rho[BX] = plane[...]
    shape = (BY, Z0)
    y = iota(shape, 0)
    gy = where[1] * BY + y
    lane = iota(shape, 1)
    gz = where[2] * BZ + jnp.where(lane < 192, lane, lane - 256)

    def one_plane(p, n):
        c = rho[p]
        raw_x[p] = face(c + jnp.where(where[0] * BX + p == nx - 1, GAS, rho[p + 1]))
        after = jnp.where(y == BY - 1, rows_above[p, 0:1], roll(c, -1, 0))
        raw_y[p] = face(c + jnp.where(gy == ny - 1, GAS, after))
        raw_z[p] = face(c + jnp.where(gz == nz - 1, GAS, roll(c, -1, 1)))

    loop(0, BX, 1, one_plane, UC)
    lanes, odd_lanes = lane_pairs(256, 0.125), lane_pairs(256, 0.125, True)
    for n, (raw, rows, columns) in enumerate((
        (raw_x, row_pairs(16, odd_x=True), lanes),
        (raw_y, row_pairs(16, odd_y=True), lanes),
        (raw_z, row_pairs(16), odd_lanes),
    )):
        for g in range(4):
            packed[16 * n + 4 * g : 16 * n + 4 * g + 4] = coarsen(raw[8 * g : 8 * g + 8], rows, columns)


def faces_0(sizes, where, lower, upper, below, above, x_below, x_above, fx, fy, fz, diag, inv, rho, low, up):
    nx, ny, nz = sizes
    gx0, gy0, gz0 = where[0] * BX, where[1] * BY, where[2] * BZ
    rho[0:9] = x_below[0:9]
    rho[41:50] = x_above[0:9]
    for tile, source in enumerate((lower, upper, above, below)):
        rho[9:41, 8 * tile : 8 * tile + 8] = source[0:BX]
    low[0:8] = x_below[9, 0:8]
    up[0:8] = x_below[9, 8:16]
    low[40:48] = x_above[9, 0:8]
    up[40:48] = x_above[9, 8:16]
    for n in range(4):
        low[8 + 8 * n : 16 + 8 * n] = below[BX + n]
        up[8 + 8 * n : 16 + 8 * n] = above[BX + n]

    def plane(p, n):
        shape = (Y0, Z0)
        row, lane = iota(shape, 0), iota(shape, 1)
        gy = gy0 + jnp.where(row < 24, row, row - 32)
        gz = gz0 + jnp.where(lane < 192, lane, lane - 256)
        gx = gx0 + p - WX
        c = rho[p + 1]
        f_x = face(c + jnp.where(gx == nx - 1, GAS, rho[p + 2]))
        l_x = jnp.where(gx == 0, 0.0, face(c + rho[p]))
        over = jnp.where(row == 23, up[pl.ds(p, 1)], roll(c, -1, 0))
        under = jnp.where(row == 24, low[pl.ds(p, 1)], roll(c, 1, 0))
        f_y = face(c + jnp.where(gy == ny - 1, GAS, over))
        l_y = jnp.where(gy == 0, 0.0, face(c + under))
        f_z = face(c + jnp.where(gz == nz - 1, GAS, roll(c, -1, 1)))
        l_z = jnp.where(gz == 0, 0.0, roll(f_z, 1, 1))
        d = f_x + l_x + f_y + l_y + f_z + l_z
        i = 1.0 / d
        diag[p] = d
        inv[p] = i
        fx[p] = jnp.where((gx == nx - 1) | (gx == -1), 0.0, f_x)
        fy[p] = jnp.where((gy == ny - 1) | (gy == -1), 0.0, f_y)
        fz[p] = jnp.where((gz == nz - 1) | (gz == -1), 0.0, f_z)

    loop(0, X0, 1, plane, UC)


def begin(own, z_below, z_above, fx, fy, fz, diag, inv, r, total, packed, d0, d1):
    def whole(p, n):
        one, two = sides(z_below, z_above, pl.ds(p, n))
        for here, side in ((pl.ds(p, n), one), (pl.ds(p + 24, n), two)):
            value = jnp.concatenate([own[here], side], 2)
            r[here] = value
            d0[here] = (FIRST * value) * inv[here]

    loop(0, 24, 4, whole)
    smooth_0(r, (fx, fy, fz, diag), inv, d0, d1, 0, X0, lambda: add_own(total, (d0, d1), True))
    restrict_0(r, packed)


def assemble_1(part, own, below, above, out):
    out[0:16] = below[part]
    out[16:32] = own[part]
    out[32:48] = above[part]


def relax_1(r, faces, inv, d0, d1, start, stop):
    def second(at, n):
        here = pl.ds(at, n)
        left = r[here] - apply_at(d0, at, n, faces)
        r[here] = left
        d1[here] = KEEP * d0[here] + GAIN * (left * inv[here])

    loop(start, stop, B1, second)


def faces_1(sizes, where, own, below, above,
            fx, fy, fz, diag, inv, gx2, gy2, gz2, diag2, inv2, packed):
    n1 = tuple(n // 2 for n in sizes)
    n2 = tuple(n // 4 for n in sizes)
    ny1 = fx.shape[1]
    ny2 = ny1 // 2
    rows, lanes, odd_lanes = row_pairs(ny1), lane_pairs(128, 0.125), lane_pairs(128, 0.125, True)
    coarse = []
    for n, (raw, rows_matrix, columns) in enumerate((
        (fx, row_pairs(ny1, odd_x=True), lanes),
        (fy, row_pairs(ny1, odd_y=True), lanes),
        (fz, rows, odd_lanes),
    )):
        assemble_1(slice(16 * n, 16 * (n + 1)), own, below, above, raw)
        coarse.append(jnp.concatenate(
            [coarsen(raw[8 * g : 8 * g + 8], rows_matrix, columns) for g in range(6)], 0))
    shape = (B1, ny1, 128)
    gy = lax.rem(where[1] * 8 + iota(shape, 1), n1[1])
    lane = iota(shape, 2)
    gz = where[2] * 64 + jnp.where(lane < 96, lane, lane - 128)

    def planes(n, count):
        at = X1 - B1 - n
        here = pl.ds(at, B1)
        gx = where[0] * 16 + at - 16 + iota(shape, 0)
        c = fx[here]
        before = jnp.concatenate([fx[pl.ds(jnp.maximum(at - 1, 0), 1)], c[:-1]], 0)
        level = level_of(c, before, fy[here], fz[here], gx, gy, gz, n1)
        fx[here], fy[here], fz[here], diag[here], inv[here] = level

    loop(0, X1, B1, planes)
    shape = (X2, ny2, 128)
    lane = iota(shape, 2)
    at_2 = (
        where[0] * 8 - 8 + iota(shape, 0),
        lax.rem(where[1] * 4 + iota(shape, 1), n2[1]),
        where[2] * 32 + jnp.where(lane < 64, lane, lane - 128),
    )
    level_2 = level_of(coarse[0], step_x(coarse[0], 1), coarse[1], coarse[2], *at_2, n2)
    gx2[...], gy2[...], gz2[...], diag2[...], inv2[...] = level_2
    sent = None
    for n, (rows_matrix, columns) in enumerate((
        (row_pairs(ny2, odd_x=True), lanes),
        (row_pairs(ny2, odd_y=True), lanes),
        (row_pairs(ny2), odd_lanes),
    )):
        at = 16 * (n + 1)
        value = roll(coarsen_all(coarse[n], rows_matrix, columns)[0:10], at, 2)
        sent = value if sent is None else jnp.where(iota(value.shape, 2) < at, sent, value)
    packed[...] = sent


def down(own, below, above, fx, fy, fz, diag, inv, gx2, gy2, gz2, diag2, inv2, *refs):
    *given, r, e, r2_out, e2_out, packed, d0, d1 = refs
    ny1 = fx.shape[1]
    ny2 = ny1 // 2
    assemble_1(slice(0, 16), own, below, above, r)
    rows, lanes = row_pairs(ny1), lane_pairs(128, 0.125)

    def begin_1(at, n):
        here = pl.ds(at, n)
        d0[here] = (FIRST * r[here]) * inv[here]

    loop(0, X1, B1, begin_1)
    faces = (fx, fy, fz, diag)
    relax_1(r, faces, inv, d0, d1, 1, X1 - 1)

    def third(at, n):
        here = pl.ds(at, n)
        r[here] = r[here] - apply_at(d1, at, n, faces)
        e[here] = d0[here] + d1[here]

    loop(2, X1 - 2, B1, third)
    e[0:2] = d0[0:2]
    e[X1 - 2 : X1] = d0[X1 - 2 : X1]
    r2 = jnp.concatenate([coarsen(r[8 * g : 8 * g + 8], rows, lanes) for g in range(6)], 0)
    faces_2 = (gx2[...], gy2[...], gz2[...], diag2[...])
    d = (FIRST * r2) * inv2[...]
    r2 = r2 - apply_to(d, faces_2)
    d_next = KEEP * d + GAIN * (r2 * inv2[...])
    r2 = r2 - apply_to(d_next, faces_2)
    r2_out[...] = r2
    e2_out[...] = d + d_next
    sent = coarsen_all(r2, row_pairs(ny2), lanes)
    if given:
        packed[...] = jnp.where(iota(packed.shape, 2) < 16, sent[0:10], given[0][...])
    else:
        packed[...] = sent[2:10]


def spread(own, below, above, out):
    shape = own.shape
    lane = iota(shape, 2)
    values = []
    for n in range(4 if out.shape[0] > shape[0] else 1):
        start = 64 * (n % 2)
        here = lane - start
        value = jnp.where(here < 16, roll(own[...], start - 16 * n, 2), 0.0)
        value = jnp.where((here >= 16) & (here < 32), roll(above[...], start + 16 - 16 * n, 2), value)
        value = jnp.where(here >= 48, roll(below[...], start + 48 - 16 * n, 2), value)
        if n % 2:
            values[-1] = jnp.where(here < 0, values[-1], value)
        else:
            values.append(value)
    for n, value in enumerate(values):
        out[shape[0] * n : shape[0] * (n + 1)] = value


def unspread(own, below, above, n):
    if own.shape[0] == 20:
        at = 10 * (n // 2)
        parts = [below[at : at + 10]] + [part[at + 2 : at + 10] for part in (own, above)]
    else:
        parts = [jnp.zeros((2,) + own.shape[1:], F32), below[...], own[...], above[...]]
    value = jnp.concatenate(parts, 0)
    lane = iota(value.shape, 2)
    near, far = (roll(value, 64, 2), value) if n % 2 else (value, roll(value, 64, 2))
    return jnp.where(lane < 32, near, jnp.where(lane >= 112, far, 0.0))


def up(sizes, last, where, own3, below3, above3, *refs):
    n3 = tuple(n // 8 for n in sizes)
    first = not last
    refs = list(refs)
    take = lambda n: [refs.pop(0) for _ in range(n)]
    if last:
        level_3 = take(5)
    gx2, gy2, gz2, diag2, inv2, r2_in, e2_in = take(7)
    fx1, fy1, fz1, diag1, inv1, r1_in, e1_in = take(7)
    fx, fy, fz, diag, inv, r_in, total_in = take(7)
    if first:
        level_3 = take(5)
        r, total, packed = take(3)
    else:
        pressure, residual = take(2)
        (r,) = take(1)
    p1, r1, a1, b1, c1, p0, d0, d1 = take(8)

    ny3 = own3.shape[1]
    shape = (X3, ny3, 128)
    r3 = unspread(own3, below3, above3, 0)
    if first:
        raw = [unspread(own3, below3, above3, n) for n in (1, 2, 3)]
        lane = iota(shape, 2)
        at = (
            where[0] * 4 - 12 + iota(shape, 0),
            lax.rem(where[1] * 2 + iota(shape, 1), n3[1]),
            where[2] * 16 + jnp.where(lane < 64, lane, lane - 128),
        )
        values = level_of(raw[0], step_x(raw[0], 1), raw[1], raw[2], *at, n3)
        for ref, value in zip(level_3, values):
            ref[...] = value
    faces = tuple(ref[...] for ref in level_3[:4])
    inv3 = level_3[4][...]
    d = (COARSE_FIRST * r3) * inv3
    total3 = d
    for keep, gain in COARSE_STEPS:
        r3 = r3 - apply_to(d, faces)
        d = keep * d + gain * (r3 * inv3)
        total3 = total3 + d

    copies_rows, copies_lanes = row_copies(2 * ny3), lane_copies(128)
    blocks = [refine(total3[8 + 4 * g : 12 + 4 * g], copies_rows, copies_lanes) for g in range(3)]
    p = jnp.concatenate(blocks, 0)
    faces = (gx2[...], gy2[...], gz2[...], diag2[...])
    r2 = r2_in[...] - apply_to(p, faces)
    d = (FIRST * r2) * inv2[...]
    r2 = r2 - apply_to(d, faces)
    d_next = KEEP * d + GAIN * (r2 * inv2[...])
    e2 = e2_in[...] + p + d + d_next

    copies_rows = row_copies(4 * ny3)
    for g in range(4):
        p1[8 + 8 * g : 16 + 8 * g] = refine(e2[4 + 4 * g : 8 + 4 * g], copies_rows, copies_lanes)
    faces = (fx1, fy1, fz1, diag1)

    def lift_1(at, n):
        here = pl.ds(at, n)
        left = r1_in[here] - apply_at(p1, at, n, faces)
        r1[here] = left
        a1[here] = (FIRST * left) * inv1[here]

    loop(11, 37, B1, lift_1)
    relax_1(r1, faces, inv1, a1, b1, 12, 36)

    def sum_1(at, n):
        here = pl.ds(at, n)
        value = e1_in[here] + p1[here] + a1[here] + b1[here]
        c1[here, 0:8] = value[:, 0:8]
        tile = (n, 8, 128)
        c1[here, 8:16] = jnp.where(iota(tile, 1) < 4, value[:, 8:16], value[:, -8:])

    loop(12, 36, B1, sum_1)

    copies_rows, copies_lanes = row_copies(32), lane_copies(256)
    for g in range(6):
        p0[8 * g : 8 * g + 8] = refine(c1[12 + 4 * g : 16 + 4 * g], copies_rows, copies_lanes)
    faces = (fx, fy, fz, diag)
    begin_at, end_at = (6, 42) if last else (2, 46)

    def lift_0(at, n):
        here = pl.ds(at, n)
        left = r_in[here] - apply_at(p0, at, n, faces)
        r[here] = left
        d0[here] = (FIRST * left) * inv[here]

    loop(begin_at, end_at, B0, lift_0, U0)
    into = pressure if last else total
    into[...] = total_in[...]
    smooth_0(r, faces, inv, d0, d1, begin_at, end_at, lambda: add_own(into, (p0, d0, d1), False), again=first)
    if last:
        residual[...] = r[WX : WX + BX, 0:BY, 0:BZ]
    else:
        smooth_0(r, faces, inv, d0, d1, 4, 44, lambda: add_own(total, (d0, d1), False))
        restrict_0(r, packed)


def call(kernel, name, args, outs, scratch=(), us=0, after=()):
    body, count = kernel, len(args)
    if after:
        def kernel(*refs):
            body(*refs[:count], *refs[count + len(after) :])

    vmem = pl.BlockSpec(memory_space=pltpu.VMEM)
    smem = pl.BlockSpec(memory_space=pltpu.SMEM)
    return pl.pallas_call(
        kernel,
        out_shape=[jax.ShapeDtypeStruct(s, F32) for s in outs],
        in_specs=[smem if a.ndim == 1 else vmem for a in args] + [pl.BlockSpec(memory_space=pl.ANY)] * len(after),
        out_specs=[vmem] * len(outs),
        scratch_shapes=[pltpu.VMEM(s, F32) for s in scratch],
        compiler_params=pltpu.CompilerParams(vmem_limit_bytes=VMEM_LIMIT),
        name=name,
        cost_estimate=pl.CostEstimate(flops=0, bytes_accessed=us * 3_500_000, transcendentals=0) if us else None,
        interpret=INTERPRET,
    )(*args, *after)


def from_below(array, axis, by=1):
    n = lax.axis_size(axis)
    return lax.ppermute(array, axis, [(i, (i + by) % n) for i in range(n)])


def from_above(array, axis, by=1):
    n = lax.axis_size(axis)
    return lax.ppermute(array, axis, [((i + by) % n, i) for i in range(n)])


def body(right_side, phase_mask):
    nx, ny, nz = (lax.axis_size(a) for a in ("gx", "gy", "gz"))
    sizes = (nx * BX, ny * BY, nz * BZ)
    where = jnp.stack([lax.axis_index(a) for a in ("gx", "gy", "gz")]).astype(jnp.int32)
    own = (BX, BY, BZ)
    full = (X0, Y0, Z0)
    full_1 = (X1, 8 * ny, 128)
    full_2 = (X2, 4 * ny, 128)
    full_3 = (X3, 2 * ny, 128)

    def along_y(packed):
        return [packed] + [from_above(packed, "gy", s) for s in range(1, ny)]

    def along_x(parts):
        rows = jnp.concatenate(parts, 1)
        return rows, from_below(rows, "gx"), from_above(rows, "gx")

    to_upper, to_lower = call(send_z_own, "send_z_own", (phase_mask,), [(16, BY, 128)] * 2)
    beside_own = (from_below(to_upper, "gz"), from_above(to_lower, "gz"))
    upper, lower, plane = call(
        send_y, "send_y", (right_side, phase_mask, *beside_own), [(52, 8, Z0)] * 2 + [(BY, Z0)])
    below, above = from_below(upper, "gy"), from_above(lower, "gy")
    plane = from_above(plane, "gx")
    pieces = (lower, upper, below, above)
    to_upper, to_lower = call(send_x, "send_x", pieces, [(14, Y0, Z0)] * 2, after=(plane,))
    pieces += (from_below(to_upper, "gx"), from_above(to_lower, "gx"))
    (packed,) = call(
        functools.partial(own_faces_0, sizes), "own_faces_0", (where, phase_mask, *beside_own, above, plane),
        [(48, 8, 128)], [(BX + 1, BY, Z0)] + [(BX, BY, Z0)] * 3, us=2)
    parts = along_y(packed)
    around_faces = along_x(parts)
    r_own, to_upper, to_lower = call(
        send_z, "send_z", pieces, [(X0, Y0, 128)] + [(24, Y0, 128)] * 2, after=(packed, parts[1]))
    residual = (r_own, from_below(to_upper, "gz"), from_above(to_lower, "gz"))
    level_0 = call(
        functools.partial(faces_0, sizes), "faces_0", (where, *pieces), [full] * 5,
        [(X0 + 2, Y0, Z0), (X0, Z0), (X0, Z0)], us=4)
    r0, total, packed = call(
        begin, "begin", (*residual, *level_0), [full, own, (16, 8, 128)], [full] * 2, us=6)
    *levels, faces_3 = call(
        functools.partial(faces_1, sizes), "faces_1", (where, *around_faces),
        [full_1] * 5 + [full_2] * 5 + [(10, 2 * ny, 128)], us=3)
    level_3 = []
    for cycle in range(2):
        first = cycle == 0
        r1, e1, r2, e2, packed = call(
            down, "down", (*along_x(along_y(packed)), *levels, *([faces_3] if first else [])),
            [full_1] * 2 + [full_2] * 2 + [(10 if first else 8, 2 * ny, 128)], [full_1] * 2, us=4)
        below, above = from_below(packed, "gz"), from_above(packed, "gz")
        (wide,) = call(spread, "spread", (packed, below, above), [(20 if first else 8, 2 * ny, 128)])
        gathered = (wide, from_below(wide, "gx", 2), from_above(wide, "gx", 2))
        args = (where, *gathered, *level_3, *levels[5:], r2, e2, *levels[:5], r1, e1, *level_0, r0, total)
        scratch = [full_1] * 4 + [(X1, 16, 128)] + [full] * 3
        if first:
            *level_3, r0, total, packed = call(
                functools.partial(up, sizes, False), "up", args,
                [full_3] * 5 + [full, own, (16, 8, 128)], scratch, us=15)
        else:
            return tuple(call(functools.partial(up, sizes, True), "up_last", args, [own] * 2, [full] + scratch, us=10))


def solution(mesh):
    spec = P("gx", "gy", "gz")
    return jax.shard_map(body, mesh=mesh, in_specs=(spec, spec), out_specs=(spec, spec), check_vma=False)
```

```python
import functools

import jax
import jax.numpy as jnp
from jax import lax
from jax.experimental import pallas as pl
from jax.experimental.pallas import tpu as pltpu
from jax.sharding import PartitionSpec as P

COARSE_ITERS = 8
SMOOTH_LOW = 0.25
SMOOTH_HIGH = 2.0
COARSE_LOW = 0.02
LIQUID = 10.0
GAS = 1.0

INTERPRET = False
VMEM_LIMIT = 24 * 1024 * 1024

BX, BY, BZ = 32, 16, 128
WX = 8
X0, Y0, Z0 = BX + 2 * WX, 32, 256
X1, Y1G, Z1 = 48, 8, 128
X2 = 24
X3 = 26
F32 = jnp.float32
BF16 = jnp.bfloat16
DOWN, UP = 3, 3
UC, B0, U0, B1 = 4, 2, 4, 16


def chebyshev(low, degree):
    theta = 0.5 * (SMOOTH_HIGH + low)
    delta = 0.5 * (SMOOTH_HIGH - low)
    sigma = theta / delta
    rho_old = 1.0 / sigma
    steps = []
    for _ in range(1, degree):
        rho_new = 1.0 / (2.0 * sigma - rho_old)
        steps.append((rho_new * rho_old, 2.0 * rho_new / delta))
        rho_old = rho_new
    return 1.0 / theta, steps


FIRST, ((KEEP, GAIN),) = chebyshev(SMOOTH_LOW, 2)
COARSE_FIRST, COARSE_STEPS = chebyshev(COARSE_LOW, COARSE_ITERS)


def roll(values, shift, axis):
    return pltpu.roll(values, shift % values.shape[axis], axis)


def iota(shape, dim):
    return lax.broadcasted_iota(jnp.int32, shape, dim)


def split(values, terms):
    parts = []
    for n in range(terms):
        part = values.astype(BF16)
        parts.append(part)
        if n + 1 < terms:
            values = values - part.astype(F32)
    return parts


def times(values, matrix, terms):
    return sum(jnp.dot(p, matrix, preferred_element_type=F32) for p in split(values, terms))


def times_left(matrix, values, terms):
    return sum(jnp.dot(matrix, p, preferred_element_type=F32) for p in split(values, terms))


def lane_pairs(fine, weight, odd_only=False):
    z = iota((fine, 128), 0)
    half = z >> 1
    if fine == 128:
        half = jnp.where(z >= 96, half + 64, half)
    hit = half == iota((fine, 128), 1)
    if odd_only:
        hit = hit & ((z & 1) == 1)
    return jnp.where(hit, weight, 0.0).astype(BF16)


def lane_copies(fine):
    z = iota((128, fine), 1)
    half = z >> 1
    if fine == 128:
        half = jnp.where(z >= 96, half + 64, half)
    return jnp.where(half == iota((128, fine), 0), 1.0, 0.0).astype(BF16)


def row_pairs(rows, odd_x=False, odd_y=False):
    shape = (2 * rows, 8 * rows)
    shift = rows.bit_length() - 1
    c, f = iota(shape, 0), iota(shape, 1)
    cx, cy = c >> (shift - 1), c & (rows // 2 - 1)
    x, y = f >> shift, f & (rows - 1)
    hit = ((x >> 1) == cx) & ((y >> 1) == cy)
    if odd_x:
        hit = hit & ((x & 1) == 1)
    if odd_y:
        hit = hit & ((y & 1) == 1)
    return jnp.where(hit, 1.0, 0.0).astype(BF16)


def row_copies(rows):
    shape = (8 * rows, 2 * rows)
    shift = rows.bit_length() - 1
    f, c = iota(shape, 0), iota(shape, 1)
    hit = ((f >> (shift + 1)) == (c >> (shift - 1))) & (((f & (rows - 1)) >> 1) == (c & (rows // 2 - 1)))
    return jnp.where(hit, 1.0, 0.0).astype(BF16)


def coarsen(block, rows_matrix, lanes_matrix):
    planes, rows, lanes = block.shape
    out = times(times_left(rows_matrix, block.reshape(planes * rows, lanes), DOWN), lanes_matrix, DOWN)
    return out.reshape(4, rows // 2, 128)


def coarsen_all(planes, rows_matrix, lanes_matrix):
    return jnp.concatenate(
        [coarsen(planes[at : at + 8], rows_matrix, lanes_matrix) for at in range(0, planes.shape[0], 8)], 0)


def refine(block, rows_matrix, lanes_matrix):
    planes, rows, lanes = block.shape
    out = times_left(rows_matrix, times(block.reshape(planes * rows, lanes), lanes_matrix, UP), UP)
    return out.reshape(8, 2 * rows, lanes_matrix.shape[1])


def apply_at(v, at, planes, faces):
    fx, fy, fz, diag = faces
    here = pl.ds(at, planes)
    wide = v[pl.ds(at - 1, planes + 2)]
    x = fx[pl.ds(at - 1, planes + 1)]
    c = wide[1:-1]
    y, z = fy[here], fz[here]
    out = diag[here] * c - x[1:] * wide[2:] - x[:-1] * wide[:-2]
    out = out - y * roll(c, -1, 1) - roll(y * c, 1, 1)
    return out - z * roll(c, -1, 2) - roll(z * c, 1, 2)


def step_x(values, by):
    if by > 0:
        return jnp.concatenate([values[-1:], values[:-1]], 0)
    return jnp.concatenate([values[1:], values[:1]], 0)


def apply_to(v, faces):
    fx, fy, fz, diag = faces
    out = diag * v - fx * step_x(v, -1) - step_x(fx * v, 1)
    out = out - fy * roll(v, -1, 1) - roll(fy * v, 1, 1)
    return out - fz * roll(v, -1, 2) - roll(fz * v, 1, 2)


def inverse(diag):
    return 1.0 / jnp.where(diag > 0.0, diag, 1.0)


def level_of(fx, fx_before, fy, fz, gx, gy, gz, sizes):
    nx, ny, nz = sizes
    diag = fx + jnp.where((gx == 0) | (gx == nx), 0.0, fx_before)
    diag = diag + fy + jnp.where(gy == 0, 0.0, roll(fy, 1, 1))
    diag = diag + fz + jnp.where(gz == 0, 0.0, roll(fz, 1, 2))
    fx = jnp.where((gx == nx - 1) | (gx == -1), 0.0, fx)
    fy = jnp.where((gy == ny - 1) | (gy == -1), 0.0, fy)
    fz = jnp.where((gz == nz - 1) | (gz == -1), 0.0, fz)
    return fx, fy, fz, diag, inverse(diag)


def loop(start, stop, block, body, unroll=1):
    count = (stop - start) // block

    def step(i, carry):
        body(start + i * block, block)
        return carry

    if count:
        lax.fori_loop(0, count, step, 0, unroll=unroll)
    rest = stop - start - count * block
    if rest:
        body(stop - rest, rest)


def beside(one, two, high):
    axis = one.ndim - 1
    return jnp.where((iota(one.shape, axis) >= 64) == high, one, roll(two, 64, axis))


def sides(below, above, at):
    one, two = above[at], below[at]
    axis = one.ndim - 1
    lane = iota(one.shape, axis)
    return jnp.where(lane < 64, one, two), roll(jnp.where(lane >= 64, one, two), 64, axis)


def density_of(mask):
    return GAS + (LIQUID - GAS) * mask[...].astype(F32)


def send_z_own(mask, to_upper, to_lower):
    density = density_of(mask)
    for out, high in ((to_upper, True), (to_lower, False)):
        out[...] = beside(density[0:16], density[16:32], high)


def send_y(r, mask, z_below, z_above, to_upper, to_lower, plane):
    density = density_of(mask)
    side = jnp.concatenate(sides(z_below, z_above, slice(0, 16)), 0)
    plane[:, 0:128] = density[0]
    plane[:, 128:256] = side[0]
    for out, rows, line in ((to_upper, slice(8, 16), 7), (to_lower, slice(0, 8), 8)):
        out[0:BX, :, 0:128] = density[:, rows]
        out[0:BX, :, 128:256] = side[:, rows]
        for x in range(BX):
            at = BX + x // 8
            out[at, x % 8 : x % 8 + 1, 0:128] = density[x, line : line + 1]
            out[at, x % 8 : x % 8 + 1, 128:256] = side[x, line : line + 1]
        out[36:52, :, 0:128] = r[0:16, rows]
        out[36:52, :, 128:256] = r[16:32, rows]


def send_x(lower, upper, below, above, to_upper, to_lower):
    for out, at, pack, r_at, lanes in ((to_upper, BX - 9, 3, 44, slice(128, 256)), (to_lower, 0, 0, 36, slice(0, 128))):
        for tile, source in enumerate((lower, upper, above, below)):
            rows = slice(8 * tile, 8 * tile + 8)
            out[0:9, rows] = source[at : at + 9]
            out[10:14, rows, 0:128] = source[r_at : r_at + 4, :, lanes]
            out[10:14, rows, 128:256] = source[r_at + 4 : r_at + 8, :, lanes]
        out[9, 0:8] = below[BX + pack]
        out[9, 8:16] = above[BX + pack]
        out[9, 16:32] = jnp.zeros((16, Z0), F32)


def send_z(lower, upper, below, above, x_below, x_above, own, to_upper, to_lower):
    one, two = slice(0, 128), slice(128, 256)
    own[0:4] = x_below[10:14, :, one]
    own[4:8] = x_below[10:14, :, two]
    own[40:44] = x_above[10:14, :, one]
    own[44:48] = x_above[10:14, :, two]
    for tile, source in enumerate((lower, upper, above, below)):
        rows = slice(8 * tile, 8 * tile + 8)
        own[8:24, rows] = source[36:52, :, one]
        own[24:40, rows] = source[36:52, :, two]
    for out, high in ((to_upper, True), (to_lower, False)):
        out[...] = beside(own[0:24], own[24:48], high)


def last_sweep_0(r, faces, d1, residual):
    fx, fy, fz, diag = faces
    rows, lanes = slice(0, BY), slice(0, BZ)

    def own(at, n):
        here = pl.ds(at, n)
        wide = d1[pl.ds(at - 1, n + 2), rows, lanes]
        x = fx[pl.ds(at - 1, n + 1), rows, lanes]
        out = diag[here, rows, lanes] * wide[1:-1] - x[1:] * wide[2:] - x[:-1] * wide[:-2]
        c, y = d1[here, :, lanes], fy[here, :, lanes]
        out = out - y[:, rows] * roll(c, -1, 1)[:, rows] - roll(y * c, 1, 1)[:, rows]
        c, z = d1[here, rows, :], fz[here, rows, :]
        out = out - z[:, :, lanes] * roll(c, -1, 2)[:, :, lanes] - roll(z * c, 1, 2)[:, :, lanes]
        residual[pl.ds(at - WX, n)] = r[here, rows, lanes] - out

    loop(WX, WX + BX, B0, own, U0)


def smooth_0(r, faces, inv, d0, d1, start, stop, between, again=False, residual=None):
    def second(at, n):
        here = pl.ds(at, n)
        left = r[here] - apply_at(d0, at, n, faces)
        r[here] = left
        d1[here] = KEEP * d0[here] + GAIN * (left * inv[here])

    loop(start + 1, stop - 1, B0, second, U0)
    between()
    if residual is not None:
        last_sweep_0(r, faces, d1, residual)
        return

    def third(at, n):
        here = pl.ds(at, n)
        left = r[here] - apply_at(d1, at, n, faces)
        r[here] = left
        if again:
            d0[here] = (FIRST * left) * inv[here]

    loop(start + 2, stop - 2, B0, third, U0)


def restrict_0(r, out):
    rows, lanes = row_pairs(16), lane_pairs(256, 0.125)
    for g in range(4):
        block = r[WX + 8 * g : WX + 8 * g + 8, 0:16, :]
        out[4 * g : 4 * g + 4] = coarsen(block, rows, lanes)


def add_own(total, terms, first):
    value = None if first else total[...]
    for term in terms:
        own = term[WX : WX + BX, 0:BY, 0:BZ]
        value = own if value is None else value + own
    total[...] = value


def face(total):
    return jnp.where(total < 5.0, 1.0, jnp.where(total < 15.0, 2.0 / 11.0, 0.1))


def own_faces_0(sizes, where, mask, below, above, rows_above, plane, packed, rho, raw_x, raw_y, raw_z):
    nx, ny, nz = sizes
    own, side = slice(0, 128), slice(128, 256)
    rho[0:BX, :, own] = density_of(mask)
    rho[0:16, :, side], rho[16:32, :, side] = sides(below, above, slice(0, 16))
    rho[BX] = plane[...]
    shape = (BY, Z0)
    y = iota(shape, 0)
    gy = where[1] * BY + y
    lane = iota(shape, 1)
    gz = where[2] * BZ + jnp.where(lane < 192, lane, lane - 256)

    def one_plane(p, n):
        c = rho[p]
        raw_x[p] = face(c + jnp.where(where[0] * BX + p == nx - 1, GAS, rho[p + 1]))
        after = jnp.where(y == BY - 1, rows_above[p, 0:1], roll(c, -1, 0))
        raw_y[p] = face(c + jnp.where(gy == ny - 1, GAS, after))
        raw_z[p] = face(c + jnp.where(gz == nz - 1, GAS, roll(c, -1, 1)))

    loop(0, BX, 1, one_plane, UC)
    lanes, odd_lanes = lane_pairs(256, 0.125), lane_pairs(256, 0.125, True)
    for n, (raw, rows, columns) in enumerate((
        (raw_x, row_pairs(16, odd_x=True), lanes),
        (raw_y, row_pairs(16, odd_y=True), lanes),
        (raw_z, row_pairs(16), odd_lanes),
    )):
        for g in range(4):
            packed[16 * n + 4 * g : 16 * n + 4 * g + 4] = coarsen(raw[8 * g : 8 * g + 8], rows, columns)


def faces_0(sizes, where, lower, upper, below, above, x_below, x_above, fx, fy, fz, diag, inv, rho, low, up):
    nx, ny, nz = sizes
    gx0, gy0, gz0 = where[0] * BX, where[1] * BY, where[2] * BZ
    rho[0:9] = x_below[0:9]
    rho[41:50] = x_above[0:9]
    for tile, source in enumerate((lower, upper, above, below)):
        rho[9:41, 8 * tile : 8 * tile + 8] = source[0:BX]
    low[0:8] = x_below[9, 0:8]
    up[0:8] = x_below[9, 8:16]
    low[40:48] = x_above[9, 0:8]
    up[40:48] = x_above[9, 8:16]
    for n in range(4):
        low[8 + 8 * n : 16 + 8 * n] = below[BX + n]
        up[8 + 8 * n : 16 + 8 * n] = above[BX + n]

    def plane(p, n):
        shape = (Y0, Z0)
        row, lane = iota(shape, 0), iota(shape, 1)
        gy = gy0 + jnp.where(row < 24, row, row - 32)
        gz = gz0 + jnp.where(lane < 192, lane, lane - 256)
        gx = gx0 + p - WX
        c = rho[p + 1]
        f_x = face(c + jnp.where(gx == nx - 1, GAS, rho[p + 2]))
        l_x = jnp.where(gx == 0, 0.0, face(c + rho[p]))
        over = jnp.where(row == 23, up[pl.ds(p, 1)], roll(c, -1, 0))
        under = jnp.where(row == 24, low[pl.ds(p, 1)], roll(c, 1, 0))
        f_y = face(c + jnp.where(gy == ny - 1, GAS, over))
        l_y = jnp.where(gy == 0, 0.0, face(c + under))
        f_z = face(c + jnp.where(gz == nz - 1, GAS, roll(c, -1, 1)))
        l_z = jnp.where(gz == 0, 0.0, roll(f_z, 1, 1))
        d = f_x + l_x + f_y + l_y + f_z + l_z
        i = 1.0 / d
        diag[p] = d
        inv[p] = i
        fx[p] = jnp.where((gx == nx - 1) | (gx == -1), 0.0, f_x)
        fy[p] = jnp.where((gy == ny - 1) | (gy == -1), 0.0, f_y)
        fz[p] = jnp.where((gz == nz - 1) | (gz == -1), 0.0, f_z)

    loop(0, X0, 1, plane, UC)


def begin(own, z_below, z_above, fx, fy, fz, diag, inv, r, total, packed, d0, d1):
    def whole(p, n):
        one, two = sides(z_below, z_above, pl.ds(p, n))
        for here, side in ((pl.ds(p, n), one), (pl.ds(p + 24, n), two)):
            value = jnp.concatenate([own[here], side], 2)
            r[here] = value
            d0[here] = (FIRST * value) * inv[here]

    loop(0, 24, 4, whole)
    smooth_0(r, (fx, fy, fz, diag), inv, d0, d1, 0, X0, lambda: add_own(total, (d0, d1), True))
    restrict_0(r, packed)


def assemble_1(part, own, below, above, out):
    out[0:16] = below[part]
    out[16:32] = own[part]
    out[32:48] = above[part]


def relax_1(r, faces, inv, d0, d1, start, stop):
    def second(at, n):
        here = pl.ds(at, n)
        left = r[here] - apply_at(d0, at, n, faces)
        r[here] = left
        d1[here] = KEEP * d0[here] + GAIN * (left * inv[here])

    loop(start, stop, B1, second)


def faces_1(sizes, where, own, below, above,
            fx, fy, fz, diag, inv, gx2, gy2, gz2, diag2, inv2, packed):
    n1 = tuple(n // 2 for n in sizes)
    n2 = tuple(n // 4 for n in sizes)
    ny1 = fx.shape[1]
    ny2 = ny1 // 2
    rows, lanes, odd_lanes = row_pairs(ny1), lane_pairs(128, 0.125), lane_pairs(128, 0.125, True)
    coarse = []
    for n, (raw, rows_matrix, columns) in enumerate((
        (fx, row_pairs(ny1, odd_x=True), lanes),
        (fy, row_pairs(ny1, odd_y=True), lanes),
        (fz, rows, odd_lanes),
    )):
        assemble_1(slice(16 * n, 16 * (n + 1)), own, below, above, raw)
        coarse.append(jnp.concatenate(
            [coarsen(raw[8 * g : 8 * g + 8], rows_matrix, columns) for g in range(6)], 0))
    shape = (B1, ny1, 128)
    gy = lax.rem(where[1] * 8 + iota(shape, 1), n1[1])
    lane = iota(shape, 2)
    gz = where[2] * 64 + jnp.where(lane < 96, lane, lane - 128)

    def planes(n, count):
        at = X1 - B1 - n
        here = pl.ds(at, B1)
        gx = where[0] * 16 + at - 16 + iota(shape, 0)
        c = fx[here]
        before = jnp.concatenate([fx[pl.ds(jnp.maximum(at - 1, 0), 1)], c[:-1]], 0)
        level = level_of(c, before, fy[here], fz[here], gx, gy, gz, n1)
        fx[here], fy[here], fz[here], diag[here], inv[here] = level

    loop(0, X1, B1, planes)
    shape = (X2, ny2, 128)
    lane = iota(shape, 2)
    at_2 = (
        where[0] * 8 - 8 + iota(shape, 0),
        lax.rem(where[1] * 4 + iota(shape, 1), n2[1]),
        where[2] * 32 + jnp.where(lane < 64, lane, lane - 128),
    )
    level_2 = level_of(coarse[0], step_x(coarse[0], 1), coarse[1], coarse[2], *at_2, n2)
    gx2[...], gy2[...], gz2[...], diag2[...], inv2[...] = level_2
    sent = None
    for n, (rows_matrix, columns) in enumerate((
        (row_pairs(ny2, odd_x=True), lanes),
        (row_pairs(ny2, odd_y=True), lanes),
        (row_pairs(ny2), odd_lanes),
    )):
        at = 16 * (n + 1)
        value = roll(coarsen_all(coarse[n], rows_matrix, columns)[0:10], at, 2)
        sent = value if sent is None else jnp.where(iota(value.shape, 2) < at, sent, value)
    packed[...] = sent


def down(own, below, above, fx, fy, fz, diag, inv, gx2, gy2, gz2, diag2, inv2, *refs):
    *given, r, e, r2_out, e2_out, packed, d0, d1 = refs
    ny1 = fx.shape[1]
    ny2 = ny1 // 2
    assemble_1(slice(0, 16), own, below, above, r)
    rows, lanes = row_pairs(ny1), lane_pairs(128, 0.125)

    def begin_1(at, n):
        here = pl.ds(at, n)
        d0[here] = (FIRST * r[here]) * inv[here]

    loop(0, X1, B1, begin_1)
    faces = (fx, fy, fz, diag)
    relax_1(r, faces, inv, d0, d1, 1, X1 - 1)

    def third(at, n):
        here = pl.ds(at, n)
        r[here] = r[here] - apply_at(d1, at, n, faces)
        e[here] = d0[here] + d1[here]

    loop(2, X1 - 2, B1, third)
    e[0:2] = d0[0:2]
    e[X1 - 2 : X1] = d0[X1 - 2 : X1]
    r2 = jnp.concatenate([coarsen(r[8 * g : 8 * g + 8], rows, lanes) for g in range(6)], 0)
    faces_2 = (gx2[...], gy2[...], gz2[...], diag2[...])
    d = (FIRST * r2) * inv2[...]
    r2 = r2 - apply_to(d, faces_2)
    d_next = KEEP * d + GAIN * (r2 * inv2[...])
    r2 = r2 - apply_to(d_next, faces_2)
    r2_out[...] = r2
    e2_out[...] = d + d_next
    sent = coarsen_all(r2, row_pairs(ny2), lanes)
    if given:
        packed[...] = jnp.where(iota(packed.shape, 2) < 16, sent[0:10], given[0][...])
    else:
        packed[...] = sent[2:10]


def spread(own, below, above, out):
    shape = own.shape
    lane = iota(shape, 2)
    values = []
    for n in range(4 if out.shape[0] > shape[0] else 1):
        start = 64 * (n % 2)
        here = lane - start
        value = jnp.where(here < 16, roll(own[...], start - 16 * n, 2), 0.0)
        value = jnp.where((here >= 16) & (here < 32), roll(above[...], start + 16 - 16 * n, 2), value)
        value = jnp.where(here >= 48, roll(below[...], start + 48 - 16 * n, 2), value)
        if n % 2:
            values[-1] = jnp.where(here < 0, values[-1], value)
        else:
            values.append(value)
    for n, value in enumerate(values):
        out[shape[0] * n : shape[0] * (n + 1)] = value


def unspread(own, below, above, n):
    if own.shape[0] == 20:
        at = 10 * (n // 2)
        parts = [below[at : at + 10]] + [part[at + 2 : at + 10] for part in (own, above)]
    else:
        parts = [jnp.zeros((2,) + own.shape[1:], F32), below[...], own[...], above[...]]
    value = jnp.concatenate(parts, 0)
    lane = iota(value.shape, 2)
    near, far = (roll(value, 64, 2), value) if n % 2 else (value, roll(value, 64, 2))
    return jnp.where(lane < 32, near, jnp.where(lane >= 112, far, 0.0))


def up(sizes, last, where, own3, below3, above3, *refs):
    n3 = tuple(n // 8 for n in sizes)
    first = not last
    refs = list(refs)
    take = lambda n: [refs.pop(0) for _ in range(n)]
    if last:
        level_3 = take(5)
    gx2, gy2, gz2, diag2, inv2, r2_in, e2_in = take(7)
    fx1, fy1, fz1, diag1, inv1, r1_in, e1_in = take(7)
    fx, fy, fz, diag, inv, r_in, total_in = take(7)
    if first:
        level_3 = take(5)
        r, total, packed = take(3)
    else:
        pressure, residual = take(2)
        (r,) = take(1)
    p1, r1, a1, b1, c1, p0, d0, d1 = take(8)

    ny3 = own3.shape[1]
    shape = (X3, ny3, 128)
    r3 = unspread(own3, below3, above3, 0)
    if first:
        raw = [unspread(own3, below3, above3, n) for n in (1, 2, 3)]
        lane = iota(shape, 2)
        at = (
            where[0] * 4 - 12 + iota(shape, 0),
            lax.rem(where[1] * 2 + iota(shape, 1), n3[1]),
            where[2] * 16 + jnp.where(lane < 64, lane, lane - 128),
        )
        values = level_of(raw[0], step_x(raw[0], 1), raw[1], raw[2], *at, n3)
        for ref, value in zip(level_3, values):
            ref[...] = value
    faces = tuple(ref[...] for ref in level_3[:4])
    inv3 = level_3[4][...]
    d = (COARSE_FIRST * r3) * inv3
    total3 = d
    for keep, gain in COARSE_STEPS:
        r3 = r3 - apply_to(d, faces)
        d = keep * d + gain * (r3 * inv3)
        total3 = total3 + d

    copies_rows, copies_lanes = row_copies(2 * ny3), lane_copies(128)
    blocks = [refine(total3[8 + 4 * g : 12 + 4 * g], copies_rows, copies_lanes) for g in range(3)]
    p = jnp.concatenate(blocks, 0)
    faces = (gx2[...], gy2[...], gz2[...], diag2[...])
    r2 = r2_in[...] - apply_to(p, faces)
    d = (FIRST * r2) * inv2[...]
    r2 = r2 - apply_to(d, faces)
    d_next = KEEP * d + GAIN * (r2 * inv2[...])
    e2 = e2_in[...] + p + d + d_next

    copies_rows = row_copies(4 * ny3)
    for g in range(4):
        p1[8 + 8 * g : 16 + 8 * g] = refine(e2[4 + 4 * g : 8 + 4 * g], copies_rows, copies_lanes)
    faces = (fx1, fy1, fz1, diag1)

    def lift_1(at, n):
        here = pl.ds(at, n)
        left = r1_in[here] - apply_at(p1, at, n, faces)
        r1[here] = left
        a1[here] = (FIRST * left) * inv1[here]

    loop(11, 37, B1, lift_1)
    relax_1(r1, faces, inv1, a1, b1, 12, 36)

    def sum_1(at, n):
        here = pl.ds(at, n)
        value = e1_in[here] + p1[here] + a1[here] + b1[here]
        c1[here, 0:8] = value[:, 0:8]
        tile = (n, 8, 128)
        c1[here, 8:16] = jnp.where(iota(tile, 1) < 4, value[:, 8:16], value[:, -8:])

    loop(12, 36, B1, sum_1)

    copies_rows, copies_lanes = row_copies(32), lane_copies(256)
    for g in range(6):
        p0[8 * g : 8 * g + 8] = refine(c1[12 + 4 * g : 16 + 4 * g], copies_rows, copies_lanes)
    faces = (fx, fy, fz, diag)
    begin_at, end_at = (6, 42) if last else (2, 46)

    def lift_0(at, n):
        here = pl.ds(at, n)
        left = r_in[here] - apply_at(p0, at, n, faces)
        r[here] = left
        d0[here] = (FIRST * left) * inv[here]

    loop(begin_at, end_at, B0, lift_0, U0)
    into = pressure if last else total
    into[...] = total_in[...]
    smooth_0(r, faces, inv, d0, d1, begin_at, end_at, lambda: add_own(into, (p0, d0, d1), False),
             again=first, residual=residual if last else None)
    if not last:
        smooth_0(r, faces, inv, d0, d1, 4, 44, lambda: add_own(total, (d0, d1), False))
        restrict_0(r, packed)


def call(kernel, name, args, outs, scratch=(), us=0, after=()):
    body, count = kernel, len(args)
    if after:
        def kernel(*refs):
            body(*refs[:count], *refs[count + len(after) :])

    vmem = pl.BlockSpec(memory_space=pltpu.VMEM)
    smem = pl.BlockSpec(memory_space=pltpu.SMEM)
    return pl.pallas_call(
        kernel,
        out_shape=[jax.ShapeDtypeStruct(s, F32) for s in outs],
        in_specs=[smem if a.ndim == 1 else vmem for a in args] + [pl.BlockSpec(memory_space=pl.ANY)] * len(after),
        out_specs=[vmem] * len(outs),
        scratch_shapes=[pltpu.VMEM(s, F32) for s in scratch],
        compiler_params=pltpu.CompilerParams(vmem_limit_bytes=VMEM_LIMIT),
        name=name,
        cost_estimate=pl.CostEstimate(flops=0, bytes_accessed=us * 3_500_000, transcendentals=0) if us else None,
        interpret=INTERPRET,
    )(*args, *after)


def from_below(array, axis, by=1):
    n = lax.axis_size(axis)
    return lax.ppermute(array, axis, [(i, (i + by) % n) for i in range(n)])


def from_above(array, axis, by=1):
    n = lax.axis_size(axis)
    return lax.ppermute(array, axis, [((i + by) % n, i) for i in range(n)])


def body(right_side, phase_mask):
    nx, ny, nz = (lax.axis_size(a) for a in ("gx", "gy", "gz"))
    sizes = (nx * BX, ny * BY, nz * BZ)
    where = jnp.stack([lax.axis_index(a) for a in ("gx", "gy", "gz")]).astype(jnp.int32)
    own = (BX, BY, BZ)
    full = (X0, Y0, Z0)
    full_1 = (X1, 8 * ny, 128)
    full_2 = (X2, 4 * ny, 128)
    full_3 = (X3, 2 * ny, 128)

    def along_y(packed):
        return [packed] + [from_above(packed, "gy", s) for s in range(1, ny)]

    def along_x(parts):
        rows = jnp.concatenate(parts, 1)
        return rows, from_below(rows, "gx"), from_above(rows, "gx")

    to_upper, to_lower = call(send_z_own, "send_z_own", (phase_mask,), [(16, BY, 128)] * 2)
    beside_own = (from_below(to_upper, "gz"), from_above(to_lower, "gz"))
    upper, lower, plane = call(
        send_y, "send_y", (right_side, phase_mask, *beside_own), [(52, 8, Z0)] * 2 + [(BY, Z0)])
    below, above = from_below(upper, "gy"), from_above(lower, "gy")
    plane = from_above(plane, "gx")
    pieces = (lower, upper, below, above)
    to_upper, to_lower = call(send_x, "send_x", pieces, [(14, Y0, Z0)] * 2, after=(plane,))
    pieces += (from_below(to_upper, "gx"), from_above(to_lower, "gx"))
    (packed,) = call(
        functools.partial(own_faces_0, sizes), "own_faces_0", (where, phase_mask, *beside_own, above, plane),
        [(48, 8, 128)], [(BX + 1, BY, Z0)] + [(BX, BY, Z0)] * 3, us=2)
    parts = along_y(packed)
    around_faces = along_x(parts)
    r_own, to_upper, to_lower = call(
        send_z, "send_z", pieces, [(X0, Y0, 128)] + [(24, Y0, 128)] * 2, after=(packed, parts[1]))
    residual = (r_own, from_below(to_upper, "gz"), from_above(to_lower, "gz"))
    level_0 = call(
        functools.partial(faces_0, sizes), "faces_0", (where, *pieces), [full] * 5,
        [(X0 + 2, Y0, Z0), (X0, Z0), (X0, Z0)], us=4)
    r0, total, packed = call(
        begin, "begin", (*residual, *level_0), [full, own, (16, 8, 128)], [full] * 2, us=6)
    *levels, faces_3 = call(
        functools.partial(faces_1, sizes), "faces_1", (where, *around_faces),
        [full_1] * 5 + [full_2] * 5 + [(10, 2 * ny, 128)], us=3)
    level_3 = []
    for cycle in range(2):
        first = cycle == 0
        r1, e1, r2, e2, packed = call(
            down, "down", (*along_x(along_y(packed)), *levels, *([faces_3] if first else [])),
            [full_1] * 2 + [full_2] * 2 + [(10 if first else 8, 2 * ny, 128)], [full_1] * 2, us=4)
        below, above = from_below(packed, "gz"), from_above(packed, "gz")
        (wide,) = call(spread, "spread", (packed, below, above), [(20 if first else 8, 2 * ny, 128)])
        gathered = (wide, from_below(wide, "gx", 2), from_above(wide, "gx", 2))
        args = (where, *gathered, *level_3, *levels[5:], r2, e2, *levels[:5], r1, e1, *level_0, r0, total)
        scratch = [full_1] * 4 + [(X1, 16, 128)] + [full] * 3
        if first:
            *level_3, r0, total, packed = call(
                functools.partial(up, sizes, False), "up", args,
                [full_3] * 5 + [full, own, (16, 8, 128)], scratch, us=15)
        else:
            return tuple(call(functools.partial(up, sizes, True), "up_last", args, [own] * 2, [full] + scratch, us=10))


def solution(mesh):
    spec = P("gx", "gy", "gz")
    return jax.shard_map(body, mesh=mesh, in_specs=(spec, spec), out_specs=(spec, spec), check_vma=False)
```

```python
import functools

import jax
import jax.numpy as jnp
from jax import lax
from jax.experimental import pallas as pl
from jax.experimental.pallas import tpu as pltpu
from jax.sharding import PartitionSpec as P

COARSE_ITERS = 8
SMOOTH_LOW = 0.25
SMOOTH_HIGH = 2.0
COARSE_LOW = 0.02
LIQUID = 10.0
GAS = 1.0

INTERPRET = False
VMEM_LIMIT = 24 * 1024 * 1024

BX, BY, BZ = 32, 16, 128
WX = 8
X0, Y0, Z0 = BX + 2 * WX, 32, 256
X1, Y1G, Z1 = 48, 8, 128
X2 = 24
X3 = 26
F32 = jnp.float32
BF16 = jnp.bfloat16
DOWN, UP = 3, 3
UC, B0, U0, B1 = 4, 2, 4, 16


def chebyshev(low, degree):
    theta = 0.5 * (SMOOTH_HIGH + low)
    delta = 0.5 * (SMOOTH_HIGH - low)
    sigma = theta / delta
    rho_old = 1.0 / sigma
    steps = []
    for _ in range(1, degree):
        rho_new = 1.0 / (2.0 * sigma - rho_old)
        steps.append((rho_new * rho_old, 2.0 * rho_new / delta))
        rho_old = rho_new
    return 1.0 / theta, steps


FIRST, ((KEEP, GAIN),) = chebyshev(SMOOTH_LOW, 2)
COARSE_FIRST, COARSE_STEPS = chebyshev(COARSE_LOW, COARSE_ITERS)


def roll(values, shift, axis):
    return pltpu.roll(values, shift % values.shape[axis], axis)


def iota(shape, dim):
    return lax.broadcasted_iota(jnp.int32, shape, dim)


def split(values, terms):
    parts = []
    for n in range(terms):
        part = values.astype(BF16)
        parts.append(part)
        if n + 1 < terms:
            values = values - part.astype(F32)
    return parts


def times(values, matrix, terms):
    return sum(jnp.dot(p, matrix, preferred_element_type=F32) for p in split(values, terms))


def times_left(matrix, values, terms):
    return sum(jnp.dot(matrix, p, preferred_element_type=F32) for p in split(values, terms))


def lane_pairs(fine, weight, odd_only=False):
    z = iota((fine, 128), 0)
    half = z >> 1
    if fine == 128:
        half = jnp.where(z >= 96, half + 64, half)
    hit = half == iota((fine, 128), 1)
    if odd_only:
        hit = hit & ((z & 1) == 1)
    return jnp.where(hit, weight, 0.0).astype(BF16)


def lane_copies(fine):
    z = iota((128, fine), 1)
    half = z >> 1
    if fine == 128:
        half = jnp.where(z >= 96, half + 64, half)
    return jnp.where(half == iota((128, fine), 0), 1.0, 0.0).astype(BF16)


def row_pairs(rows, odd_x=False, odd_y=False):
    shape = (2 * rows, 8 * rows)
    shift = rows.bit_length() - 1
    c, f = iota(shape, 0), iota(shape, 1)
    cx, cy = c >> (shift - 1), c & (rows // 2 - 1)
    x, y = f >> shift, f & (rows - 1)
    hit = ((x >> 1) == cx) & ((y >> 1) == cy)
    if odd_x:
        hit = hit & ((x & 1) == 1)
    if odd_y:
        hit = hit & ((y & 1) == 1)
    return jnp.where(hit, 1.0, 0.0).astype(BF16)


def row_copies(rows):
    shape = (8 * rows, 2 * rows)
    shift = rows.bit_length() - 1
    f, c = iota(shape, 0), iota(shape, 1)
    hit = ((f >> (shift + 1)) == (c >> (shift - 1))) & (((f & (rows - 1)) >> 1) == (c & (rows // 2 - 1)))
    return jnp.where(hit, 1.0, 0.0).astype(BF16)


def coarsen(block, rows_matrix, lanes_matrix):
    planes, rows, lanes = block.shape
    out = times(times_left(rows_matrix, block.reshape(planes * rows, lanes), DOWN), lanes_matrix, DOWN)
    return out.reshape(4, rows // 2, 128)


def coarsen_all(planes, rows_matrix, lanes_matrix):
    return jnp.concatenate(
        [coarsen(planes[at : at + 8], rows_matrix, lanes_matrix) for at in range(0, planes.shape[0], 8)], 0)


def refine(block, rows_matrix, lanes_matrix):
    planes, rows, lanes = block.shape
    out = times_left(rows_matrix, times(block.reshape(planes * rows, lanes), lanes_matrix, UP), UP)
    return out.reshape(8, 2 * rows, lanes_matrix.shape[1])


def apply_at(v, at, planes, faces):
    fx, fy, fz, diag = faces
    here = pl.ds(at, planes)
    wide = v[pl.ds(at - 1, planes + 2)]
    x = fx[pl.ds(at - 1, planes + 1)]
    c = wide[1:-1]
    y, z = fy[here], fz[here]
    out = diag[here] * c - x[1:] * wide[2:] - x[:-1] * wide[:-2]
    out = out - y * roll(c, -1, 1) - roll(y * c, 1, 1)
    return out - z * roll(c, -1, 2) - roll(z * c, 1, 2)


def step_x(values, by):
    if by > 0:
        return jnp.concatenate([values[-1:], values[:-1]], 0)
    return jnp.concatenate([values[1:], values[:1]], 0)


def apply_to(v, faces):
    fx, fy, fz, diag = faces
    out = diag * v - fx * step_x(v, -1) - step_x(fx * v, 1)
    out = out - fy * roll(v, -1, 1) - roll(fy * v, 1, 1)
    return out - fz * roll(v, -1, 2) - roll(fz * v, 1, 2)


def inverse(diag):
    return 1.0 / jnp.where(diag > 0.0, diag, 1.0)


def level_of(fx, fx_before, fy, fz, gx, gy, gz, sizes):
    nx, ny, nz = sizes
    diag = fx + jnp.where((gx == 0) | (gx == nx), 0.0, fx_before)
    diag = diag + fy + jnp.where(gy == 0, 0.0, roll(fy, 1, 1))
    diag = diag + fz + jnp.where(gz == 0, 0.0, roll(fz, 1, 2))
    fx = jnp.where((gx == nx - 1) | (gx == -1), 0.0, fx)
    fy = jnp.where((gy == ny - 1) | (gy == -1), 0.0, fy)
    fz = jnp.where((gz == nz - 1) | (gz == -1), 0.0, fz)
    return fx, fy, fz, diag, inverse(diag)


def loop(start, stop, block, body, unroll=1):
    count = (stop - start) // block

    def step(i, carry):
        body(start + i * block, block)
        return carry

    if count:
        lax.fori_loop(0, count, step, 0, unroll=unroll)
    rest = stop - start - count * block
    if rest:
        body(stop - rest, rest)


def beside(one, two, high):
    axis = one.ndim - 1
    return jnp.where((iota(one.shape, axis) >= 64) == high, one, roll(two, 64, axis))


def sides(below, above, at):
    one, two = above[at], below[at]
    axis = one.ndim - 1
    lane = iota(one.shape, axis)
    return jnp.where(lane < 64, one, two), roll(jnp.where(lane >= 64, one, two), 64, axis)


def density_of(mask):
    return GAS + (LIQUID - GAS) * mask[...].astype(F32)


def send_z_own(mask, to_upper, to_lower):
    density = density_of(mask)
    for out, high in ((to_upper, True), (to_lower, False)):
        out[...] = beside(density[0:16], density[16:32], high)


def send_y(r, mask, z_below, z_above, to_upper, to_lower, plane):
    density = density_of(mask)
    side = jnp.concatenate(sides(z_below, z_above, slice(0, 16)), 0)
    plane[:, 0:128] = density[0]
    plane[:, 128:256] = side[0]
    for out, rows, line in ((to_upper, slice(8, 16), 7), (to_lower, slice(0, 8), 8)):
        out[0:BX, :, 0:128] = density[:, rows]
        out[0:BX, :, 128:256] = side[:, rows]
        for x in range(BX):
            at = BX + x // 8
            out[at, x % 8 : x % 8 + 1, 0:128] = density[x, line : line + 1]
            out[at, x % 8 : x % 8 + 1, 128:256] = side[x, line : line + 1]
        out[36:52, :, 0:128] = r[0:16, rows]
        out[36:52, :, 128:256] = r[16:32, rows]


def send_x(lower, upper, below, above, to_upper, to_lower):
    for out, at, pack, r_at, lanes in ((to_upper, BX - 9, 3, 44, slice(128, 256)), (to_lower, 0, 0, 36, slice(0, 128))):
        for tile, source in enumerate((lower, upper, above, below)):
            rows = slice(8 * tile, 8 * tile + 8)
            out[0:9, rows] = source[at : at + 9]
            out[10:14, rows, 0:128] = source[r_at : r_at + 4, :, lanes]
            out[10:14, rows, 128:256] = source[r_at + 4 : r_at + 8, :, lanes]
        out[9, 0:8] = below[BX + pack]
        out[9, 8:16] = above[BX + pack]
        out[9, 16:32] = jnp.zeros((16, Z0), F32)


def send_z(lower, upper, below, above, x_below, x_above, own, to_upper, to_lower):
    one, two = slice(0, 128), slice(128, 256)
    own[0:4] = x_below[10:14, :, one]
    own[4:8] = x_below[10:14, :, two]
    own[40:44] = x_above[10:14, :, one]
    own[44:48] = x_above[10:14, :, two]
    for tile, source in enumerate((lower, upper, above, below)):
        rows = slice(8 * tile, 8 * tile + 8)
        own[8:24, rows] = source[36:52, :, one]
        own[24:40, rows] = source[36:52, :, two]
    for out, high in ((to_upper, True), (to_lower, False)):
        out[...] = beside(own[0:24], own[24:48], high)


def last_sweep_0(r, faces, d1, residual):
    fx, fy, fz, diag = faces
    rows, lanes = slice(0, BY), slice(0, BZ)

    def own(at, n):
        here = pl.ds(at, n)
        wide = d1[pl.ds(at - 1, n + 2), rows, lanes]
        x = fx[pl.ds(at - 1, n + 1), rows, lanes]
        out = diag[here, rows, lanes] * wide[1:-1] - x[1:] * wide[2:] - x[:-1] * wide[:-2]
        c, y = d1[here, :, lanes], fy[here, :, lanes]
        out = out - y[:, rows] * roll(c, -1, 1)[:, rows] - roll(y * c, 1, 1)[:, rows]
        c, z = d1[here, rows, :], fz[here, rows, :]
        out = out - z[:, :, lanes] * roll(c, -1, 2)[:, :, lanes] - roll(z * c, 1, 2)[:, :, lanes]
        residual[pl.ds(at - WX, n)] = r[here, rows, lanes] - out

    loop(WX, WX + BX, B0, own, U0)


def smooth_0(r, faces, inv, d0, d1, start, stop, between, again=False, residual=None):
    def second(at, n):
        here = pl.ds(at, n)
        left = r[here] - apply_at(d0, at, n, faces)
        r[here] = left
        d1[here] = KEEP * d0[here] + GAIN * (left * inv[here])

    loop(start + 1, stop - 1, B0, second, U0)
    between()
    if residual is not None:
        last_sweep_0(r, faces, d1, residual)
        return

    def third(at, n):
        here = pl.ds(at, n)
        left = r[here] - apply_at(d1, at, n, faces)
        r[here] = left
        if again:
            d0[here] = (FIRST * left) * inv[here]

    loop(start + 2, stop - 2, B0, third, U0)


def restrict_0(r, out):
    rows, lanes = row_pairs(16), lane_pairs(256, 0.125)
    for g in range(4):
        block = r[WX + 8 * g : WX + 8 * g + 8, 0:16, :]
        out[4 * g : 4 * g + 4] = coarsen(block, rows, lanes)


def add_own(total, terms, first):
    value = None if first else total[...]
    for term in terms:
        own = term[WX : WX + BX, 0:BY, 0:BZ]
        value = own if value is None else value + own
    total[...] = value


def face(total):
    return jnp.where(total < 5.0, 1.0, jnp.where(total < 15.0, 2.0 / 11.0, 0.1))


def own_faces_0(sizes, where, mask, below, above, rows_above, plane, packed, rho, raw_x, raw_y, raw_z):
    nx, ny, nz = sizes
    own, side = slice(0, 128), slice(128, 256)
    rho[0:BX, :, own] = density_of(mask)
    rho[0:16, :, side], rho[16:32, :, side] = sides(below, above, slice(0, 16))
    rho[BX] = plane[...]
    shape = (BY, Z0)
    y = iota(shape, 0)
    gy = where[1] * BY + y
    lane = iota(shape, 1)
    gz = where[2] * BZ + jnp.where(lane < 192, lane, lane - 256)

    def one_plane(p, n):
        c = rho[p]
        raw_x[p] = face(c + jnp.where(where[0] * BX + p == nx - 1, GAS, rho[p + 1]))
        after = jnp.where(y == BY - 1, rows_above[p, 0:1], roll(c, -1, 0))
        raw_y[p] = face(c + jnp.where(gy == ny - 1, GAS, after))
        raw_z[p] = face(c + jnp.where(gz == nz - 1, GAS, roll(c, -1, 1)))

    loop(0, BX, 1, one_plane, UC)
    lanes, odd_lanes = lane_pairs(256, 0.125), lane_pairs(256, 0.125, True)
    for n, (raw, rows, columns) in enumerate((
        (raw_x, row_pairs(16, odd_x=True), lanes),
        (raw_y, row_pairs(16, odd_y=True), lanes),
        (raw_z, row_pairs(16), odd_lanes),
    )):
        for g in range(4):
            packed[16 * n + 4 * g : 16 * n + 4 * g + 4] = coarsen(raw[8 * g : 8 * g + 8], rows, columns)


def faces_0(sizes, where, lower, upper, below, above, x_below, x_above, fx, fy, fz, diag, inv, rho, low, up):
    nx, ny, nz = sizes
    gx0, gy0, gz0 = where[0] * BX, where[1] * BY, where[2] * BZ
    rho[0:9] = x_below[0:9]
    rho[41:50] = x_above[0:9]
    for tile, source in enumerate((lower, upper, above, below)):
        rho[9:41, 8 * tile : 8 * tile + 8] = source[0:BX]
    low[0:8] = x_below[9, 0:8]
    up[0:8] = x_below[9, 8:16]
    low[40:48] = x_above[9, 0:8]
    up[40:48] = x_above[9, 8:16]
    for n in range(4):
        low[8 + 8 * n : 16 + 8 * n] = below[BX + n]
        up[8 + 8 * n : 16 + 8 * n] = above[BX + n]

    def plane(p, n):
        shape = (Y0, Z0)
        row, lane = iota(shape, 0), iota(shape, 1)
        gy = gy0 + jnp.where(row < 24, row, row - 32)
        gz = gz0 + jnp.where(lane < 192, lane, lane - 256)
        gx = gx0 + p - WX
        c = rho[p + 1]
        f_x = face(c + jnp.where(gx == nx - 1, GAS, rho[p + 2]))
        l_x = jnp.where(gx == 0, 0.0, face(c + rho[p]))
        over = jnp.where(row == 23, up[pl.ds(p, 1)], roll(c, -1, 0))
        under = jnp.where(row == 24, low[pl.ds(p, 1)], roll(c, 1, 0))
        f_y = face(c + jnp.where(gy == ny - 1, GAS, over))
        l_y = jnp.where(gy == 0, 0.0, face(c + under))
        f_z = face(c + jnp.where(gz == nz - 1, GAS, roll(c, -1, 1)))
        l_z = jnp.where(gz == 0, 0.0, roll(f_z, 1, 1))
        d = f_x + l_x + f_y + l_y + f_z + l_z
        i = 1.0 / d
        diag[p] = d
        inv[p] = i
        fx[p] = jnp.where((gx == nx - 1) | (gx == -1), 0.0, f_x)
        fy[p] = jnp.where((gy == ny - 1) | (gy == -1), 0.0, f_y)
        fz[p] = jnp.where((gz == nz - 1) | (gz == -1), 0.0, f_z)

    loop(0, X0, 1, plane, UC)


def begin(own, z_below, z_above, fx, fy, fz, diag, inv, r, total, packed, d0, d1):
    def whole(p, n):
        one, two = sides(z_below, z_above, pl.ds(p, n))
        for here, side in ((pl.ds(p, n), one), (pl.ds(p + 24, n), two)):
            value = jnp.concatenate([own[here], side], 2)
            r[here] = value
            d0[here] = (FIRST * value) * inv[here]

    loop(0, 24, 4, whole)
    smooth_0(r, (fx, fy, fz, diag), inv, d0, d1, 0, X0, lambda: add_own(total, (d0, d1), True))
    restrict_0(r, packed)


def assemble_1(n, own, below, above, out):
    width = below.shape[0] // (own.shape[0] // 16)
    part = slice(width * n, width * (n + 1))
    out[16:32] = own[16 * n : 16 * n + 16]
    out[16 - width : 16] = below[part]
    out[32 : 32 + width] = above[part]
    rest = jnp.zeros((16 - width,) + own.shape[1:], F32)
    out[0 : 16 - width] = rest
    out[32 + width : 48] = rest


def relax_1(r, faces, inv, d0, d1, start, stop):
    def second(at, n):
        here = pl.ds(at, n)
        left = r[here] - apply_at(d0, at, n, faces)
        r[here] = left
        d1[here] = KEEP * d0[here] + GAIN * (left * inv[here])

    loop(start, stop, B1, second)


def faces_1(sizes, where, own, below, above,
            fx, fy, fz, diag, inv, gx2, gy2, gz2, diag2, inv2, packed):
    n1 = tuple(n // 2 for n in sizes)
    n2 = tuple(n // 4 for n in sizes)
    ny1 = fx.shape[1]
    ny2 = ny1 // 2
    rows, lanes, odd_lanes = row_pairs(ny1), lane_pairs(128, 0.125), lane_pairs(128, 0.125, True)
    coarse = []
    for n, (raw, rows_matrix, columns) in enumerate((
        (fx, row_pairs(ny1, odd_x=True), lanes),
        (fy, row_pairs(ny1, odd_y=True), lanes),
        (fz, rows, odd_lanes),
    )):
        assemble_1(n, own, below, above, raw)
        coarse.append(jnp.concatenate(
            [coarsen(raw[8 * g : 8 * g + 8], rows_matrix, columns) for g in range(6)], 0))
    shape = (B1, ny1, 128)
    gy = lax.rem(where[1] * 8 + iota(shape, 1), n1[1])
    lane = iota(shape, 2)
    gz = where[2] * 64 + jnp.where(lane < 96, lane, lane - 128)

    def planes(n, count):
        at = X1 - B1 - n
        here = pl.ds(at, B1)
        gx = where[0] * 16 + at - 16 + iota(shape, 0)
        c = fx[here]
        before = jnp.concatenate([fx[pl.ds(jnp.maximum(at - 1, 0), 1)], c[:-1]], 0)
        level = level_of(c, before, fy[here], fz[here], gx, gy, gz, n1)
        fx[here], fy[here], fz[here], diag[here], inv[here] = level

    loop(0, X1, B1, planes)
    shape = (X2, ny2, 128)
    lane = iota(shape, 2)
    at_2 = (
        where[0] * 8 - 8 + iota(shape, 0),
        lax.rem(where[1] * 4 + iota(shape, 1), n2[1]),
        where[2] * 32 + jnp.where(lane < 64, lane, lane - 128),
    )
    level_2 = level_of(coarse[0], step_x(coarse[0], 1), coarse[1], coarse[2], *at_2, n2)
    gx2[...], gy2[...], gz2[...], diag2[...], inv2[...] = level_2
    sent = None
    for n, (rows_matrix, columns) in enumerate((
        (row_pairs(ny2, odd_x=True), lanes),
        (row_pairs(ny2, odd_y=True), lanes),
        (row_pairs(ny2), odd_lanes),
    )):
        at = 16 * (n + 1)
        value = roll(coarsen_all(coarse[n], rows_matrix, columns)[0:10], at, 2)
        sent = value if sent is None else jnp.where(iota(value.shape, 2) < at, sent, value)
    packed[...] = sent


def down(own, below, above, fx, fy, fz, diag, inv, gx2, gy2, gz2, diag2, inv2, *refs):
    *given, r, e, r2_out, e2_out, packed, d0, d1 = refs
    ny1 = fx.shape[1]
    ny2 = ny1 // 2
    assemble_1(0, own, below, above, r)
    rows, lanes = row_pairs(ny1), lane_pairs(128, 0.125)

    def begin_1(at, n):
        here = pl.ds(at, n)
        d0[here] = (FIRST * r[here]) * inv[here]

    loop(0, X1, B1, begin_1)
    faces = (fx, fy, fz, diag)
    relax_1(r, faces, inv, d0, d1, 1, X1 - 1)

    def third(at, n):
        here = pl.ds(at, n)
        r[here] = r[here] - apply_at(d1, at, n, faces)
        e[here] = d0[here] + d1[here]

    loop(2, X1 - 2, B1, third)
    e[0:2] = d0[0:2]
    e[X1 - 2 : X1] = d0[X1 - 2 : X1]
    r2 = jnp.concatenate([coarsen(r[8 * g : 8 * g + 8], rows, lanes) for g in range(6)], 0)
    faces_2 = (gx2[...], gy2[...], gz2[...], diag2[...])
    d = (FIRST * r2) * inv2[...]
    r2 = r2 - apply_to(d, faces_2)
    d_next = KEEP * d + GAIN * (r2 * inv2[...])
    r2 = r2 - apply_to(d_next, faces_2)
    r2_out[...] = r2
    e2_out[...] = d + d_next
    sent = coarsen_all(r2, row_pairs(ny2), lanes)
    if given:
        packed[...] = jnp.where(iota(packed.shape, 2) < 16, sent[0:10], given[0][...])
    else:
        packed[...] = sent[2:10]


def spread(own, below, above, out):
    shape = own.shape
    lane = iota(shape, 2)
    values = []
    for n in range(4 if out.shape[0] > shape[0] else 1):
        start = 64 * (n % 2)
        here = lane - start
        value = jnp.where(here < 16, roll(own[...], start - 16 * n, 2), 0.0)
        value = jnp.where((here >= 16) & (here < 32), roll(above[...], start + 16 - 16 * n, 2), value)
        value = jnp.where(here >= 48, roll(below[...], start + 48 - 16 * n, 2), value)
        if n % 2:
            values[-1] = jnp.where(here < 0, values[-1], value)
        else:
            values.append(value)
    for n, value in enumerate(values):
        out[shape[0] * n : shape[0] * (n + 1)] = value


def unspread(own, below, above, n):
    if own.shape[0] == 20:
        at = 10 * (n // 2)
        parts = [below[at : at + 10]] + [part[at + 2 : at + 10] for part in (own, above)]
    else:
        parts = [jnp.zeros((2,) + own.shape[1:], F32), below[...], own[...], above[...]]
    value = jnp.concatenate(parts, 0)
    lane = iota(value.shape, 2)
    near, far = (roll(value, 64, 2), value) if n % 2 else (value, roll(value, 64, 2))
    return jnp.where(lane < 32, near, jnp.where(lane >= 112, far, 0.0))


def up(sizes, last, where, own3, below3, above3, *refs):
    n3 = tuple(n // 8 for n in sizes)
    first = not last
    refs = list(refs)
    take = lambda n: [refs.pop(0) for _ in range(n)]
    if last:
        level_3 = take(5)
    gx2, gy2, gz2, diag2, inv2, r2_in, e2_in = take(7)
    fx1, fy1, fz1, diag1, inv1, r1_in, e1_in = take(7)
    fx, fy, fz, diag, inv, r_in, total_in = take(7)
    if first:
        level_3 = take(5)
        r, total, packed = take(3)
    else:
        pressure, residual = take(2)
        (r,) = take(1)
    p1, r1, a1, b1, c1, p0, d0, d1 = take(8)

    ny3 = own3.shape[1]
    shape = (X3, ny3, 128)
    r3 = unspread(own3, below3, above3, 0)
    if first:
        raw = [unspread(own3, below3, above3, n) for n in (1, 2, 3)]
        lane = iota(shape, 2)
        at = (
            where[0] * 4 - 12 + iota(shape, 0),
            lax.rem(where[1] * 2 + iota(shape, 1), n3[1]),
            where[2] * 16 + jnp.where(lane < 64, lane, lane - 128),
        )
        values = level_of(raw[0], step_x(raw[0], 1), raw[1], raw[2], *at, n3)
        for ref, value in zip(level_3, values):
            ref[...] = value
    faces = tuple(ref[...] for ref in level_3[:4])
    inv3 = level_3[4][...]
    d = (COARSE_FIRST * r3) * inv3
    total3 = d
    for keep, gain in COARSE_STEPS:
        r3 = r3 - apply_to(d, faces)
        d = keep * d + gain * (r3 * inv3)
        total3 = total3 + d

    copies_rows, copies_lanes = row_copies(2 * ny3), lane_copies(128)
    blocks = [refine(total3[8 + 4 * g : 12 + 4 * g], copies_rows, copies_lanes) for g in range(3)]
    p = jnp.concatenate(blocks, 0)
    faces = (gx2[...], gy2[...], gz2[...], diag2[...])
    r2 = r2_in[...] - apply_to(p, faces)
    d = (FIRST * r2) * inv2[...]
    r2 = r2 - apply_to(d, faces)
    d_next = KEEP * d + GAIN * (r2 * inv2[...])
    e2 = e2_in[...] + p + d + d_next

    copies_rows = row_copies(4 * ny3)
    for g in range(4):
        p1[8 + 8 * g : 16 + 8 * g] = refine(e2[4 + 4 * g : 8 + 4 * g], copies_rows, copies_lanes)
    faces = (fx1, fy1, fz1, diag1)

    def lift_1(at, n):
        here = pl.ds(at, n)
        left = r1_in[here] - apply_at(p1, at, n, faces)
        r1[here] = left
        a1[here] = (FIRST * left) * inv1[here]

    loop(11, 37, B1, lift_1)
    relax_1(r1, faces, inv1, a1, b1, 12, 36)

    def sum_1(at, n):
        here = pl.ds(at, n)
        value = e1_in[here] + p1[here] + a1[here] + b1[here]
        c1[here, 0:8] = value[:, 0:8]
        tile = (n, 8, 128)
        c1[here, 8:16] = jnp.where(iota(tile, 1) < 4, value[:, 8:16], value[:, -8:])

    loop(12, 36, B1, sum_1)

    copies_rows, copies_lanes = row_copies(32), lane_copies(256)
    for g in range(6):
        p0[8 * g : 8 * g + 8] = refine(c1[12 + 4 * g : 16 + 4 * g], copies_rows, copies_lanes)
    faces = (fx, fy, fz, diag)
    begin_at, end_at = (6, 42) if last else (2, 46)

    def lift_0(at, n):
        here = pl.ds(at, n)
        left = r_in[here] - apply_at(p0, at, n, faces)
        r[here] = left
        d0[here] = (FIRST * left) * inv[here]

    loop(begin_at, end_at, B0, lift_0, U0)
    into = pressure if last else total
    into[...] = total_in[...]
    smooth_0(r, faces, inv, d0, d1, begin_at, end_at, lambda: add_own(into, (p0, d0, d1), False),
             again=first, residual=residual if last else None)
    if not last:
        smooth_0(r, faces, inv, d0, d1, 4, 44, lambda: add_own(total, (d0, d1), False))
        restrict_0(r, packed)


def call(kernel, name, args, outs, scratch=(), us=0, after=()):
    body, count = kernel, len(args)
    if after:
        def kernel(*refs):
            body(*refs[:count], *refs[count + len(after) :])

    vmem = pl.BlockSpec(memory_space=pltpu.VMEM)
    smem = pl.BlockSpec(memory_space=pltpu.SMEM)
    return pl.pallas_call(
        kernel,
        out_shape=[jax.ShapeDtypeStruct(s, F32) for s in outs],
        in_specs=[smem if a.ndim == 1 else vmem for a in args] + [pl.BlockSpec(memory_space=pl.ANY)] * len(after),
        out_specs=[vmem] * len(outs),
        scratch_shapes=[pltpu.VMEM(s, F32) for s in scratch],
        compiler_params=pltpu.CompilerParams(vmem_limit_bytes=VMEM_LIMIT),
        name=name,
        cost_estimate=pl.CostEstimate(flops=0, bytes_accessed=us * 3_500_000, transcendentals=0) if us else None,
        interpret=INTERPRET,
    )(*args, *after)


def from_below(array, axis, by=1):
    n = lax.axis_size(axis)
    return lax.ppermute(array, axis, [(i, (i + by) % n) for i in range(n)])


def from_above(array, axis, by=1):
    n = lax.axis_size(axis)
    return lax.ppermute(array, axis, [((i + by) % n, i) for i in range(n)])


def body(right_side, phase_mask):
    nx, ny, nz = (lax.axis_size(a) for a in ("gx", "gy", "gz"))
    sizes = (nx * BX, ny * BY, nz * BZ)
    where = jnp.stack([lax.axis_index(a) for a in ("gx", "gy", "gz")]).astype(jnp.int32)
    own = (BX, BY, BZ)
    full = (X0, Y0, Z0)
    full_1 = (X1, 8 * ny, 128)
    full_2 = (X2, 4 * ny, 128)
    full_3 = (X3, 2 * ny, 128)

    def along_y(packed):
        return [packed] + [from_above(packed, "gy", s) for s in range(1, ny)]

    def along_x(parts, width):
        rows = jnp.concatenate(parts, 1)
        planes = rows.reshape((-1, 16) + rows.shape[1:])
        last, first = (p.reshape((-1,) + rows.shape[1:]) for p in (planes[:, 16 - width :], planes[:, :width]))
        return rows, from_below(last, "gx"), from_above(first, "gx")

    to_upper, to_lower = call(send_z_own, "send_z_own", (phase_mask,), [(16, BY, 128)] * 2)
    beside_own = (from_below(to_upper, "gz"), from_above(to_lower, "gz"))
    upper, lower, plane = call(
        send_y, "send_y", (right_side, phase_mask, *beside_own), [(52, 8, Z0)] * 2 + [(BY, Z0)])
    below, above = from_below(upper, "gy"), from_above(lower, "gy")
    plane = from_above(plane, "gx")
    pieces = (lower, upper, below, above)
    to_upper, to_lower = call(send_x, "send_x", pieces, [(14, Y0, Z0)] * 2, after=(plane,))
    pieces += (from_below(to_upper, "gx"), from_above(to_lower, "gx"))
    (packed,) = call(
        functools.partial(own_faces_0, sizes), "own_faces_0", (where, phase_mask, *beside_own, above, plane),
        [(48, 8, 128)], [(BX + 1, BY, Z0)] + [(BX, BY, Z0)] * 3, us=2)
    parts = along_y(packed)
    around_faces = along_x(parts, 15)
    r_own, to_upper, to_lower = call(
        send_z, "send_z", pieces, [(X0, Y0, 128)] + [(24, Y0, 128)] * 2, after=(packed, parts[1]))
    residual = (r_own, from_below(to_upper, "gz"), from_above(to_lower, "gz"))
    level_0 = call(
        functools.partial(faces_0, sizes), "faces_0", (where, *pieces), [full] * 5,
        [(X0 + 2, Y0, Z0), (X0, Z0), (X0, Z0)], us=4)
    r0, total, packed = call(
        begin, "begin", (*residual, *level_0), [full, own, (16, 8, 128)], [full] * 2, us=6)
    *levels, faces_3 = call(
        functools.partial(faces_1, sizes), "faces_1", (where, *around_faces),
        [full_1] * 5 + [full_2] * 5 + [(10, 2 * ny, 128)], us=3)
    level_3 = []
    for cycle in range(2):
        first = cycle == 0
        r1, e1, r2, e2, packed = call(
            down, "down", (*along_x(along_y(packed), 14), *levels, *([faces_3] if first else [])),
            [full_1] * 2 + [full_2] * 2 + [(10 if first else 8, 2 * ny, 128)], [full_1] * 2, us=4)
        below, above = from_below(packed, "gz"), from_above(packed, "gz")
        (wide,) = call(spread, "spread", (packed, below, above), [(20 if first else 8, 2 * ny, 128)])
        gathered = (wide, from_below(wide, "gx", 2), from_above(wide, "gx", 2))
        args = (where, *gathered, *level_3, *levels[5:], r2, e2, *levels[:5], r1, e1, *level_0, r0, total)
        scratch = [full_1] * 4 + [(X1, 16, 128)] + [full] * 3
        if first:
            *level_3, r0, total, packed = call(
                functools.partial(up, sizes, False), "up", args,
                [full_3] * 5 + [full, own, (16, 8, 128)], scratch, us=15)
        else:
            return tuple(call(functools.partial(up, sizes, True), "up_last", args, [own] * 2, [full] + scratch, us=10))


def solution(mesh):
    spec = P("gx", "gy", "gz")
    return jax.shard_map(body, mesh=mesh, in_specs=(spec, spec), out_specs=(spec, spec), check_vma=False)
```
